128 devices in a mesh: dp: 16 (over z_hi, x, core), tensor: 8 (over z_lo, y).
Axes of the slice: x: 4, y: 4, z: 4 (z_hi: 2, z_lo: 2; z = z_hi * 2 + z_lo), core: 2. Of those that a mesh axis runs over, the one named last changes fastest.
Arguments:
- tokens: bfloat16 [16384, 2048], P('dp'), may hold values from -6 to 6
- cotangent: bfloat16 [16384, 2048], P('dp'), may hold values from -6 to 6
- seq_lengths: int32 [16, 8], P('dp'), may hold values from 0 to 1024, as said below
- ln_gain: bfloat16 [2048], replicated, may hold values from 0.5 to 1.5
- ln_bias: bfloat16 [2048], replicated, may hold values from -1.75 to 1.75
- w_qkv: bfloat16 [2048, 6144], P(None, 'tensor'), may hold values from -0.125 to 0.125
- b_qkv: bfloat16 [6144], P('tensor'), may hold values from -3 to 3
- w_dense: bfloat16 [2048, 2048], P('tensor'), may hold values from -0.5 to 0.5
- b_dense: bfloat16 [2048], replicated, may hold values from -1.75 to 1.75
- w_fc1: bfloat16 [2048, 8192], P(None, 'tensor'), may hold values from -0.125 to 0.125
- b_fc1: bfloat16 [8192], P('tensor'), may hold values from -3 to 3
- w_fc2: bfloat16 [8192, 2048], P('tensor'), may hold values from -0.0625 to 0.0625
- b_fc2: bfloat16 [2048], replicated, may hold values from -1.75 to 1.75
Outputs:
- output: bfloat16 [16384, 2048], P('dp')
- grad_tokens: bfloat16 [16384, 2048], P('dp')
- grad_ln_gain: float32 [2048], P('dp')
- grad_ln_bias: float32 [2048], P('dp')
- grad_w_qkv: float32 [2048, 6144], P('dp', 'tensor')
- grad_b_qkv: float32 [6144], P(('tensor', 'dp'))
- grad_w_dense: float32 [2048, 2048], P('tensor', 'dp')
- grad_b_dense: float32 [2048], P('dp')
- grad_w_fc1: float32 [2048, 8192], P('dp', 'tensor')
- grad_b_fc1: float32 [8192], P(('tensor', 'dp'))
- grad_w_fc2: float32 [8192, 2048], P('tensor', 'dp')
- grad_b_fc2: float32 [2048], P('dp')
The draws below stay inside these ranges and needn't reach their ends.
Inputs may be any that keep to these rules, and one draw needn't show every extreme that they name: `seq_lengths`: row r lists the lengths of the sequences packed in order from the start of slot r of 1024 positions; the rest of the slot is padding and zero entries are unused places. In every draw one row is a single sequence of exactly 1024.
All inputs are finite; a program needn't handle non-finite values.
Results may differ from the reference program's by a relative error of at most 0.014.
Values may be sent and summed in bfloat16 or wider, within the bound.
No kernel may reach another device: no remote copies, remote signals or barrier semaphores. Data moves between devices by JAX's collectives and lax.ppermute only.
A program may use at most 192 MiB of HBM per device.

```python
import jax
import jax.numpy as jnp
from jax import lax

HEADS = 32
HEAD_DIM = 64
ROTARY = 32
FF = 8192
D = 2048
SLOT = 1024
SEQS = 8
MINLEN = 64
TOKENS = 16384
N_DP = 16


def draw_seq_lengths(key, part):
    key = jax.random.fold_in(key, 7)
    key_level, key_jitter, key_fill, key_full = jax.random.split(key, 4)
    levels = jax.random.randint(key_level, (N_DP, SEQS), 0, 5)
    factors = jnp.array([1, 2, 4, 8, 16], jnp.int32)[levels]
    base_len = MINLEN * factors + jax.random.randint(key_jitter, (N_DP, SEQS), 0, MINLEN)
    fill_at = jax.random.randint(key_fill, (N_DP, 1), SLOT // 2, SLOT + 1)
    seq_ends = jnp.minimum(jnp.cumsum(base_len, axis=1).astype(jnp.int32), fill_at)
    starts = jnp.concatenate([jnp.zeros((N_DP, 1), jnp.int32), seq_ends[:, :-1]], axis=1)
    lengths = seq_ends - starts
    chosen = jax.random.randint(key_full, (), 0, N_DP)
    full_row = jnp.where(jnp.arange(SEQS) == 0, SLOT, 0).astype(jnp.int32)
    return jnp.where((jnp.arange(N_DP) == chosen)[:, None], full_row[None, :], lengths).astype(jnp.int32)


def with_spikes(drawn, key, source, target, blocks, factor):
    def block_of(dim):
        return (jnp.arange(drawn.shape[dim]) // (drawn.shape[dim] // blocks)).reshape((-1,) + (1,) * (drawn.ndim - 1 - dim))

    first = jax.random.permutation(key, blocks)[block_of(target)]
    other_side = (block_of(target) + blocks // 2) % blocks
    return jnp.where((block_of(source) == first) | (block_of(source) == other_side), factor * drawn, drawn)


def level_of(stream_key, extent, cuts, low, high):
    factor_of = 1.0
    for axis_at, parts in cuts:
        steps = jax.random.uniform(jax.random.fold_in(jax.random.fold_in(stream_key, 6), axis_at), (parts,), jnp.float32, low / len(cuts), high / len(cuts))
        factor_of = factor_of * jnp.repeat(jnp.exp(steps), extent[axis_at] // parts).reshape((-1,) + (1,) * (len(extent) - 1 - axis_at))
    return factor_of


def bell_draw(rng, dims, spread, reach, shards=(), kind=jnp.bfloat16):
    gain = level_of(rng, dims, shards, -0.22, 0.18) if shards else 1.0
    entries = jax.random.normal(rng, dims, jnp.float32) * spread * gain
    return jnp.minimum(jnp.maximum(entries, -reach), reach).astype(kind)


def noise_with(rng, dims, deviation, bound, cuts, heavy, held_as=jnp.bfloat16):
    result = deviation * jax.random.normal(rng, dims, jnp.float32)
    if cuts:
        result = result * level_of(rng, dims, cuts, -0.22, 0.18)
    return jnp.clip(with_spikes(result, jax.random.fold_in(rng, 3), *heavy), -bound, bound).astype(held_as)


def setup_inputs(seed: int = 0) -> dict:
    seeds = jax.random.split(jax.random.key(seed), 14)
    return {
        "tokens": bell_draw(seeds[0], (TOKENS, D), 1.0, 6.0, ((0, 16),)),
        "cotangent": noise_with(seeds[1], (TOKENS, D), 1.0, 6.0, ((0, 16),), (0, 1, 16, 2.0)),
        "seq_lengths": draw_seq_lengths(jax.random.fold_in(seeds[13], 71), 0),
        "ln_gain": jnp.clip(1.0 + 0.1 * jax.random.normal(seeds[3], (D,), jnp.float32), 0.5, 1.5).astype(jnp.bfloat16),
        "ln_bias": bell_draw(seeds[4], (D,), 0.3, 1.75),
        "w_qkv": bell_draw(seeds[5], (D, 3 * D), D ** -0.5, 0.125, ((1, 8),)),
        "b_qkv": bell_draw(seeds[6], (3 * D,), 0.5, 3.0, ((0, 8),)),
        "w_dense": bell_draw(seeds[7], (D, D), (D // 16) ** -0.5, 0.5, ((0, 8),)),
        "b_dense": bell_draw(seeds[8], (D,), 0.3, 1.75),
        "w_fc1": bell_draw(seeds[9], (D, FF), D ** -0.5, 0.125, ((1, 8),)),
        "b_fc1": bell_draw(seeds[10], (FF,), 0.5, 3.0, ((0, 8),)),
        "w_fc2": bell_draw(seeds[11], (FF, D), FF ** -0.5, 0.0625, ((0, 8),)),
        "b_fc2": bell_draw(seeds[12], (D,), 0.3, 1.75),
    }


@jax.custom_vjp
def low(v):
    return lax.optimization_barrier(v.astype(jnp.bfloat16)).astype(jnp.float32)

@jax.custom_vjp
def low_back(v):
    return v

def low_keep(v):
    return (low(v), None)

def low_pass(kept, grad):
    return (grad,)

def back_keep(v):
    return (v, None)

def back_low(kept, grad):
    return (low(grad),)
low.defvjp(low_keep, low_pass)
low_back.defvjp(back_keep, back_low)

def slot_layout(lengths_row, slot_len):
    places = jnp.arange(slot_len, dtype=jnp.int32)
    seq_ends = jnp.cumsum(lengths_row).astype(jnp.int32)
    segment = lax.optimization_barrier(jnp.sum((places[:, None] >= seq_ends[None, :]).astype(jnp.int32), axis=1)).astype(jnp.int32)
    starts = jnp.concatenate([jnp.zeros((1,), jnp.int32), seq_ends])
    picked = segment[:, None] == jnp.arange(starts.shape[0], dtype=jnp.int32)[None, :]
    position = (places - lax.optimization_barrier(jnp.sum(jnp.where(picked, starts[None, :], 0), axis=1))).astype(jnp.int32)
    valid_rows = (places < seq_ends[-1]).astype(jnp.float32)
    return (segment, position, valid_rows)

def rotary_tables(position):
    half_rot = ROTARY // 2
    frequency = 10000.0 ** (-jnp.arange(half_rot, dtype=jnp.float32) * 2.0 / ROTARY)
    angles = position.astype(jnp.float32)[:, None] * frequency[None, :]
    cosines = jnp.concatenate([jnp.cos(angles), jnp.cos(angles)], axis=1)
    sines = jnp.concatenate([jnp.sin(angles), jnp.sin(angles)], axis=1)
    return (cosines, sines)

def rotate(heads_in, cosines, sines):
    half_rot = ROTARY // 2
    rotary = heads_in[..., :ROTARY]
    turned = jnp.concatenate([-rotary[..., half_rot:ROTARY], rotary[..., :half_rot]], axis=-1)
    mixed_rot = rotary * cosines[:, None, :] + turned * sines[:, None, :]
    return jnp.concatenate([mixed_rot, heads_in[..., ROTARY:]], axis=-1)

def reference(tokens, cotangent, seq_lengths, ln_gain, ln_bias, w_qkv, b_qkv, w_dense, b_dense, w_fc1, b_fc1, w_fc2, b_fc2):
    highest = lax.Precision.HIGHEST
    segment, position, valid_rows = jax.vmap(lambda lengths_row: slot_layout(lengths_row, SLOT))(seq_lengths)
    cosines, sines = rotary_tables(position.reshape(-1))
    valid_flat = valid_rows.reshape(-1)
    places = jnp.arange(SLOT, dtype=jnp.int32)
    causal = places[:, None] >= places[None, :]
    score_scale = HEAD_DIM ** (-0.5)

    def attend(pieces):
        queries, keys_in, values, seg_row = pieces
        scores = jnp.einsum('qhd,khd->hqk', queries, keys_in, precision=highest) * score_scale
        scores = low_back(scores)
        allowed = (seg_row[:, None] == seg_row[None, :]) & causal
        scores = jnp.where(allowed[None], scores, -1e+30)
        row_max = lax.optimization_barrier(jnp.max(scores, axis=2, keepdims=True))
        exp_scores = jnp.exp(scores - row_max)
        softmax_out = low(exp_scores / lax.optimization_barrier(jnp.sum(exp_scores, axis=2, keepdims=True)))
        return jnp.einsum('hqk,khd->qhd', softmax_out, values, precision=highest)

    def forward(inputs, norm_gain, norm_bias, qkv_weight, qkv_bias, dense_weight, dense_bias, fc1_weight, fc1_bias, fc2_weight, fc2_bias):
        center = inputs - lax.optimization_barrier(jnp.mean(inputs, axis=1, keepdims=True))
        inv_sigma = lax.rsqrt(lax.optimization_barrier(jnp.mean(center * center, axis=1, keepdims=True)) + 1e-05)
        hidden = low(center * inv_sigma * norm_gain + norm_bias)
        projected = jnp.dot(hidden, qkv_weight, precision=highest, preferred_element_type=jnp.float32) + qkv_bias
        projected = low_back(projected).reshape(TOKENS, HEADS, 3, HEAD_DIM)
        queries = low(rotate(projected[:, :, 0], cosines, sines))
        keys_in = low(rotate(projected[:, :, 1], cosines, sines))
        values = low(projected[:, :, 2])
        context = lax.map(jax.checkpoint(attend), (queries.reshape(N_DP, SLOT, HEADS, HEAD_DIM), keys_in.reshape(N_DP, SLOT, HEADS, HEAD_DIM), values.reshape(N_DP, SLOT, HEADS, HEAD_DIM), segment))
        context = low(low_back(context.reshape(TOKENS, D)))
        attn_out = jnp.dot(context, dense_weight, precision=highest, preferred_element_type=jnp.float32)
        up_pre = low_back(jnp.dot(hidden, fc1_weight, precision=highest, preferred_element_type=jnp.float32) + fc1_bias)
        activated = low(jax.nn.gelu(up_pre, approximate=True))
        mlp_out = jnp.dot(activated, fc2_weight, precision=highest, preferred_element_type=jnp.float32)
        branch = low_back(attn_out + mlp_out + dense_bias + fc2_bias)
        return inputs + valid_flat[:, None] * branch
    params = [tokens, ln_gain, ln_bias, w_qkv, b_qkv, w_dense, b_dense, w_fc1, b_fc1, w_fc2, b_fc2]
    params = [item.astype(jnp.float32) for item in params]
    output, pullback = jax.vjp(forward, *params)
    gradients = pullback(cotangent.astype(jnp.float32))
    return (output.astype(jnp.bfloat16), gradients[0].astype(jnp.bfloat16), gradients[1], gradients[2], gradients[3], gradients[4], gradients[5], gradients[6], gradients[7], gradients[8], gradients[9], gradients[10])
```

```python
import functools

import jax
import jax.numpy as jnp
from jax import lax
from jax.experimental import pallas as pl
from jax.experimental.pallas import tpu as pltpu
from jax.sharding import Mesh
from jax.sharding import PartitionSpec as P

HEAD_DIM = 64
ROTARY = 32
DP = ("zh", "x", "core")
TENSOR = ("zl", "y")
BF16 = jnp.bfloat16
F32 = jnp.float32
ROWS = 256
BLOCK = 128
VMEM_BYTES = 56 * 2**20
GELU = 0.7978845608
SMALL_COST = pl.CostEstimate(flops=1, bytes_accessed=1, transcendentals=0)


def dot(left, right, left_dim, right_dim):
    return lax.dot_general(
        left, right, (((left_dim,), (right_dim,)), ((), ())), preferred_element_type=F32
    )


def kernel_call(kernel, name, out_shape, prefetch=0, **spec):
    if prefetch:
        spec = {
            "grid_spec": pltpu.PrefetchScalarGridSpec(
                num_scalar_prefetch=prefetch,
                grid=spec.pop("grid"),
                in_specs=spec.pop("in_specs"),
                out_specs=spec.pop("out_specs"),
                scratch_shapes=spec.pop("scratch_shapes", ()),
            ),
            **spec,
        }
    return pl.pallas_call(
        kernel,
        out_shape=out_shape,
        compiler_params=pltpu.CompilerParams(vmem_limit_bytes=VMEM_BYTES),
        cost_estimate=SMALL_COST,
        name=name,
        **spec,
    )


def made(rows, columns, kind=BF16):
    return jax.ShapeDtypeStruct((rows, columns), kind)


def kept(array):
    return pl.BlockSpec(array.shape, lambda *_: (0,) * array.ndim)


AWAY = pl.BlockSpec(memory_space=pl.ANY)
NEAR = pl.BlockSpec(memory_space=pltpu.VMEM)
SCALARS = pl.BlockSpec(memory_space=pltpu.SMEM)


def ends_of(lengths_ref):
    ends = []
    total = jnp.int32(0)
    for place in range(lengths_ref.shape[1]):
        total = total + lengths_ref[0, place]
        ends.append(total)
    return ends


def starts_at(ends, places):
    start = jnp.zeros_like(places)
    for end in ends:
        start = jnp.maximum(start, jnp.where(places >= end, end, 0))
    return start


def turned_halves(columns):
    lane = lax.broadcasted_iota(jnp.int32, columns.shape, 1)
    return jnp.where(
        lane % ROTARY < ROTARY // 2, pltpu.roll(columns, 112, 1), pltpu.roll(columns, 16, 1)
    )


def weight_copies(step, sources, targets, sems):
    copies = [
        pltpu.make_async_copy(source, target, sems.at[i])
        for i, (source, target) in enumerate(zip(sources, targets))
    ]

    @pl.when(step == 0)
    def _():
        for copy in copies:
            copy.start()

    def wait(i):
        @pl.when(step == 0)
        def _():
            copies[i].wait()

    return wait


def front_kernel(
    lengths_ref,
    freq_ref,
    tokens_ref,
    cot_ref,
    gain_ref,
    bias_ref,
    b_qkv_ref,
    b_fc1_ref,
    w_qkv_hbm,
    w_fc1_hbm,
    w_dense_hbm,
    hidden_ref,
    grad_ref,
    qkv_ref,
    act_ref,
    slope_ref,
    ctx_grad_ref,
    cos_ref,
    sin_ref,
    stats_ref,
    w_qkv,
    w_fc1,
    w_dense,
    sems,
):
    step = pl.program_id(0)
    wait = weight_copies(
        step, (w_qkv_hbm, w_fc1_hbm, w_dense_hbm), (w_qkv, w_fc1, w_dense), sems
    )
    rows = tokens_ref.shape[0]
    ends = ends_of(lengths_ref)
    places = step * rows + lax.broadcasted_iota(jnp.int32, (rows, 128), 0)
    position = (places - starts_at(ends, places)).astype(F32)
    lane = lax.broadcasted_iota(jnp.int32, (rows, 128), 1)
    angle = position * freq_ref[...]
    cosines = jnp.where(lane % HEAD_DIM < ROTARY, jnp.cos(angle), 1.0)
    sines = jnp.sin(angle)
    sines = jnp.where(
        lane % HEAD_DIM < ROTARY // 2, -sines, jnp.where(lane % HEAD_DIM < ROTARY, sines, 0.0)
    )
    cos_ref[...] = cosines
    sin_ref[...] = sines
    valid = (places < ends[-1])[:, :1]
    inputs = tokens_ref[...].astype(F32)
    mean = jnp.mean(inputs, axis=1, keepdims=True)
    center = inputs - mean
    inv_sigma = lax.rsqrt(jnp.mean(center * center, axis=1, keepdims=True) + 1e-05)
    stats_ref[...] = jnp.where(lane == 0, mean, inv_sigma)
    hidden = (
        center * inv_sigma * gain_ref[...].astype(F32)[None] + bias_ref[...].astype(F32)[None]
    ).astype(BF16)
    grad = jnp.where(valid, cot_ref[...], jnp.zeros_like(cot_ref))
    hidden_ref[...] = hidden
    grad_ref[...] = grad
    wait(0)
    projected = dot(hidden, w_qkv[...], 1, 0) + b_qkv_ref[...].astype(F32)[None]
    for block in range(qkv_ref.shape[1] // 128):
        columns = slice(block * 128, block * 128 + 128)
        plain = projected[:, columns]
        turned = plain * cosines + turned_halves(plain) * sines
        if block % 3 == 1:
            turned = jnp.where(lane < HEAD_DIM, plain, turned)
        if block % 3 == 2:
            turned = jnp.where(lane < HEAD_DIM, turned, plain)
        qkv_ref[:, columns] = turned.astype(BF16)
    wait(1)
    for block in range(w_fc1.shape[1] // 256):
        columns = slice(block * 256, block * 256 + 256)
        up = dot(hidden, w_fc1[:, columns], 1, 0) + b_fc1_ref[columns].astype(F32)[None]
        square = up * up
        tanh = jnp.tanh(GELU * up * (1.0 + 0.044715 * square))
        act_ref[:, columns] = (0.5 * up * (1.0 + tanh)).astype(BF16)
        slope_ref[:, columns] = (
            0.5 * (1.0 + tanh)
            + 0.5 * up * (1.0 - tanh * tanh) * (GELU + (GELU * 3 * 0.044715) * square)
        ).astype(BF16)
    wait(2)
    ctx_grad_ref[...] = dot(grad, w_dense[...], 1, 1).astype(BF16)


def front(lengths, freq, tokens, cot, gain, bias, b_qkv, b_fc1, w_qkv, w_fc1, w_dense):
    slot_len, width = tokens.shape

    def row(columns):
        return pl.BlockSpec((ROWS, columns), lambda i: (i, 0))

    widths = (width, width, w_qkv.shape[1], w_fc1.shape[1], w_fc1.shape[1], w_dense.shape[0])
    return kernel_call(
        front_kernel,
        "front",
        [made(slot_len, w) for w in widths] + [made(slot_len, 128, F32)] * 3,
        grid=(slot_len // ROWS,),
        in_specs=[SCALARS, kept(freq), row(width), row(width)]
        + [kept(a) for a in (gain, bias, b_qkv, b_fc1)]
        + [AWAY] * 3,
        out_specs=[row(w) for w in widths] + [row(128)] * 3,
        scratch_shapes=[
            pltpu.VMEM(w_qkv.shape, BF16),
            pltpu.VMEM(w_fc1.shape, BF16),
            pltpu.VMEM(w_dense.shape, BF16),
            pltpu.SemaphoreType.DMA((3,)),
        ],
    )(lengths, freq, tokens, cot, gain, bias, b_qkv, b_fc1, w_qkv, w_fc1, w_dense)


def attention_kernel(
    lengths_ref, qkv_ref, ctx_grad_ref, cos_ref, sin_ref, ctx_ref, qkv_grad_ref, turn_sum, value_sum
):
    slot_len = qkv_ref.shape[0]
    ends = ends_of(lengths_ref)
    for head in range(2):
        at = 3 * HEAD_DIM * head
        mine = slice(HEAD_DIM * head, HEAD_DIM * head + HEAD_DIM)
        for block in reversed(range(slot_len // ROWS)):
            rows = slice(block * ROWS, block * ROWS + ROWS)
            reach = (block + 1) * ROWS
            query = qkv_ref[rows, at : at + 64] * BF16(HEAD_DIM**-0.5)
            key = qkv_ref[0:reach, at + 64 : at + 128]
            value = qkv_ref[0:reach, at + 128 : at + 192]
            upstream = ctx_grad_ref[rows, mine]
            scores = dot(key, query, 1, 1)
            place = block * ROWS + lax.broadcasted_iota(jnp.int32, (1, ROWS), 1)
            start = starts_at(ends, place)
            key_place = lax.broadcasted_iota(jnp.int32, (reach, ROWS), 0)
            scores = jnp.where((key_place >= start) & (key_place <= place), scores, -1e30)
            raised = jnp.exp(scores - jnp.max(scores, axis=0, keepdims=True))
            prob = raised * (1.0 / jnp.sum(raised, axis=0, keepdims=True))
            prob_low = prob.astype(BF16)
            ctx = dot(value, prob_low, 0, 0)
            prob_grad = dot(value, upstream, 1, 1)
            row_dot = jnp.sum(prob_grad * prob, axis=0, keepdims=True)
            score_grad = (prob * (prob_grad - row_dot)).astype(BF16)
            query_grad = dot(key, score_grad, 0, 0)
            value_part = dot(prob_low, upstream, 1, 0)
            key_part = dot(score_grad, query, 1, 0)
            if reach == slot_len:
                value_sum[...] = value_part
                turn_sum[:, 64:128] = key_part
            else:
                value_sum[0:reach] += value_part
                turn_sum[0:reach, 64:128] += key_part
            turn_sum[rows, 0:64] = query_grad.T * HEAD_DIM**-0.5
            ctx_ref[rows, mine] = ctx.T.astype(BF16)
        both = turn_sum[...]
        both = both * cos_ref[...] - turned_halves(both) * sin_ref[...]
        qkv_grad_ref[:, at : at + 128] = both.astype(BF16)
        qkv_grad_ref[:, at + 128 : at + 192] = value_sum[...].astype(BF16)


def attention(lengths, qkv, ctx_grad, cosines, sines):
    slot_len = qkv.shape[0]
    pairs = qkv.shape[1] // 384

    def mine(columns):
        return pl.BlockSpec((slot_len, columns), lambda i: (0, i))

    return kernel_call(
        attention_kernel,
        "attention",
        [made(slot_len, 128 * pairs), made(slot_len, 384 * pairs)],
        grid=(pairs,),
        in_specs=[SCALARS, mine(384), mine(128), kept(cosines), kept(sines)],
        out_specs=[mine(128), mine(384)],
        scratch_shapes=[pltpu.VMEM((slot_len, 128), F32), pltpu.VMEM((slot_len, 64), F32)],
    )(lengths, qkv, ctx_grad, cosines, sines)


OFFSETS = tuple((planes, places) for planes in range(2) for places in range(4))
FAR = (1, 2)
CUTS = (0, 48, 96, 128)
PARTS = tuple(zip(CUTS, CUTS[1:]))
BLOCK_NAMES = tuple(o for o in OFFSETS if o != FAR) + (0, 1, 2)


def block_shapes(width):
    return [made(BLOCK, width)] * 7 + [made(high - low, width) for low, high in PARTS]


def block_specs(columns):
    heights = [BLOCK] * 7 + [high - low for low, high in PARTS]
    return [pl.BlockSpec((height, columns), lambda i, *_: (0, i)) for height in heights]


def store_blocks(places_ref, total, refs):
    def rows(offset, low, high):
        first = pl.multiple_of(places_ref[OFFSETS.index(offset)] * BLOCK, BLOCK)
        return total[pl.ds(first + low, high - low), :].astype(BF16)

    for name, ref in zip(BLOCK_NAMES, refs):
        if isinstance(name, int):
            ref[...] = rows(FAR, *PARTS[name])
        else:
            ref[...] = rows(name, 0, BLOCK)


def branch_kernel(ctx_ref, act_ref, w_dense_ref, w_fc2_ref, out_ref):
    out_ref[...] = (
        dot(ctx_ref[...], w_dense_ref[...], 1, 0) + dot(act_ref[...], w_fc2_ref[...], 1, 0)
    ).astype(BF16)


def branch(context, activated, w_dense, w_fc2):
    slot_len, width = context.shape[0], w_fc2.shape[1]

    def chunk(rows):
        return pl.BlockSpec((rows, 256), lambda i: (0, i))

    return kernel_call(
        branch_kernel,
        "branch",
        made(slot_len, width),
        grid=(width // 256,),
        in_specs=[
            kept(context),
            kept(activated),
            chunk(w_dense.shape[0]),
            chunk(w_fc2.shape[0]),
        ],
        out_specs=chunk(slot_len),
    )(context, activated, w_dense, w_fc2)


def units_kernel(grad_ref, w_fc2_ref, slope_ref, up_grad_ref, unit_sums_ref, grad_sums_ref):
    up_grad = (dot(grad_ref[...], w_fc2_ref[...], 1, 1) * slope_ref[...].astype(F32)).astype(BF16)
    up_grad_ref[...] = up_grad
    unit_sums_ref[...] = jnp.sum(up_grad.astype(F32), axis=0, keepdims=True)

    @pl.when(pl.program_id(0) == 0)
    def _():
        grad_sums_ref[...] = jnp.sum(grad_ref[...].astype(F32), axis=0, keepdims=True)


def units_back(grad, w_fc2, slope):
    slot_len, width = grad.shape
    units = w_fc2.shape[0]
    return kernel_call(
        units_kernel,
        "units",
        [made(slot_len, units), made(1, units, F32), made(1, width, F32)],
        grid=(units // 256,),
        in_specs=[
            kept(grad),
            pl.BlockSpec((256, width), lambda i: (i, 0)),
            pl.BlockSpec((slot_len, 256), lambda i: (0, i)),
        ],
        out_specs=[
            pl.BlockSpec((slot_len, 256), lambda i: (0, i)),
            pl.BlockSpec((1, 256), lambda i: (0, i)),
            pl.BlockSpec((1, width), lambda i: (0, 0)),
        ],
    )(grad, w_fc2, slope)


def hidden_kernel(
    places_ref,
    up_grad_ref,
    qkv_grad_ref,
    w_fc1_ref,
    w_qkv_ref,
    tokens_ref,
    stats_ref,
    gain_sum_ref,
    shift_sum_ref,
    head_sum_ref,
    *rest,
):
    *refs, total = rest
    part = dot(up_grad_ref[...], w_fc1_ref[...], 1, 1) + dot(
        qkv_grad_ref[...], w_qkv_ref[...], 1, 1
    )
    total[...] = part
    store_blocks(places_ref, total, refs)
    normed = (tokens_ref[...].astype(F32) - stats_ref[:, 0:1]) * stats_ref[:, 1:2]
    gain_sum_ref[...] = jnp.sum(part * normed, axis=0, keepdims=True)
    shift_sum_ref[...] = jnp.sum(part, axis=0, keepdims=True)

    @pl.when(pl.program_id(0) == 0)
    def _():
        head_sum_ref[...] = jnp.sum(qkv_grad_ref[...].astype(F32), axis=0, keepdims=True)


def hidden_blocks(places, up_grad, qkv_grad, w_fc1, w_qkv, tokens, stats):
    slot_len, width = tokens.shape

    def chunk(rows):
        return pl.BlockSpec((rows, 256), lambda i, *_: (0, i))

    gain_sum, shift_sum, head_sum, *blocks = kernel_call(
        hidden_kernel,
        "hidden",
        [made(1, width, F32), made(1, width, F32), made(1, qkv_grad.shape[1], F32)]
        + block_shapes(width),
        prefetch=1,
        grid=(width // 256,),
        in_specs=[
            kept(up_grad),
            kept(qkv_grad),
            pl.BlockSpec((256, w_fc1.shape[1]), lambda i, *_: (i, 0)),
            pl.BlockSpec((256, w_qkv.shape[1]), lambda i, *_: (i, 0)),
            chunk(slot_len),
            kept(stats),
        ],
        out_specs=[
            chunk(1),
            chunk(1),
            pl.BlockSpec((1, qkv_grad.shape[1]), lambda i, *_: (0, 0)),
        ]
        + block_specs(256),
        scratch_shapes=[pltpu.VMEM((slot_len, 256), F32)],
    )(places, up_grad, qkv_grad, w_fc1, w_qkv, tokens, stats)
    return gain_sum, shift_sum, head_sum, dict(zip(BLOCK_NAMES, blocks))


def weight_kernel(order_ref, left_a_ref, left_b_ref, first_ref, second_ref, *rest):
    *sums, out_ref = rest
    cut, end = first_ref.shape[1], first_ref.shape[1] + second_ref.shape[1]
    left = jnp.concatenate([left_a_ref[...], left_b_ref[...]], axis=1)
    out_ref[:, 0:cut] = dot(left, first_ref[...], 0, 0).astype(BF16)
    out_ref[:, cut:end] = dot(left, second_ref[...], 0, 0).astype(BF16)
    if sums:
        for half in range(2):
            block = order_ref[2 * pl.program_id(0) + half]
            lines = [ref[pl.ds(block, 1), :] for ref in sums]
            lines.append(jnp.zeros((BLOCK - len(lines), BLOCK), F32))
            columns = jnp.concatenate(lines, axis=0).T
            out_ref[half * BLOCK : half * BLOCK + BLOCK, end:] = columns.astype(BF16)


def weight_blocks(order, left, first, second, *sums):
    slot_len = left.shape[0]
    width = first.shape[1] + second.shape[1] + (BLOCK if sums else 0)
    return kernel_call(
        weight_kernel,
        "weights",
        made(left.shape[1], width),
        prefetch=1,
        grid=(left.shape[1] // (2 * BLOCK),),
        in_specs=[
            pl.BlockSpec((slot_len, BLOCK), lambda i, order: (0, order[2 * i])),
            pl.BlockSpec((slot_len, BLOCK), lambda i, order: (0, order[2 * i + 1])),
            kept(first),
            kept(second),
            *[kept(array) for array in sums],
        ],
        out_specs=pl.BlockSpec((2 * BLOCK, width), lambda i, order: (i, 0)),
    )(order, left, left, first, second, *sums)


def combine(name, *sums):
    arrays = [term[0] for terms in sums for term in terms]
    specs = [
        pl.BlockSpec((term[1], term[0].shape[1]), functools.partial(lambda at, _: (at, 0), term[2]))
        for terms in sums
        for term in terms
    ]
    heights = [max(term[4] for term in terms) for terms in sums]

    def kernel(*refs):
        ins, outs = list(refs[: len(arrays)]), refs[len(arrays) :]
        for terms, height, out in zip(sums, heights, outs):
            mine = [(ins.pop(0), term[3], term[4]) for term in terms]
            cuts = sorted({cut for _, low, high in mine for cut in (low, high)})
            for low, high in zip(cuts, cuts[1:]):
                parts = [
                    ref[low - first : high - first, :].astype(F32)
                    for ref, first, last in mine
                    if first <= low and high <= last
                ]
                out[low:high, :] = functools.reduce(lambda a, b: a + b, parts).astype(BF16)

    shapes = [made(height, terms[0][0].shape[1]) for height, terms in zip(heights, sums)]
    return kernel_call(
        kernel,
        name,
        shapes,
        grid=(1,),
        in_specs=specs,
        out_specs=[pl.BlockSpec(shape.shape, lambda _: (0, 0)) for shape in shapes],
    )(*arrays)


def whole_term(array, low=0):
    return (array, array.shape[0], 0, low, low + array.shape[0])


def output_kernel(lengths_ref, tokens_ref, branch_ref, b_dense_ref, b_fc2_ref, out_ref):
    bias = b_dense_ref[...].astype(F32) + b_fc2_ref[...].astype(F32)
    rows = tokens_ref.shape[0]
    place = pl.program_id(0) * rows + lax.broadcasted_iota(jnp.int32, (rows, 1), 0)
    total = jnp.where(
        place < ends_of(lengths_ref)[-1], branch_ref[...].astype(F32) + bias[None], 0.0
    )
    out_ref[...] = (tokens_ref[...].astype(F32) + total).astype(BF16)


def finish_output(lengths, tokens, branch_sum, b_dense, b_fc2):
    slot_len, width = tokens.shape
    row = pl.BlockSpec((ROWS, width), lambda i: (i, 0))
    return kernel_call(
        output_kernel,
        "output",
        made(slot_len, width),
        grid=(slot_len // ROWS,),
        in_specs=[SCALARS, row, row, kept(b_dense), kept(b_fc2)],
        out_specs=row,
    )(lengths, tokens, branch_sum, b_dense, b_fc2)


def input_kernel(places_ref, *refs):
    *terms, tokens_ref, cot_ref, stats_ref, gain_ref, out_ref = refs
    total = functools.reduce(lambda a, b: a + b, [t[...].astype(F32) for t in terms])
    inv_sigma = stats_ref[:, 1:2]
    normed = (tokens_ref[...].astype(F32) - stats_ref[:, 0:1]) * inv_sigma
    scaled = total * gain_ref[...].astype(F32)[None]
    out_ref[...] = (
        cot_ref[...].astype(F32)
        + inv_sigma
        * (
            scaled
            - jnp.mean(scaled, axis=1, keepdims=True)
            - normed * jnp.mean(scaled * normed, axis=1, keepdims=True)
        )
    ).astype(BF16)


def input_rows(places, terms, tokens, cot, stats, gain):
    width = tokens.shape[1]

    def mine(columns):
        return pl.BlockSpec((BLOCK, columns), lambda i, places: (places[0], 0))

    return kernel_call(
        input_kernel,
        "input",
        made(BLOCK, width),
        prefetch=1,
        grid=(1,),
        in_specs=[kept(t) for t in terms] + [mine(width), mine(width), mine(128), kept(gain)],
        out_specs=pl.BlockSpec((BLOCK, width), lambda *_: (0, 0)),
    )(places, *terms, tokens, cot, stats, gain)


def place_kernel(blocks, places_ref, *refs):
    pieces, out_ref, sems = refs[: len(blocks)], refs[-2], refs[-1]
    copies = []
    for i, ((offset, low, high), piece) in enumerate(zip(blocks, pieces)):
        first = pl.multiple_of(places_ref[OFFSETS.index(offset)] * BLOCK, BLOCK)
        copies.append(
            pltpu.make_async_copy(
                piece, out_ref.at[pl.ds(first + low, high - low), :], sems.at[i]
            )
        )
    for copy in copies:
        copy.start()
    for copy in copies:
        copy.wait()


def place_rows(places, blocks, pieces, whole=None):
    rest = {} if whole is None else {"input_output_aliases": {len(pieces) + 1: 0}}
    given = [] if whole is None else [whole]
    return kernel_call(
        functools.partial(place_kernel, blocks),
        "place",
        made(8 * BLOCK, pieces[0].shape[1]),
        in_specs=[SCALARS] + [NEAR] * len(pieces) + [AWAY] * len(given),
        out_specs=AWAY,
        scratch_shapes=[pltpu.SemaphoreType.DMA((len(pieces),))],
        **rest,
    )(places, *pieces, *given)


def up_kernel(near_ref, far_ref, first_ref, second_ref, sums_ref):
    total = near_ref[...].astype(F32) + far_ref[...].astype(F32)
    cut, end = first_ref.shape[1], first_ref.shape[1] + second_ref.shape[1]
    first_ref[...] = total[:, :cut]
    second_ref[...] = total[:, cut:end]
    sums_ref[...] = total[:, end:].T[: sums_ref.shape[0]]


def down_kernel(near_ref, far_ref, first_ref, second_ref):
    total = near_ref[...].astype(F32) + far_ref[...].astype(F32)
    cut = first_ref.shape[0]
    first_ref[...] = total[:, :cut].T
    second_ref[...] = total[:, cut:].T


def last_sum(kernel, name, shapes, near, far):
    return kernel_call(
        kernel,
        name,
        [made(*shape, F32) for shape in shapes],
        grid=(1,),
        in_specs=[pl.BlockSpec(far.shape, lambda _: (0, 0))] * 2,
        out_specs=[pl.BlockSpec(shape, lambda _: (0, 0)) for shape in shapes],
    )(near, far)


def shift(array, axis, size, by):
    return lax.ppermute(array, axis, [(i, (i + by) % size) for i in range(size)])


def y_up(array):
    return shift(array, "y", 4, 1)


def y_down(array):
    return shift(array, "y", 4, 3)


def across(array):
    return shift(array, "zl", 2, 1)


def after(arrays, *earlier):
    return lax.optimization_barrier((arrays, earlier))[0]


class TensorSum:
    def __init__(self, blocks):
        self.blocks = blocks

    def send_far(self, earlier):
        b = self.blocks
        sent = after([b[0], b[1], b[2], b[(0, 3)]], earlier)
        self.far = across(sent[0]), y_up(sent[1]), y_down(sent[2])
        self.near = [y_down(sent[3])]
        return sent

    def send_middle(self, earlier):
        b = self.blocks
        far = after(self.far, earlier)
        sent = combine(
            "middle",
            *[
                [whole_term(b[offset]), whole_term(part, low)]
                for offset, part, (low, _) in zip(((0, 2), (1, 1), (1, 3)), far, PARTS)
            ],
        )
        self.middle = y_up(sent[0]), across(sent[1]), y_down(sent[2])
        return sent

    def send_near(self, earlier):
        b = self.blocks
        two_on, diagonal, other = after(self.middle, earlier)
        sent = combine(
            "near",
            [whole_term(b[(0, 1)]), whole_term(two_on), whole_term(diagonal)],
            [whole_term(b[(1, 0)]), whole_term(other)],
        )
        self.near += [y_up(sent[0]), across(sent[1])]
        return sent

    def terms(self, earlier):
        return after([self.blocks[(0, 0)], *self.near], earlier)


class TensorGather:
    def __init__(self, places, rows):
        self.places, self.rows = places, rows
        self.one = y_up(rows), y_down(rows), across(rows)

    def second(self, earlier):
        before, ahead, partner = self.one = after(self.one, earlier)
        self.two = y_down(ahead), across(ahead), y_up(partner)
        return self.one

    def third(self, earlier):
        two_on, diagonal, other = self.two = after(self.two, earlier)
        (a, b), (c, d), (e, f) = PARTS
        self.three = across(two_on[a:b]), y_down(diagonal[c:d]), y_up(other[e:f])
        blocks = [(0, 0), (0, 3), (0, 1), (1, 0), (0, 2), (1, 1), (1, 3)]
        self.whole = place_rows(
            self.places,
            [(offset, 0, BLOCK) for offset in blocks],
            [self.rows, *self.one, *self.two],
        )
        return self.whole

    def finish(self, earlier):
        parts = after(self.three, earlier)
        return place_rows(
            self.places, [(FAR, low, high) for low, high in PARTS], list(parts), self.whole
        )


class DataSum:
    def __init__(self, partial_sums, earlier):
        self.near = lax.psum_scatter(
            after(partial_sums, earlier), ("x", "core"), scatter_dimension=0, tiled=True
        )

    def send(self, earlier):
        self.near = after(self.near, earlier)
        self.far = shift(self.near[BLOCK:], "zh", 2, 1)

    def finish(self, kernel, name, shapes, earlier):
        near, far = after([self.near, self.far], earlier)
        return last_sum(kernel, name, shapes, near, far)


def dp_order():
    half = lax.axis_index("zh")
    return jnp.stack(
        [(half + part) % 2 * 8 + block for block in range(8) for part in range(2)]
    ).astype(jnp.int32)


def per_device(
    tokens,
    cotangent,
    seq_lengths,
    ln_gain,
    ln_bias,
    w_qkv,
    b_qkv,
    w_dense,
    b_dense,
    w_fc1,
    b_fc1,
    w_fc2,
    b_fc2,
):
    units = w_fc2.shape[0]
    plane, place = lax.axis_index("zl"), lax.axis_index("y")
    places = jnp.stack(
        [(plane + planes) % 2 * 4 + (place + steps) % 4 for planes, steps in OFFSETS]
    ).astype(jnp.int32)
    order = dp_order()
    frequency = 10000.0 ** (-jnp.arange(ROTARY // 2, dtype=F32) * 2.0 / ROTARY)
    frequency = jnp.tile(frequency, 8)[None]
    hidden, grad, qkv, activated, slope, ctx_grad, cosines, sines, stats = front(
        seq_lengths,
        frequency,
        tokens,
        cotangent,
        ln_gain,
        ln_bias,
        b_qkv,
        b_fc1,
        w_qkv,
        w_fc1,
        w_dense,
    )
    context, qkv_grad = attention(seq_lengths, qkv, ctx_grad, cosines, sines)
    branch_part = branch(context, activated, w_dense, w_fc2)
    branch_sum = lax.psum(branch_part, TENSOR)
    up_grad, unit_sum, grad_sum = units_back(*after((grad, w_fc2, slope), branch_part))
    gain_sum, shift_sum, head_sum, blocks = hidden_blocks(
        places, up_grad, qkv_grad, w_fc1, w_qkv, tokens, stats
    )
    backward = TensorSum(blocks)
    sums = [
        gain_sum.reshape(16, -1),
        shift_sum.reshape(16, -1),
        grad_sum.reshape(16, -1),
        jnp.pad(head_sum.reshape(16, -1), ((0, 0), (0, 80))),
        jnp.pad(unit_sum.reshape(16, -1), ((0, 0), (0, 64))),
    ]
    done = backward.send_far(())
    up_part = weight_blocks(order, *after((hidden, up_grad, qkv_grad, *sums), done))
    done = backward.send_middle(up_part)
    up = DataSum(up_part, done)
    down_part = weight_blocks(order, *after((grad, activated, context), done))
    done = backward.send_near(down_part)
    down = DataSum(down_part, done)
    in_rows = input_rows(places, backward.terms((down_part, branch_sum)), tokens, cotangent, stats, ln_gain)
    input_grad = TensorGather(places, in_rows)
    up.send(in_rows)
    output = finish_output(seq_lengths, tokens, after(branch_sum, up.near), b_dense, b_fc2)
    done = input_grad.second(output)
    down.send(done)
    grad_fc1, grad_qkv, small = up.finish(
        up_kernel,
        "up",
        ((BLOCK, units), (BLOCK, w_qkv.shape[1]), (8, BLOCK)),
        down.near,
    )
    norm_sum = lax.psum(small[:2], TENSOR)
    input_grad.third(norm_sum)
    grad_fc2, grad_dense = down.finish(
        down_kernel, "down", ((units, BLOCK), (w_dense.shape[0], BLOCK)), input_grad.whole
    )
    input_grad = input_grad.finish(grad_dense)
    out_bias = small[2]
    return (
        output,
        input_grad,
        norm_sum[0],
        norm_sum[1],
        grad_qkv,
        small[3, :48],
        grad_dense,
        out_bias,
        grad_fc1,
        small[4, :64],
        grad_fc2,
        out_bias,
    )


def solution(mesh):
    parts = Mesh(mesh.devices.reshape(2, 4, 2, 2, 4), DP + TENSOR)
    rows = P(DP, None)
    placed = (
        rows,
        rows,
        rows,
        P(),
        P(),
        P(None, TENSOR),
        P(TENSOR),
        P(TENSOR, None),
        P(),
        P(None, TENSOR),
        P(TENSOR),
        P(TENSOR, None),
        P(),
    )
    return jax.shard_map(
        per_device,
        mesh=parts,
        in_specs=placed,
        out_specs=(
            rows,
            rows,
            P(DP),
            P(DP),
            P(DP, TENSOR),
            P(TENSOR + DP),
            P(TENSOR, DP),
            P(DP),
            P(DP, TENSOR),
            P(TENSOR + DP),
            P(TENSOR, DP),
            P(DP),
        ),
        check_vma=False,
    )
```

```python
import functools

import jax
import jax.numpy as jnp
from jax import lax
from jax.experimental import pallas as pl
from jax.experimental.pallas import tpu as pltpu
from jax.sharding import Mesh
from jax.sharding import PartitionSpec as P

HEAD_DIM = 64
ROTARY = 32
DP = ("zh", "x", "core")
TENSOR = ("zl", "y")
BF16 = jnp.bfloat16
F32 = jnp.float32
ROWS = 256
QUERIES = 512
BLOCK = 128
AT_ONCE = 4
VMEM_BYTES = 56 * 2**20
GELU = 0.7978845608


def dot(left, right, left_dim, right_dim):
    return lax.dot_general(
        left, right, (((left_dim,), (right_dim,)), ((), ())), preferred_element_type=F32
    )


def kernel_call(kernel, name, out_shape, prefetch=0, vmem=VMEM_BYTES, flops=1, **spec):
    if prefetch:
        spec = {
            "grid_spec": pltpu.PrefetchScalarGridSpec(
                num_scalar_prefetch=prefetch,
                grid=spec.pop("grid"),
                in_specs=spec.pop("in_specs"),
                out_specs=spec.pop("out_specs"),
                scratch_shapes=spec.pop("scratch_shapes", ()),
            ),
            **spec,
        }
    return pl.pallas_call(
        kernel,
        out_shape=out_shape,
        compiler_params=pltpu.CompilerParams(vmem_limit_bytes=vmem),
        cost_estimate=pl.CostEstimate(flops=flops, bytes_accessed=1, transcendentals=0),
        name=name,
        **spec,
    )


def made(rows, columns, kind=BF16):
    return jax.ShapeDtypeStruct((rows, columns), kind)


def kept(array):
    return pl.BlockSpec(array.shape, lambda *_: (0,) * array.ndim)


AWAY = pl.BlockSpec(memory_space=pltpu.HBM)
NEAR = pl.BlockSpec(memory_space=pltpu.VMEM)
SCALARS = pl.BlockSpec(memory_space=pltpu.SMEM)


def ends_of(lengths_ref):
    ends = []
    total = jnp.int32(0)
    for place in range(lengths_ref.shape[1]):
        total = total + lengths_ref[0, place]
        ends.append(total)
    return ends


def starts_at(ends, places):
    start = jnp.zeros_like(places)
    for end in ends:
        start = jnp.maximum(start, jnp.where(places >= end, end, 0))
    return start


def turned_halves(columns):
    lane = lax.broadcasted_iota(jnp.int32, columns.shape, 1)
    return jnp.where(
        lane % ROTARY < ROTARY // 2, pltpu.roll(columns, 112, 1), pltpu.roll(columns, 16, 1)
    )


class Copies:
    def __init__(self, sems):
        self.sems, self.made = sems, {}

    def start(self, name, source, target):
        copy = pltpu.make_async_copy(source, target, self.sems.at[len(self.made)])
        self.made[name] = copy
        copy.start()

    def wait(self, *names):
        for name in names:
            self.made[name].wait()


def forward_kernel(
    lengths_ref,
    freq_ref,
    gain_ref,
    bias_ref,
    b_qkv_ref,
    b_fc1_ref,
    tokens_hbm,
    cot_hbm,
    w_qkv_hbm,
    w_fc1_hbm,
    w_dense_hbm,
    w_fc2_hbm,
    hidden_hbm,
    grad_hbm,
    act_hbm,
    slope_hbm,
    ctx_hbm,
    qkv_grad_hbm,
    stats_hbm,
    branch_hbm,
    tokens,
    grad,
    hidden,
    w_qkv,
    w_fc1,
    w_dense,
    w_fc2,
    qkv,
    act,
    slope,
    ctx_grad,
    ctx,
    qkv_grad,
    cosines,
    sines,
    stats,
    turn_sum,
    value_sum,
    sems,
):
    slot_len, width = tokens.shape
    blocks = slot_len // ROWS
    copies = Copies(sems)
    ends = ends_of(lengths_ref)

    def rows_of(block, blocks_each=1):
        return slice(block * ROWS, (block + blocks_each) * ROWS)

    def bring_rows(block):
        at = rows_of(block)
        copies.start(("tokens", block), tokens_hbm.at[at, :], tokens.at[at, :])
        copies.start(("cot", block), cot_hbm.at[at, :], grad.at[at, :])

    def bring(name, source, target):
        copies.start(name, source, target)

    def send_rows(name, block, source, target):
        at = rows_of(block)
        copies.start((name, block), source.at[at, :], target.at[at, :])

    def normalise(block, part, parts=4):
        height = ROWS // parts
        first = block * ROWS + part * height
        at = slice(first, first + height)
        places = first + lax.broadcasted_iota(jnp.int32, (height, 128), 0)
        lane = lax.broadcasted_iota(jnp.int32, (height, 128), 1)
        position = (places - starts_at(ends, places)).astype(F32)
        angle = position * freq_ref[...]
        cosines[at, :] = jnp.where(lane % HEAD_DIM < ROTARY, jnp.cos(angle), 1.0)
        sine = jnp.sin(angle)
        sines[at, :] = jnp.where(
            lane % HEAD_DIM < ROTARY // 2, -sine, jnp.where(lane % HEAD_DIM < ROTARY, sine, 0.0)
        )
        valid = (places < ends[-1])[:, :1]
        inputs = tokens[at, :].astype(F32)
        mean = jnp.mean(inputs, axis=1, keepdims=True)
        center = inputs - mean
        inv_sigma = lax.rsqrt(jnp.mean(center * center, axis=1, keepdims=True) + 1e-05)
        stats[at, :] = jnp.where(lane == 0, mean, inv_sigma)
        hidden[at, :] = (
            center * inv_sigma * gain_ref[...].astype(F32)[None]
            + bias_ref[...].astype(F32)[None]
        ).astype(BF16)
        grad[at, :] = jnp.where(valid, grad[at, :], jnp.zeros((height, width), BF16))

    def turn(at, projected):
        lane = lax.broadcasted_iota(jnp.int32, (ROWS, 128), 1)
        cosine, sine = cosines[at, :], sines[at, :]
        for block in range(qkv.shape[1] // 128):
            columns = slice(block * 128, block * 128 + 128)
            plain = projected[:, columns]
            turned = plain * cosine + turned_halves(plain) * sine
            if block % 3 == 1:
                turned = jnp.where(lane < HEAD_DIM, plain, turned)
            if block % 3 == 2:
                turned = jnp.where(lane < HEAD_DIM, turned, plain)
            qkv[at, columns] = turned.astype(BF16)

    def activate(at, up, columns):
        square = up * up
        share = 0.5 * jnp.tanh(up * (GELU + (GELU * 0.044715) * square)) + 0.5
        active = up * share
        act[at, columns] = active.astype(BF16)
        slope[at, columns] = (
            share + active * (1.0 - share) * (2 * GELU + (6 * GELU * 0.044715) * square)
        ).astype(BF16)

    def multiply(block, between):
        at = rows_of(block)
        if block == 0:
            copies.wait("w_qkv")
        between(0)
        projected = dot(hidden[at, :], w_qkv[...], 1, 0) + b_qkv_ref[...].astype(F32)[None]
        between(1)
        turn(at, projected)
        if block == 0:
            copies.wait("w_fc1", "w_dense")
        half = w_fc1.shape[1] // 2
        for part in range(2):
            columns = slice(part * half, part * half + half)
            up = dot(hidden[at, :], w_fc1[:, columns], 1, 0)
            up = up + b_fc1_ref[columns].astype(F32)[None]
            between(2 + part)
            activate(at, up, columns)
        ctx_grad[at, :] = dot(grad[at, :], w_dense[...], 1, 1).astype(BF16)

    def attend(head):
        at = 3 * HEAD_DIM * head
        mine = slice(HEAD_DIM * head, HEAD_DIM * head + HEAD_DIM)
        for block in reversed(range(slot_len // QUERIES)):
            rows = slice(block * QUERIES, block * QUERIES + QUERIES)
            reach = (block + 1) * QUERIES
            query = qkv[rows, at : at + 64] * BF16(HEAD_DIM**-0.5)
            key = qkv[0:reach, at + 64 : at + 128]
            value = qkv[0:reach, at + 128 : at + 192]
            upstream = ctx_grad[rows, mine]
            scores = dot(key, query, 1, 1)
            place = block * QUERIES + lax.broadcasted_iota(jnp.int32, (1, QUERIES), 1)
            start = starts_at(ends, place)
            key_place = lax.broadcasted_iota(jnp.int32, (reach, QUERIES), 0)
            scores = jnp.where((key_place >= start) & (key_place <= place), scores, -1e30)
            raised = jnp.exp(scores - jnp.max(scores, axis=0, keepdims=True))
            prob = raised * (1.0 / jnp.sum(raised, axis=0, keepdims=True))
            prob_low = prob.astype(BF16)
            context = dot(value, prob_low, 0, 0)
            prob_grad = dot(value, upstream, 1, 1)
            row_dot = jnp.sum(prob_grad * prob, axis=0, keepdims=True)
            score_grad = (prob * (prob_grad - row_dot)).astype(BF16)
            query_grad = dot(key, score_grad, 0, 0)
            value_part = dot(prob_low, upstream, 1, 0)
            key_part = dot(score_grad, query, 1, 0)
            if reach == slot_len:
                value_sum[...] = value_part
                turn_sum[:, 64:128] = key_part
            else:
                value_sum[0:reach] += value_part
                turn_sum[0:reach, 64:128] += key_part
            turn_sum[rows, 0:64] = query_grad.T * HEAD_DIM**-0.5
            ctx[rows, mine] = context.T.astype(BF16)
        both = turn_sum[...]
        both = both * cosines[...] - turned_halves(both) * sines[...]
        qkv_grad[:, at : at + 128] = both.astype(BF16)
        qkv_grad[:, at + 128 : at + 192] = value_sum[...].astype(BF16)

    bring_rows(0)
    bring("w_qkv", w_qkv_hbm, w_qkv)
    bring_rows(1)
    bring("w_fc1", w_fc1_hbm, w_fc1)
    bring("w_dense", w_dense_hbm, w_dense)
    copies.wait(("tokens", 0), ("cot", 0))
    for block in range(2, blocks):
        bring_rows(block)
    bring("w_fc2", w_fc2_hbm, w_fc2)
    for part in range(4):
        normalise(0, part)
    for block in range(blocks):
        send_rows("hidden", block, hidden, hidden_hbm)
        send_rows("grad", block, grad, grad_hbm)
        if block + 1 < blocks:
            copies.wait(("tokens", block + 1), ("cot", block + 1))
            multiply(block, functools.partial(normalise, block + 1))
        else:
            multiply(block, lambda part: None)
        send_rows("act", block, act, act_hbm)
        send_rows("slope", block, slope, slope_hbm)
    copies.start("stats", stats, stats_hbm)
    for head in range(qkv.shape[1] // (3 * HEAD_DIM)):
        attend(head)
    copies.start("ctx", ctx, ctx_hbm)
    copies.start("qkv_grad", qkv_grad, qkv_grad_hbm)
    copies.wait("w_fc2")
    size = 512
    for part in range(width // size):
        columns = slice(part * size, part * size + size)
        tokens[:, columns] = (
            dot(ctx[...], w_dense[:, columns], 1, 0) + dot(act[...], w_fc2[:, columns], 1, 0)
        ).astype(BF16)
        copies.start(("branch", part), tokens.at[:, columns], branch_hbm.at[:, columns])
    brought = {"w_qkv", "w_fc1", "w_dense", "w_fc2"}
    copies.wait(
        *[
            name
            for name in copies.made
            if name not in brought and name[0] not in ("tokens", "cot")
        ]
    )


def forward(lengths, freq, tokens, cot, gain, bias, b_qkv, b_fc1, w_qkv, w_fc1, w_dense, w_fc2):
    slot_len, width = tokens.shape
    units, heads, ctx_width = w_fc2.shape[0], w_qkv.shape[1], w_dense.shape[0]
    row_kinds = (width, width, units, units, ctx_width, heads)

    def room(rows, columns, kind=BF16):
        return pltpu.VMEM((rows, columns), kind)

    return kernel_call(
        forward_kernel,
        "forward",
        [made(slot_len, columns) for columns in row_kinds]
        + [made(slot_len, 128, F32), made(slot_len, width)],
        grid=(1,),
        in_specs=[SCALARS] + [kept(a) for a in (freq, gain, bias, b_qkv, b_fc1)] + [AWAY] * 6,
        out_specs=[AWAY] * 8,
        scratch_shapes=[room(slot_len, width)] * 3
        + [pltpu.VMEM(w.shape, BF16) for w in (w_qkv, w_fc1, w_dense, w_fc2)]
        + [
            room(slot_len, heads),
            room(slot_len, units),
            room(slot_len, units),
            room(slot_len, ctx_width),
            room(slot_len, ctx_width),
            room(slot_len, heads),
        ]
        + [room(slot_len, 128, F32)] * 4
        + [room(slot_len, 64, F32), pltpu.SemaphoreType.DMA((48,))],
    )(lengths, freq, gain, bias, b_qkv, b_fc1, tokens, cot, w_qkv, w_fc1, w_dense, w_fc2)


OFFSETS = tuple((planes, places) for planes in range(2) for places in range(4))
FAR = (1, 2)
CUTS = (0, 48, 96, 128)
PARTS = tuple(zip(CUTS, CUTS[1:]))
BLOCK_NAMES = tuple(o for o in OFFSETS if o != FAR) + (0, 1, 2)


def block_shapes(width):
    return [made(BLOCK, width)] * 7 + [made(high - low, width) for low, high in PARTS]


def backward_kernel(
    places_ref,
    grad_hbm,
    slope_hbm,
    qkv_grad_hbm,
    tokens_hbm,
    stats_hbm,
    w_fc2_hbm,
    w_fc1_hbm,
    w_qkv_hbm,
    gain_sum_ref,
    shift_sum_ref,
    grad_sum_ref,
    head_sum_ref,
    unit_sum_ref,
    up_grad_hbm,
    *rest,
):
    blocks, scratch = rest[: len(BLOCK_NAMES)], rest[len(BLOCK_NAMES) :]
    grad, slope, qkv_grad, tokens, stats, w_fc2, w_fc1, w_qkv, up_grad, hidden, sems = scratch
    copies = Copies(sems)
    slot_len, width = grad.shape
    units, size = w_fc2.shape[0], 512

    def part_of(part):
        return slice(part * size, part * size + size)

    def bring_rows(name, part, source, target):
        at = part_of(part)
        copies.start((name, part), source.at[at, :], target.at[at, :])

    def add_to(ref, columns, array, fresh):
        total = jnp.sum(array, axis=0, keepdims=True)
        ref[:, columns] = total if fresh else ref[:, columns] + total

    def to_units(rows, part):
        at, columns = part_of(rows), part_of(part)
        up = dot(grad[at, :], w_fc2[columns, :], 1, 1) * slope[at, columns].astype(F32)
        up = up.astype(BF16)
        up_grad[at, columns] = up
        add_to(unit_sum_ref, columns, up.astype(F32), rows == 0)

    def to_hidden(rows, part):
        at, columns = part_of(rows), part_of(part)
        result = dot(up_grad[at, :], w_fc1[columns, :], 1, 1) + dot(
            qkv_grad[at, :], w_qkv[columns, :], 1, 1
        )
        hidden[at, columns] = result.astype(BF16)
        normed = (tokens[at, columns].astype(F32) - stats[at, 0:1]) * stats[at, 1:2]
        add_to(gain_sum_ref, columns, result * normed, rows == 0)
        add_to(shift_sum_ref, columns, result, rows == 0)

    bring_rows("w_fc2", 0, w_fc2_hbm, w_fc2)
    for rows in range(2):
        bring_rows("grad", rows, grad_hbm, grad)
        bring_rows("slope", rows, slope_hbm, slope)
    bring_rows("w_fc2", 1, w_fc2_hbm, w_fc2)
    copies.wait(("w_fc2", 0), ("grad", 0), ("slope", 0))
    copies.start("w_fc1", w_fc1_hbm, w_fc1)
    copies.start("w_qkv", w_qkv_hbm, w_qkv)
    copies.start("qkv_grad", qkv_grad_hbm, qkv_grad)
    copies.start("tokens", tokens_hbm, tokens)
    copies.start("stats", stats_hbm, stats)
    to_units(0, 0)
    copies.wait(("w_fc2", 1))
    to_units(0, 1)
    copies.wait(("grad", 1), ("slope", 1))
    to_units(1, 0)
    to_units(1, 1)
    copies.start("up_grad", up_grad, up_grad_hbm)
    everything = slice(0, width)
    for rows in range(2):
        add_to(grad_sum_ref, everything, grad[part_of(rows), :].astype(F32), rows == 0)
    copies.wait("w_fc1", "w_qkv", "qkv_grad", "tokens", "stats")
    add_to(head_sum_ref, slice(0, qkv_grad.shape[1]), qkv_grad[...].astype(F32), True)
    for part in range(width // size):
        for rows in range(slot_len // size):
            to_hidden(rows, part)
        columns = part_of(part)
        for name, ref in zip(BLOCK_NAMES, blocks):
            low, high = PARTS[name] if isinstance(name, int) else (0, BLOCK)
            place = places_ref[OFFSETS.index(FAR if isinstance(name, int) else name)]
            first = pl.multiple_of(place * BLOCK, BLOCK) + low
            copies.start(
                ("block", name, part),
                hidden.at[pl.ds(first, high - low), columns],
                ref.at[:, columns],
            )
    copies.wait(
        "up_grad",
        *[("block", name, part) for name in BLOCK_NAMES for part in range(width // size)],
    )


def backward(places, grad, slope, qkv_grad, tokens, stats, w_fc2, w_fc1, w_qkv):
    slot_len, width = tokens.shape
    units, heads = w_fc2.shape[0], w_qkv.shape[1]
    sums = [made(1, size, F32) for size in (width, width, width, heads, units)]
    arrays = (grad, slope, qkv_grad, tokens, stats, w_fc2, w_fc1, w_qkv)
    gain_sum, shift_sum, grad_sum, head_sum, unit_sum, up_grad, *blocks = kernel_call(
        backward_kernel,
        "backward",
        sums + [made(slot_len, units)] + block_shapes(width),
        grid=(1,),
        in_specs=[SCALARS] + [AWAY] * len(arrays),
        out_specs=[kept(array) for array in sums] + [AWAY] * (1 + len(BLOCK_NAMES)),
        scratch_shapes=[pltpu.VMEM(array.shape, array.dtype) for array in arrays]
        + [pltpu.VMEM((slot_len, units), BF16), pltpu.VMEM((slot_len, width), BF16)]
        + [pltpu.SemaphoreType.DMA((64,))],
    )(places, *arrays)
    small = (gain_sum, shift_sum, grad_sum, head_sum, unit_sum)
    return up_grad, small, dict(zip(BLOCK_NAMES, blocks))


def weight_kernel(order_ref, *refs):
    lefts, (first_ref, second_ref, *sums, out_ref) = refs[:AT_ONCE], refs[AT_ONCE:]
    cut, end = first_ref.shape[1], first_ref.shape[1] + second_ref.shape[1]
    left = jnp.concatenate([ref[...] for ref in lefts], axis=1)
    out_ref[:, 0:cut] = dot(left, first_ref[...], 0, 0).astype(BF16)
    out_ref[:, cut:end] = dot(left, second_ref[...], 0, 0).astype(BF16)
    if sums:
        for half in range(AT_ONCE):
            block = order_ref[AT_ONCE * pl.program_id(0) + half]
            lines = [ref[pl.ds(block, 1), :] for ref in sums]
            lines.append(jnp.zeros((BLOCK - len(lines), BLOCK), F32))
            columns = jnp.concatenate(lines, axis=0).T
            out_ref[half * BLOCK : half * BLOCK + BLOCK, end:] = columns.astype(BF16)


def weight_blocks(order, left, first, second, *sums):
    slot_len = left.shape[0]
    width = first.shape[1] + second.shape[1] + (BLOCK if sums else 0)
    return kernel_call(
        weight_kernel,
        "weights",
        made(left.shape[1], width),
        prefetch=1,
        grid=(left.shape[1] // (AT_ONCE * BLOCK),),
        in_specs=[
            *[
                pl.BlockSpec(
                    (slot_len, BLOCK),
                    functools.partial(lambda at, i, order: (0, order[AT_ONCE * i + at]), at),
                )
                for at in range(AT_ONCE)
            ],
            kept(first),
            kept(second),
            *[kept(array) for array in sums],
        ],
        out_specs=pl.BlockSpec((AT_ONCE * BLOCK, width), lambda i, order: (i, 0)),
    )(order, *[left] * AT_ONCE, first, second, *sums)


def combine(name, *sums):
    arrays = [term[0] for terms in sums for term in terms]
    specs = [
        pl.BlockSpec((term[1], term[0].shape[1]), functools.partial(lambda at, _: (at, 0), term[2]))
        for terms in sums
        for term in terms
    ]
    heights = [max(term[4] for term in terms) for terms in sums]

    def kernel(*refs):
        ins, outs = list(refs[: len(arrays)]), refs[len(arrays) :]
        for terms, height, out in zip(sums, heights, outs):
            mine = [(ins.pop(0), term[3], term[4]) for term in terms]
            cuts = sorted({cut for _, low, high in mine for cut in (low, high)})
            for low, high in zip(cuts, cuts[1:]):
                parts = [
                    ref[low - first : high - first, :].astype(F32)
                    for ref, first, last in mine
                    if first <= low and high <= last
                ]
                out[low:high, :] = functools.reduce(lambda a, b: a + b, parts).astype(BF16)

    shapes = [made(height, terms[0][0].shape[1]) for height, terms in zip(heights, sums)]
    return kernel_call(
        kernel,
        name,
        shapes,
        grid=(1,),
        in_specs=specs,
        out_specs=[pl.BlockSpec(shape.shape, lambda _: (0, 0)) for shape in shapes],
    )(*arrays)


def whole_term(array, low=0):
    return (array, array.shape[0], 0, low, low + array.shape[0])


def output_kernel(lengths_ref, tokens_ref, branch_ref, b_dense_ref, b_fc2_ref, out_ref):
    bias = b_dense_ref[...].astype(F32) + b_fc2_ref[...].astype(F32)
    rows = tokens_ref.shape[0]
    place = pl.program_id(0) * rows + lax.broadcasted_iota(jnp.int32, (rows, 1), 0)
    total = jnp.where(
        place < ends_of(lengths_ref)[-1], branch_ref[...].astype(F32) + bias[None], 0.0
    )
    out_ref[...] = (tokens_ref[...].astype(F32) + total).astype(BF16)


def finish_output(lengths, tokens, branch_sum, b_dense, b_fc2):
    slot_len, width = tokens.shape
    row = pl.BlockSpec((ROWS, width), lambda i: (i, 0))
    return kernel_call(
        output_kernel,
        "output",
        made(slot_len, width),
        grid=(slot_len // ROWS,),
        in_specs=[SCALARS, row, row, kept(b_dense), kept(b_fc2)],
        out_specs=row,
    )(lengths, tokens, branch_sum, b_dense, b_fc2)


def input_kernel(places_ref, *refs):
    *terms, tokens_ref, cot_ref, stats_ref, gain_ref, out_ref = refs
    total = functools.reduce(lambda a, b: a + b, [t[...].astype(F32) for t in terms])
    inv_sigma = stats_ref[:, 1:2]
    normed = (tokens_ref[...].astype(F32) - stats_ref[:, 0:1]) * inv_sigma
    scaled = total * gain_ref[...].astype(F32)[None]
    out_ref[...] = (
        cot_ref[...].astype(F32)
        + inv_sigma
        * (
            scaled
            - jnp.mean(scaled, axis=1, keepdims=True)
            - normed * jnp.mean(scaled * normed, axis=1, keepdims=True)
        )
    ).astype(BF16)


def input_rows(places, terms, tokens, cot, stats, gain):
    width = tokens.shape[1]

    def mine(columns):
        return pl.BlockSpec((BLOCK, columns), lambda i, places: (places[0], 0))

    return kernel_call(
        input_kernel,
        "input",
        made(BLOCK, width),
        prefetch=1,
        grid=(1,),
        in_specs=[kept(t) for t in terms] + [mine(width), mine(width), mine(128), kept(gain)],
        out_specs=pl.BlockSpec((BLOCK, width), lambda *_: (0, 0)),
    )(places, *terms, tokens, cot, stats, gain)


def place_kernel(blocks, places_ref, *refs):
    pieces, out_ref, sems = refs[: len(blocks)], refs[-2], refs[-1]
    copies = []
    for i, ((offset, low, high), piece) in enumerate(zip(blocks, pieces)):
        first = pl.multiple_of(places_ref[OFFSETS.index(offset)] * BLOCK, BLOCK)
        copies.append(
            pltpu.make_async_copy(
                piece, out_ref.at[pl.ds(first + low, high - low), :], sems.at[i]
            )
        )
    for copy in copies:
        copy.start()
    for copy in copies:
        copy.wait()


def place_rows(places, blocks, pieces, whole=None):
    rest = {} if whole is None else {"input_output_aliases": {len(pieces) + 1: 0}}
    given = [] if whole is None else [whole]
    return kernel_call(
        functools.partial(place_kernel, blocks),
        "place",
        made(8 * BLOCK, pieces[0].shape[1]),
        in_specs=[SCALARS] + [NEAR] * len(pieces) + [AWAY] * len(given),
        out_specs=AWAY,
        scratch_shapes=[pltpu.SemaphoreType.DMA((len(pieces),))],
        **rest,
    )(places, *pieces, *given)


def up_kernel(near_ref, far_ref, first_ref, second_ref, sums_ref):
    total = near_ref[...].astype(F32) + far_ref[...].astype(F32)
    cut, end = first_ref.shape[1], first_ref.shape[1] + second_ref.shape[1]
    first_ref[...] = total[:, :cut]
    second_ref[...] = total[:, cut:end]
    sums_ref[...] = total[:, end:].T[: sums_ref.shape[0]]


def down_kernel(near_ref, far_ref, first_ref, second_ref):
    total = near_ref[...].astype(F32) + far_ref[...].astype(F32)
    cut = first_ref.shape[0]
    first_ref[...] = total[:, :cut].T
    second_ref[...] = total[:, cut:].T


def last_sum(kernel, name, shapes, near, far):
    return kernel_call(
        kernel,
        name,
        [made(*shape, F32) for shape in shapes],
        grid=(1,),
        in_specs=[pl.BlockSpec(far.shape, lambda _: (0, 0))] * 2,
        out_specs=[pl.BlockSpec(shape, lambda _: (0, 0)) for shape in shapes],
    )(near, far)


def shift(array, axis, size, by):
    return lax.ppermute(array, axis, [(i, (i + by) % size) for i in range(size)])


def y_up(array):
    return shift(array, "y", 4, 1)


def y_down(array):
    return shift(array, "y", 4, 3)


def across(array):
    return shift(array, "zl", 2, 1)


def sum_of_pairs(array):
    array = array + across(array)
    for step in (1, 2):
        array = array + lax.ppermute(array, "y", [(i, i ^ step) for i in range(4)])
    return array


def after(arrays, *earlier):
    return lax.optimization_barrier((arrays, earlier))[0]


class TensorSum:
    def __init__(self, blocks):
        self.blocks = blocks

    def send_far(self):
        b = self.blocks
        sent = [b[0], b[1], b[2], b[(0, 3)]]
        self.far = across(sent[0]), y_up(sent[1]), y_down(sent[2])
        self.near = [y_down(sent[3])]

    def send_middle(self, earlier):
        b = self.blocks
        far = *self.far[:2], after(self.far[2], earlier)
        sent = combine(
            "middle",
            *[
                [whole_term(b[offset]), whole_term(part, low)]
                for offset, part, (low, _) in zip(((0, 2), (1, 1), (1, 3)), far, PARTS)
            ],
        )
        self.middle = y_up(sent[0]), across(sent[1]), y_down(sent[2])
        return sent

    def send_near(self, earlier):
        b = self.blocks
        two_on, diagonal, other = self.middle
        other = after(other, earlier)
        sent = combine(
            "near",
            [whole_term(b[(0, 1)]), whole_term(two_on), whole_term(diagonal)],
            [whole_term(b[(1, 0)]), whole_term(other)],
        )
        self.near += [y_up(sent[0]), across(sent[1])]
        return sent

    def terms(self):
        return [self.blocks[(0, 0)], *self.near]


class TensorGather:
    def __init__(self, places, rows):
        self.places, self.rows = places, rows
        self.one = y_up(rows), y_down(rows), across(rows)

    def second(self, earlier):
        before, ahead, partner = self.one = after(self.one, earlier)
        self.two = y_down(ahead), across(ahead), y_up(partner)
        return self.one

    def third(self, earlier):
        two_on, diagonal, other = self.two = after(self.two, earlier)
        (a, b), (c, d), (e, f) = PARTS
        self.three = across(two_on[a:b]), y_down(diagonal[c:d]), y_up(other[e:f])
        blocks = [(0, 0), (0, 3), (0, 1), (1, 0), (0, 2), (1, 1), (1, 3)]
        self.whole = place_rows(
            self.places,
            [(offset, 0, BLOCK) for offset in blocks],
            [self.rows, *self.one, *self.two],
        )
        return self.whole

    def finish(self, earlier):
        parts = after(self.three, earlier)
        return place_rows(
            self.places, [(FAR, low, high) for low, high in PARTS], list(parts), self.whole
        )


class DataSum:
    def __init__(self, partial_sums, earlier):
        self.near = lax.psum_scatter(
            after(partial_sums, earlier), ("x", "core"), scatter_dimension=0, tiled=True
        )

    def send(self, earlier):
        self.near = after(self.near, earlier)
        self.far = shift(self.near[BLOCK:], "zh", 2, 1)

    def finish(self, kernel, name, shapes, earlier):
        return last_sum(kernel, name, shapes, self.near, after(self.far, earlier))


def dp_order():
    half = lax.axis_index("zh")
    return jnp.stack(
        [(half + part) % 2 * 8 + block for block in range(8) for part in range(2)]
    ).astype(jnp.int32)


def per_device(
    tokens,
    cotangent,
    seq_lengths,
    ln_gain,
    ln_bias,
    w_qkv,
    b_qkv,
    w_dense,
    b_dense,
    w_fc1,
    b_fc1,
    w_fc2,
    b_fc2,
):
    units = w_fc2.shape[0]
    plane, place = lax.axis_index("zl"), lax.axis_index("y")
    places = jnp.stack(
        [(plane + planes) % 2 * 4 + (place + steps) % 4 for planes, steps in OFFSETS]
    ).astype(jnp.int32)
    order = dp_order()
    frequency = 10000.0 ** (-jnp.arange(ROTARY // 2, dtype=F32) * 2.0 / ROTARY)
    frequency = jnp.tile(frequency, 8)[None]
    hidden, grad, activated, slope, context, qkv_grad, stats, branch_part = forward(
        seq_lengths,
        frequency,
        tokens,
        cotangent,
        ln_gain,
        ln_bias,
        b_qkv,
        b_fc1,
        w_qkv,
        w_fc1,
        w_dense,
        w_fc2,
    )
    branch_sum = lax.psum(branch_part, TENSOR)
    up_grad, small, blocks = backward(
        after(places, branch_part), grad, slope, qkv_grad, tokens, stats, w_fc2, w_fc1, w_qkv
    )
    gain_sum, shift_sum, grad_sum, head_sum, unit_sum = small
    hidden_sum = TensorSum(blocks)
    hidden_sum.send_far()
    done = hidden_sum.send_middle(())
    sums = [
        gain_sum.reshape(16, -1),
        shift_sum.reshape(16, -1),
        grad_sum.reshape(16, -1),
        jnp.pad(head_sum.reshape(16, -1), ((0, 0), (0, 80))),
        jnp.pad(unit_sum.reshape(16, -1), ((0, 0), (0, 64))),
    ]
    up_part = weight_blocks(after(order, done), hidden, up_grad, qkv_grad, *sums)
    done = hidden_sum.send_near(up_part)
    up = DataSum(up_part, done)
    down_part = weight_blocks(after(order, done), grad, activated, context)
    rows = input_rows(
        after(places, down_part), hidden_sum.terms(), tokens, cotangent, stats, ln_gain
    )
    down = DataSum(down_part, rows)
    input_grad = TensorGather(places, rows)
    done = input_grad.second((rows, branch_sum))
    up.send(done)
    output = finish_output(after(seq_lengths, up.near), tokens, branch_sum, b_dense, b_fc2)
    grad_fc1, grad_qkv, small = up.finish(
        up_kernel,
        "up",
        ((BLOCK, units), (BLOCK, w_qkv.shape[1]), (8, BLOCK)),
        output,
    )
    input_grad.third(small)
    norm_sum = sum_of_pairs(after(small[:2], input_grad.whole))
    down.send(input_grad.whole)
    grad_fc2, grad_dense = down.finish(
        down_kernel, "down", ((units, BLOCK), (w_dense.shape[0], BLOCK)), input_grad.whole
    )
    input_grad = input_grad.finish(())
    out_bias = small[2]
    return (
        output,
        input_grad,
        norm_sum[0],
        norm_sum[1],
        grad_qkv,
        small[3, :48],
        grad_dense,
        out_bias,
        grad_fc1,
        small[4, :64],
        grad_fc2,
        out_bias,
    )


def solution(mesh):
    parts = Mesh(mesh.devices.reshape(2, 4, 2, 2, 4), DP + TENSOR)
    rows = P(DP, None)
    placed = (
        rows,
        rows,
        rows,
        P(),
        P(),
        P(None, TENSOR),
        P(TENSOR),
        P(TENSOR, None),
        P(),
        P(None, TENSOR),
        P(TENSOR),
        P(TENSOR, None),
        P(),
    )
    return jax.shard_map(
        per_device,
        mesh=parts,
        in_specs=placed,
        out_specs=(
            rows,
            rows,
            P(DP),
            P(DP),
            P(DP, TENSOR),
            P(TENSOR + DP),
            P(TENSOR, DP),
            P(DP),
            P(DP, TENSOR),
            P(TENSOR + DP),
            P(TENSOR, DP),
            P(DP),
        ),
        check_vma=False,
    )
```

```python
import functools

import jax
import jax.numpy as jnp
from jax import lax
from jax.experimental import pallas as pl
from jax.experimental.pallas import tpu as pltpu
from jax.sharding import Mesh
from jax.sharding import PartitionSpec as P

HEAD_DIM = 64
ROTARY = 32
DP = ("zh", "x", "core")
TENSOR = ("zl", "y")
BF16 = jnp.bfloat16
F32 = jnp.float32
ROWS = 256
QUERIES = 512
BLOCK = 128
AT_ONCE = 4
VMEM_BYTES = 56 * 2**20
GELU = 0.7978845608


def dot(left, right, left_dim, right_dim):
    return lax.dot_general(
        left, right, (((left_dim,), (right_dim,)), ((), ())), preferred_element_type=F32
    )


def kernel_call(kernel, name, out_shape, prefetch=0, vmem=VMEM_BYTES, flops=1, **spec):
    if prefetch:
        spec = {
            "grid_spec": pltpu.PrefetchScalarGridSpec(
                num_scalar_prefetch=prefetch,
                grid=spec.pop("grid"),
                in_specs=spec.pop("in_specs"),
                out_specs=spec.pop("out_specs"),
                scratch_shapes=spec.pop("scratch_shapes", ()),
            ),
            **spec,
        }
    return pl.pallas_call(
        kernel,
        out_shape=out_shape,
        compiler_params=pltpu.CompilerParams(vmem_limit_bytes=vmem),
        cost_estimate=pl.CostEstimate(flops=flops, bytes_accessed=1, transcendentals=0),
        name=name,
        **spec,
    )


def made(rows, columns, kind=BF16):
    return jax.ShapeDtypeStruct((rows, columns), kind)


def kept(array):
    return pl.BlockSpec(array.shape, lambda *_: (0,) * array.ndim)


AWAY = pl.BlockSpec(memory_space=pltpu.HBM)
NEAR = pl.BlockSpec(memory_space=pltpu.VMEM)
SCALARS = pl.BlockSpec(memory_space=pltpu.SMEM)


def ends_of(lengths_ref):
    ends = []
    total = jnp.int32(0)
    for place in range(lengths_ref.shape[1]):
        total = total + lengths_ref[0, place]
        ends.append(total)
    return ends


def starts_at(ends, places):
    start = jnp.zeros_like(places)
    for end in ends:
        start = jnp.maximum(start, jnp.where(places >= end, end, 0))
    return start


def turned_halves(columns):
    lane = lax.broadcasted_iota(jnp.int32, columns.shape, 1)
    return jnp.where(
        lane % ROTARY < ROTARY // 2, pltpu.roll(columns, 112, 1), pltpu.roll(columns, 16, 1)
    )


class Copies:
    def __init__(self, sems):
        self.sems, self.made = sems, {}

    def start(self, name, source, target):
        copy = pltpu.make_async_copy(source, target, self.sems.at[len(self.made)])
        self.made[name] = copy
        copy.start()

    def wait(self, *names):
        for name in names:
            self.made[name].wait()


def forward_kernel(
    lengths_ref,
    freq_ref,
    gain_ref,
    bias_ref,
    b_qkv_ref,
    b_fc1_ref,
    tokens_hbm,
    cot_hbm,
    w_qkv_hbm,
    w_fc1_hbm,
    w_dense_hbm,
    w_fc2_hbm,
    hidden_hbm,
    grad_hbm,
    act_hbm,
    slope_hbm,
    ctx_hbm,
    qkv_grad_hbm,
    stats_hbm,
    branch_hbm,
    tokens,
    grad,
    hidden,
    w_qkv,
    w_fc1,
    w_dense,
    w_fc2,
    qkv,
    act,
    slope,
    ctx_grad,
    ctx,
    qkv_grad,
    cosines,
    sines,
    stats,
    turn_sum,
    value_sum,
    sems,
):
    slot_len, width = tokens.shape
    blocks = slot_len // ROWS
    copies = Copies(sems)
    ends = ends_of(lengths_ref)

    def rows_of(block, blocks_each=1):
        return slice(block * ROWS, (block + blocks_each) * ROWS)

    def bring_rows(block):
        at = rows_of(block)
        copies.start(("tokens", block), tokens_hbm.at[at, :], tokens.at[at, :])
        copies.start(("cot", block), cot_hbm.at[at, :], grad.at[at, :])

    def bring(name, source, target):
        copies.start(name, source, target)

    def send_rows(name, block, source, target):
        at = rows_of(block)
        copies.start((name, block), source.at[at, :], target.at[at, :])

    def normalise(block, part, parts=4):
        height = ROWS // parts
        first = block * ROWS + part * height
        at = slice(first, first + height)
        places = first + lax.broadcasted_iota(jnp.int32, (height, 128), 0)
        lane = lax.broadcasted_iota(jnp.int32, (height, 128), 1)
        position = (places - starts_at(ends, places)).astype(F32)
        angle = position * freq_ref[...]
        cosines[at, :] = jnp.where(lane % HEAD_DIM < ROTARY, jnp.cos(angle), 1.0)
        sine = jnp.sin(angle)
        sines[at, :] = jnp.where(
            lane % HEAD_DIM < ROTARY // 2, -sine, jnp.where(lane % HEAD_DIM < ROTARY, sine, 0.0)
        )
        valid = (places < ends[-1])[:, :1]
        inputs = tokens[at, :].astype(F32)
        mean = jnp.mean(inputs, axis=1, keepdims=True)
        center = inputs - mean
        inv_sigma = lax.rsqrt(jnp.mean(center * center, axis=1, keepdims=True) + 1e-05)
        stats[at, :] = jnp.where(lane == 0, mean, inv_sigma)
        hidden[at, :] = (
            center * inv_sigma * gain_ref[...].astype(F32)[None]
            + bias_ref[...].astype(F32)[None]
        ).astype(BF16)
        grad[at, :] = jnp.where(valid, grad[at, :], jnp.zeros((height, width), BF16))

    def turn(at, projected):
        lane = lax.broadcasted_iota(jnp.int32, (ROWS, 128), 1)
        cosine, sine = cosines[at, :], sines[at, :]
        for block in range(qkv.shape[1] // 128):
            columns = slice(block * 128, block * 128 + 128)
            plain = projected[:, columns]
            turned = plain * cosine + turned_halves(plain) * sine
            if block % 3 == 1:
                turned = jnp.where(lane < HEAD_DIM, plain, turned)
            if block % 3 == 2:
                turned = jnp.where(lane < HEAD_DIM, turned, plain)
            qkv[at, columns] = turned.astype(BF16)

    def activate(at, up, columns):
        square = up * up
        share = 0.5 * jnp.tanh(up * (GELU + (GELU * 0.044715) * square)) + 0.5
        active = up * share
        act[at, columns] = active.astype(BF16)
        slope[at, columns] = (
            share + active * (1.0 - share) * (2 * GELU + (6 * GELU * 0.044715) * square)
        ).astype(BF16)

    def multiply(block, between):
        at = rows_of(block)
        if block == 0:
            copies.wait("w_qkv")
        between(0)
        projected = dot(hidden[at, :], w_qkv[...], 1, 0) + b_qkv_ref[...].astype(F32)[None]
        between(1)
        turn(at, projected)
        if block == 0:
            copies.wait("w_fc1", "w_dense")
        half = w_fc1.shape[1] // 2
        for part in range(2):
            columns = slice(part * half, part * half + half)
            up = dot(hidden[at, :], w_fc1[:, columns], 1, 0)
            up = up + b_fc1_ref[columns].astype(F32)[None]
            between(2 + part)
            activate(at, up, columns)
        ctx_grad[at, :] = dot(grad[at, :], w_dense[...], 1, 1).astype(BF16)

    def attend(head):
        at = 3 * HEAD_DIM * head
        mine = slice(HEAD_DIM * head, HEAD_DIM * head + HEAD_DIM)
        for block in reversed(range(slot_len // QUERIES)):
            rows = slice(block * QUERIES, block * QUERIES + QUERIES)
            reach = (block + 1) * QUERIES
            query = qkv[rows, at : at + 64] * BF16(HEAD_DIM**-0.5)
            key = qkv[0:reach, at + 64 : at + 128]
            value = qkv[0:reach, at + 128 : at + 192]
            upstream = ctx_grad[rows, mine]
            scores = dot(key, query, 1, 1)
            place = block * QUERIES + lax.broadcasted_iota(jnp.int32, (1, QUERIES), 1)
            start = starts_at(ends, place)
            key_place = lax.broadcasted_iota(jnp.int32, (reach, QUERIES), 0)
            scores = jnp.where((key_place >= start) & (key_place <= place), scores, -1e30)
            raised = jnp.exp(scores - jnp.max(scores, axis=0, keepdims=True))
            prob = raised * (1.0 / jnp.sum(raised, axis=0, keepdims=True))
            prob_low = prob.astype(BF16)
            context = dot(value, prob_low, 0, 0)
            prob_grad = dot(value, upstream, 1, 1)
            row_dot = jnp.sum(prob_grad * prob, axis=0, keepdims=True)
            score_grad = (prob * (prob_grad - row_dot)).astype(BF16)
            query_grad = dot(key, score_grad, 0, 0)
            value_part = dot(prob_low, upstream, 1, 0)
            key_part = dot(score_grad, query, 1, 0)
            if reach == slot_len:
                value_sum[...] = value_part
                turn_sum[:, 64:128] = key_part
            else:
                value_sum[0:reach] += value_part
                turn_sum[0:reach, 64:128] += key_part
            turn_sum[rows, 0:64] = query_grad.T * HEAD_DIM**-0.5
            ctx[rows, mine] = context.T.astype(BF16)
        both = turn_sum[...]
        both = both * cosines[...] - turned_halves(both) * sines[...]
        qkv_grad[:, at : at + 128] = both.astype(BF16)
        qkv_grad[:, at + 128 : at + 192] = value_sum[...].astype(BF16)

    bring_rows(0)
    bring("w_qkv", w_qkv_hbm, w_qkv)
    bring_rows(1)
    bring("w_fc1", w_fc1_hbm, w_fc1)
    bring("w_dense", w_dense_hbm, w_dense)
    copies.wait(("tokens", 0), ("cot", 0))
    for block in range(2, blocks):
        bring_rows(block)
    bring("w_fc2", w_fc2_hbm, w_fc2)
    for part in range(4):
        normalise(0, part)
    for block in range(blocks):
        send_rows("hidden", block, hidden, hidden_hbm)
        send_rows("grad", block, grad, grad_hbm)
        if block + 1 < blocks:
            copies.wait(("tokens", block + 1), ("cot", block + 1))
            multiply(block, functools.partial(normalise, block + 1))
        else:
            multiply(block, lambda part: None)
        send_rows("act", block, act, act_hbm)
        send_rows("slope", block, slope, slope_hbm)
    copies.start("stats", stats, stats_hbm)
    for head in range(qkv.shape[1] // (3 * HEAD_DIM)):
        attend(head)
    copies.start("ctx", ctx, ctx_hbm)
    copies.start("qkv_grad", qkv_grad, qkv_grad_hbm)
    copies.wait("w_fc2")
    size = 512
    for part in range(width // size):
        columns = slice(part * size, part * size + size)
        tokens[:, columns] = (
            dot(ctx[...], w_dense[:, columns], 1, 0) + dot(act[...], w_fc2[:, columns], 1, 0)
        ).astype(BF16)
        copies.start(("branch", part), tokens.at[:, columns], branch_hbm.at[:, columns])
    brought = {"w_qkv", "w_fc1", "w_dense", "w_fc2"}
    copies.wait(
        *[
            name
            for name in copies.made
            if name not in brought and name[0] not in ("tokens", "cot")
        ]
    )


def forward(lengths, freq, tokens, cot, gain, bias, b_qkv, b_fc1, w_qkv, w_fc1, w_dense, w_fc2):
    slot_len, width = tokens.shape
    units, heads, ctx_width = w_fc2.shape[0], w_qkv.shape[1], w_dense.shape[0]
    row_kinds = (width, width, units, units, ctx_width, heads)

    def room(rows, columns, kind=BF16):
        return pltpu.VMEM((rows, columns), kind)

    return kernel_call(
        forward_kernel,
        "forward",
        [made(slot_len, columns) for columns in row_kinds]
        + [made(slot_len, 128, F32), made(slot_len, width)],
        grid=(1,),
        in_specs=[SCALARS] + [kept(a) for a in (freq, gain, bias, b_qkv, b_fc1)] + [AWAY] * 6,
        out_specs=[AWAY] * 8,
        scratch_shapes=[room(slot_len, width)] * 3
        + [pltpu.VMEM(w.shape, BF16) for w in (w_qkv, w_fc1, w_dense, w_fc2)]
        + [
            room(slot_len, heads),
            room(slot_len, units),
            room(slot_len, units),
            room(slot_len, ctx_width),
            room(slot_len, ctx_width),
            room(slot_len, heads),
        ]
        + [room(slot_len, 128, F32)] * 4
        + [room(slot_len, 64, F32), pltpu.SemaphoreType.DMA((48,))],
    )(lengths, freq, gain, bias, b_qkv, b_fc1, tokens, cot, w_qkv, w_fc1, w_dense, w_fc2)


OFFSETS = tuple((planes, places) for planes in range(2) for places in range(4))
FAR = (1, 2)
CUTS = (0, 48, 96, 128)
PARTS = tuple(zip(CUTS, CUTS[1:]))
BLOCK_NAMES = tuple(o for o in OFFSETS if o != FAR) + (0, 1, 2)


def block_shapes(width):
    return [made(BLOCK, width)] * 7 + [made(high - low, width) for low, high in PARTS]


def backward_kernel(
    places_ref,
    grad_hbm,
    slope_hbm,
    qkv_grad_hbm,
    tokens_hbm,
    stats_hbm,
    w_fc2_hbm,
    w_fc1_hbm,
    w_qkv_hbm,
    norm_sum_ref,
    grad_sum_ref,
    head_sum_ref,
    unit_sum_ref,
    up_grad_hbm,
    *rest,
):
    blocks, scratch = rest[: len(BLOCK_NAMES)], rest[len(BLOCK_NAMES) :]
    grad, slope, qkv_grad, tokens, stats, w_fc2, w_fc1, w_qkv, *scratch = scratch
    up_grad, hidden, gain_sum, shift_sum, grad_sum, head_sum, unit_sum, sems = scratch
    copies = Copies(sems)
    slot_len, width = grad.shape
    units, size = w_fc2.shape[0], 512

    def part_of(part):
        return slice(part * size, part * size + size)

    def bring_rows(name, part, source, target):
        at = part_of(part)
        copies.start((name, part), source.at[at, :], target.at[at, :])

    def add_to(ref, columns, array, fresh):
        total = jnp.sum(array, axis=0, keepdims=True)
        ref[:, columns] = total if fresh else ref[:, columns] + total

    def to_units(rows, part):
        at, columns = part_of(rows), part_of(part)
        up = dot(grad[at, :], w_fc2[columns, :], 1, 1) * slope[at, columns].astype(F32)
        up = up.astype(BF16)
        up_grad[at, columns] = up
        add_to(unit_sum, columns, up.astype(F32), rows == 0)

    def to_hidden(rows, part):
        at, columns = part_of(rows), part_of(part)
        result = dot(up_grad[at, :], w_fc1[columns, :], 1, 1) + dot(
            qkv_grad[at, :], w_qkv[columns, :], 1, 1
        )
        hidden[at, columns] = result.astype(BF16)
        normed = (tokens[at, columns].astype(F32) - stats[at, 0:1]) * stats[at, 1:2]
        add_to(gain_sum, columns, result * normed, rows == 0)
        add_to(shift_sum, columns, result, rows == 0)

    bring_rows("w_fc2", 0, w_fc2_hbm, w_fc2)
    for rows in range(2):
        bring_rows("grad", rows, grad_hbm, grad)
        bring_rows("slope", rows, slope_hbm, slope)
    bring_rows("w_fc2", 1, w_fc2_hbm, w_fc2)
    copies.wait(("w_fc2", 0), ("grad", 0), ("slope", 0))
    copies.start("w_fc1", w_fc1_hbm, w_fc1)
    copies.start("w_qkv", w_qkv_hbm, w_qkv)
    copies.start("qkv_grad", qkv_grad_hbm, qkv_grad)
    copies.start("tokens", tokens_hbm, tokens)
    copies.start("stats", stats_hbm, stats)
    to_units(0, 0)
    copies.wait(("w_fc2", 1))
    to_units(0, 1)
    copies.wait(("grad", 1), ("slope", 1))
    to_units(1, 0)
    to_units(1, 1)
    copies.start("up_grad", up_grad, up_grad_hbm)
    everything = slice(0, width)
    for rows in range(2):
        add_to(grad_sum, everything, grad[part_of(rows), :].astype(F32), rows == 0)
    copies.wait("w_fc1", "w_qkv", "qkv_grad", "tokens", "stats")
    add_to(head_sum, slice(0, qkv_grad.shape[1]), qkv_grad[...].astype(F32), True)
    for part in range(width // size):
        for rows in range(slot_len // size):
            to_hidden(rows, part)
        columns = part_of(part)
        for name, ref in zip(BLOCK_NAMES, blocks):
            low, high = PARTS[name] if isinstance(name, int) else (0, BLOCK)
            place = places_ref[OFFSETS.index(FAR if isinstance(name, int) else name)]
            first = pl.multiple_of(place * BLOCK, BLOCK) + low
            copies.start(
                ("block", name, part),
                hidden.at[pl.ds(first, high - low), columns],
                ref.at[:, columns],
            )
    for ref, first, total in (
        (norm_sum_ref, 0, gain_sum),
        (norm_sum_ref, 16, shift_sum),
        (grad_sum_ref, 0, grad_sum),
        (head_sum_ref, 0, head_sum),
        (unit_sum_ref, 0, unit_sum),
    ):
        share = total.shape[1] // 16
        if share < BLOCK:
            ref[...] = jnp.zeros_like(ref)
        for row in range(16):
            ref[first + row : first + row + 1, 0:share] = total[:, row * share : row * share + share]
    copies.wait(
        "up_grad",
        *[("block", name, part) for name in BLOCK_NAMES for part in range(width // size)],
    )


def backward(places, grad, slope, qkv_grad, tokens, stats, w_fc2, w_fc1, w_qkv):
    slot_len, width = tokens.shape
    units, heads = w_fc2.shape[0], w_qkv.shape[1]
    sizes = (width, width, width, heads, units)
    sums = [made(rows, BLOCK, F32) for rows in (32, 16, 16, 16)]
    arrays = (grad, slope, qkv_grad, tokens, stats, w_fc2, w_fc1, w_qkv)
    norm_sum, grad_sum, head_sum, unit_sum, up_grad, *blocks = kernel_call(
        backward_kernel,
        "backward",
        sums + [made(slot_len, units)] + block_shapes(width),
        grid=(1,),
        in_specs=[SCALARS] + [AWAY] * len(arrays),
        out_specs=[kept(array) for array in sums] + [AWAY] * (1 + len(BLOCK_NAMES)),
        scratch_shapes=[pltpu.VMEM(array.shape, array.dtype) for array in arrays]
        + [pltpu.VMEM((slot_len, units), BF16), pltpu.VMEM((slot_len, width), BF16)]
        + [pltpu.VMEM((1, size), F32) for size in sizes]
        + [pltpu.SemaphoreType.DMA((64,))],
    )(places, *arrays)
    sums = (norm_sum, grad_sum, head_sum, unit_sum)
    return up_grad, sums, dict(zip(BLOCK_NAMES, blocks))


def weight_kernel(order_ref, *refs):
    lefts, (first_ref, second_ref, *sums, out_ref) = refs[:AT_ONCE], refs[AT_ONCE:]
    cut, end = first_ref.shape[1], first_ref.shape[1] + second_ref.shape[1]
    left = jnp.concatenate([ref[...] for ref in lefts], axis=1)
    out_ref[:, 0:cut] = dot(left, first_ref[...], 0, 0).astype(BF16)
    out_ref[:, cut:end] = dot(left, second_ref[...], 0, 0).astype(BF16)
    if sums:
        for half in range(AT_ONCE):
            block = order_ref[AT_ONCE * pl.program_id(0) + half]
            lines = [
                ref[pl.ds(first + block, 1), :]
                for ref in sums
                for first in range(0, ref.shape[0], 16)
            ]
            lines.append(jnp.zeros((BLOCK - len(lines), BLOCK), F32))
            columns = jnp.concatenate(lines, axis=0).T
            out_ref[half * BLOCK : half * BLOCK + BLOCK, end:] = columns.astype(BF16)


def weight_blocks(order, left, first, second, *sums):
    slot_len = left.shape[0]
    width = first.shape[1] + second.shape[1] + (BLOCK if sums else 0)
    return kernel_call(
        weight_kernel,
        "weights",
        made(left.shape[1], width),
        prefetch=1,
        grid=(left.shape[1] // (AT_ONCE * BLOCK),),
        in_specs=[
            *[
                pl.BlockSpec(
                    (slot_len, BLOCK),
                    functools.partial(lambda at, i, order: (0, order[AT_ONCE * i + at]), at),
                )
                for at in range(AT_ONCE)
            ],
            kept(first),
            kept(second),
            *[kept(array) for array in sums],
        ],
        out_specs=pl.BlockSpec((AT_ONCE * BLOCK, width), lambda i, order: (i, 0)),
    )(order, *[left] * AT_ONCE, first, second, *sums)


def combine(name, *sums):
    arrays = [term[0] for terms in sums for term in terms]
    specs = [
        pl.BlockSpec((term[1], term[0].shape[1]), functools.partial(lambda at, _: (at, 0), term[2]))
        for terms in sums
        for term in terms
    ]
    heights = [max(term[4] for term in terms) for terms in sums]

    def kernel(*refs):
        ins, outs = list(refs[: len(arrays)]), refs[len(arrays) :]
        for terms, height, out in zip(sums, heights, outs):
            mine = [(ins.pop(0), term[3], term[4]) for term in terms]
            cuts = sorted({cut for _, low, high in mine for cut in (low, high)})
            for low, high in zip(cuts, cuts[1:]):
                parts = [
                    ref[low - first : high - first, :].astype(F32)
                    for ref, first, last in mine
                    if first <= low and high <= last
                ]
                out[low:high, :] = functools.reduce(lambda a, b: a + b, parts).astype(BF16)

    shapes = [made(height, terms[0][0].shape[1]) for height, terms in zip(heights, sums)]
    return kernel_call(
        kernel,
        name,
        shapes,
        grid=(1,),
        in_specs=specs,
        out_specs=[pl.BlockSpec(shape.shape, lambda _: (0, 0)) for shape in shapes],
    )(*arrays)


def whole_term(array, low=0):
    return (array, array.shape[0], 0, low, low + array.shape[0])


def output_kernel(lengths_ref, tokens_ref, branch_ref, b_dense_ref, b_fc2_ref, out_ref):
    bias = b_dense_ref[...].astype(F32) + b_fc2_ref[...].astype(F32)
    rows = tokens_ref.shape[0]
    place = pl.program_id(0) * rows + lax.broadcasted_iota(jnp.int32, (rows, 1), 0)
    total = jnp.where(
        place < ends_of(lengths_ref)[-1], branch_ref[...].astype(F32) + bias[None], 0.0
    )
    out_ref[...] = (tokens_ref[...].astype(F32) + total).astype(BF16)


def finish_output(lengths, tokens, branch_sum, b_dense, b_fc2):
    slot_len, width = tokens.shape
    row = pl.BlockSpec((ROWS, width), lambda i: (i, 0))
    return kernel_call(
        output_kernel,
        "output",
        made(slot_len, width),
        grid=(slot_len // ROWS,),
        in_specs=[SCALARS, row, row, kept(b_dense), kept(b_fc2)],
        out_specs=row,
    )(lengths, tokens, branch_sum, b_dense, b_fc2)


def input_kernel(places_ref, *refs):
    *terms, tokens_ref, cot_ref, stats_ref, gain_ref, out_ref = refs
    total = functools.reduce(lambda a, b: a + b, [t[...].astype(F32) for t in terms])
    inv_sigma = stats_ref[:, 1:2]
    normed = (tokens_ref[...].astype(F32) - stats_ref[:, 0:1]) * inv_sigma
    scaled = total * gain_ref[...].astype(F32)[None]
    out_ref[...] = (
        cot_ref[...].astype(F32)
        + inv_sigma
        * (
            scaled
            - jnp.mean(scaled, axis=1, keepdims=True)
            - normed * jnp.mean(scaled * normed, axis=1, keepdims=True)
        )
    ).astype(BF16)


def input_rows(places, terms, tokens, cot, stats, gain):
    width = tokens.shape[1]

    def mine(columns):
        return pl.BlockSpec((BLOCK, columns), lambda i, places: (places[0], 0))

    return kernel_call(
        input_kernel,
        "input",
        made(BLOCK, width),
        prefetch=1,
        grid=(1,),
        in_specs=[kept(t) for t in terms] + [mine(width), mine(width), mine(128), kept(gain)],
        out_specs=pl.BlockSpec((BLOCK, width), lambda *_: (0, 0)),
    )(places, *terms, tokens, cot, stats, gain)


def place_kernel(blocks, places_ref, *refs):
    pieces, out_ref, sems = refs[: len(blocks)], refs[-2], refs[-1]
    copies = []
    for i, ((offset, low, high), piece) in enumerate(zip(blocks, pieces)):
        first = pl.multiple_of(places_ref[OFFSETS.index(offset)] * BLOCK, BLOCK)
        copies.append(
            pltpu.make_async_copy(
                piece, out_ref.at[pl.ds(first + low, high - low), :], sems.at[i]
            )
        )
    for copy in copies:
        copy.start()
    for copy in copies:
        copy.wait()


def place_rows(places, blocks, pieces, whole=None):
    rest = {} if whole is None else {"input_output_aliases": {len(pieces) + 1: 0}}
    given = [] if whole is None else [whole]
    return kernel_call(
        functools.partial(place_kernel, blocks),
        "place",
        made(8 * BLOCK, pieces[0].shape[1]),
        in_specs=[SCALARS] + [NEAR] * len(pieces) + [AWAY] * len(given),
        out_specs=AWAY,
        scratch_shapes=[pltpu.SemaphoreType.DMA((len(pieces),))],
        **rest,
    )(places, *pieces, *given)


def up_kernel(near_ref, far_ref, first_ref, second_ref):
    total = near_ref[...].astype(F32) + far_ref[...].astype(F32)
    cut = first_ref.shape[1]
    first_ref[...] = total[:, :cut]
    second_ref[...] = total[:, cut:]


def down_kernel(near_ref, far_ref, first_ref, second_ref, sums_ref):
    total = near_ref[...].astype(F32) + far_ref[...].astype(F32)
    cut, end = first_ref.shape[0], first_ref.shape[0] + second_ref.shape[0]
    first_ref[...] = total[:, :cut].T
    second_ref[...] = total[:, cut:end].T
    sums_ref[...] = total[:, end:].T[: sums_ref.shape[0]]


def last_sum(kernel, name, shapes, near, far):
    return kernel_call(
        kernel,
        name,
        [made(*shape, F32) for shape in shapes],
        grid=(1,),
        in_specs=[pl.BlockSpec(far.shape, lambda _: (0, 0))] * 2,
        out_specs=[pl.BlockSpec(shape, lambda _: (0, 0)) for shape in shapes],
    )(near, far)


def shift(array, axis, size, by):
    return lax.ppermute(array, axis, [(i, (i + by) % size) for i in range(size)])


def y_up(array):
    return shift(array, "y", 4, 1)


def y_down(array):
    return shift(array, "y", 4, 3)


def across(array):
    return shift(array, "zl", 2, 1)


def after(arrays, *earlier):
    return lax.optimization_barrier((arrays, earlier))[0]


class TensorSum:
    def __init__(self, blocks):
        self.blocks = blocks

    def send_far(self):
        b = self.blocks
        self.far = across(b[0]), y_up(b[1]), y_down(b[2])

    def send_middle(self, earlier):
        b = self.blocks
        far = *self.far[:2], after(self.far[2], earlier)
        sent = combine(
            "middle",
            *[
                [whole_term(b[offset]), whole_term(part, low)]
                for offset, part, (low, _) in zip(((0, 2), (1, 1), (1, 3)), far, PARTS)
            ],
        )
        self.middle = y_up(sent[0]), across(sent[1]), y_down(sent[2])
        return sent

    def send_near(self, earlier):
        b = self.blocks
        two_on, diagonal, other = self.middle
        other = after(other, earlier)
        sent = combine(
            "near",
            [whole_term(b[(0, 1)]), whole_term(two_on), whole_term(diagonal)],
            [whole_term(b[(1, 0)]), whole_term(other)],
        )
        self.near = [y_up(sent[0]), across(sent[1]), y_down(after(b[(0, 3)], sent))]
        return sent

    def terms(self):
        return [self.blocks[(0, 0)], *self.near]


class TensorGather:
    def __init__(self, places, rows):
        self.places, self.rows = places, rows
        self.one = y_up(rows), y_down(rows), across(rows)

    def second(self, earlier):
        before, ahead, partner = self.one = after(self.one, earlier)
        self.two = y_down(ahead), across(ahead), y_up(partner)
        return self.one

    def third(self, earlier):
        two_on, diagonal, other = self.two = after(self.two, earlier)
        (a, b), (c, d), (e, f) = PARTS
        self.three = across(two_on[a:b]), y_down(diagonal[c:d]), y_up(other[e:f])
        blocks = [(0, 0), (0, 3), (0, 1), (1, 0), (0, 2), (1, 1), (1, 3)]
        self.whole = place_rows(
            self.places,
            [(offset, 0, BLOCK) for offset in blocks],
            [self.rows, *self.one, *self.two],
        )
        return self.whole

    def finish(self, earlier):
        parts = after(self.three, earlier)
        return place_rows(
            self.places, [(FAR, low, high) for low, high in PARTS], list(parts), self.whole
        )


class DataSum:
    def __init__(self, partial_sums, earlier):
        self.near = lax.psum_scatter(
            after(partial_sums, earlier), ("x", "core"), scatter_dimension=0, tiled=True
        )

    def send(self, earlier):
        self.near = after(self.near, earlier)
        self.far = shift(self.near[BLOCK:], "zh", 2, 1)

    def finish(self, kernel, name, shapes, earlier):
        return last_sum(kernel, name, shapes, self.near, after(self.far, earlier))


def dp_order():
    half = lax.axis_index("zh")
    return jnp.stack(
        [(half + part) % 2 * 8 + block for block in range(8) for part in range(2)]
    ).astype(jnp.int32)


def per_device(
    tokens,
    cotangent,
    seq_lengths,
    ln_gain,
    ln_bias,
    w_qkv,
    b_qkv,
    w_dense,
    b_dense,
    w_fc1,
    b_fc1,
    w_fc2,
    b_fc2,
):
    units = w_fc2.shape[0]
    plane, place = lax.axis_index("zl"), lax.axis_index("y")
    places = jnp.stack(
        [(plane + planes) % 2 * 4 + (place + steps) % 4 for planes, steps in OFFSETS]
    ).astype(jnp.int32)
    order = dp_order()
    frequency = 10000.0 ** (-jnp.arange(ROTARY // 2, dtype=F32) * 2.0 / ROTARY)
    frequency = jnp.tile(frequency, 8)[None]
    hidden, grad, activated, slope, context, qkv_grad, stats, branch_part = forward(
        seq_lengths,
        frequency,
        tokens,
        cotangent,
        ln_gain,
        ln_bias,
        b_qkv,
        b_fc1,
        w_qkv,
        w_fc1,
        w_dense,
        w_fc2,
    )
    branch_sum = lax.psum(branch_part, TENSOR)
    up_grad, sums, blocks = backward(
        after(places, branch_part), grad, slope, qkv_grad, tokens, stats, w_fc2, w_fc1, w_qkv
    )
    hidden_sum = TensorSum(blocks)
    hidden_sum.send_far()
    norm_sum, *sums = sums
    norm_across = across(norm_sum)
    up_part = weight_blocks(after(order, up_grad), hidden, up_grad, qkv_grad)
    done = hidden_sum.send_middle(up_part)
    up = DataSum(up_part, done)
    norm_sum = norm_sum + after(norm_across, done)
    norm_sum = norm_sum + y_up(norm_sum) + y_down(norm_sum) + shift(norm_sum, "y", 4, 2)
    down_part = weight_blocks(after(order, done), grad, activated, context, norm_sum, *sums)
    done = hidden_sum.send_near(down_part)
    down = DataSum(down_part, done)
    rows = input_rows(
        after(places, down_part), hidden_sum.terms(), tokens, cotangent, stats, ln_gain
    )
    input_grad = TensorGather(places, rows)
    done = input_grad.second((rows, branch_sum))
    up.send(done)
    down.send(up.near)
    output = finish_output(after(seq_lengths, down.near), tokens, branch_sum, b_dense, b_fc2)
    done = input_grad.third(output)
    input_grad.three = after(input_grad.three, done)
    grad_fc1, grad_qkv = up.finish(
        up_kernel, "up", ((BLOCK, units), (BLOCK, w_qkv.shape[1])), input_grad.three[0]
    )
    grad_fc2, grad_dense, small = down.finish(
        down_kernel,
        "down",
        ((units, BLOCK), (w_dense.shape[0], BLOCK), (8, BLOCK)),
        grad_qkv,
    )
    input_grad = input_grad.finish(small)
    out_bias = small[2]
    return (
        output,
        input_grad,
        small[0],
        small[1],
        grad_qkv,
        small[3, :48],
        grad_dense,
        out_bias,
        grad_fc1,
        small[4, :64],
        grad_fc2,
        out_bias,
    )


def solution(mesh):
    parts = Mesh(mesh.devices.reshape(2, 4, 2, 2, 4), DP + TENSOR)
    rows = P(DP, None)
    placed = (
        rows,
        rows,
        rows,
        P(),
        P(),
        P(None, TENSOR),
        P(TENSOR),
        P(TENSOR, None),
        P(),
        P(None, TENSOR),
        P(TENSOR),
        P(TENSOR, None),
        P(),
    )
    return jax.shard_map(
        per_device,
        mesh=parts,
        in_specs=placed,
        out_specs=(
            rows,
            rows,
            P(DP),
            P(DP),
            P(DP, TENSOR),
            P(TENSOR + DP),
            P(TENSOR, DP),
            P(DP),
            P(DP, TENSOR),
            P(TENSOR + DP),
            P(TENSOR, DP),
            P(DP),
        ),
        check_vma=False,
    )
```

```python
import functools

import jax
import jax.numpy as jnp
from jax import lax
from jax.experimental import pallas as pl
from jax.experimental.pallas import tpu as pltpu
from jax.sharding import Mesh
from jax.sharding import PartitionSpec as P

HEAD_DIM = 64
ROTARY = 32
DP = ("zh", "x", "core")
TENSOR = ("zl", "y")
BF16 = jnp.bfloat16
F32 = jnp.float32
ROWS = 256
QUERIES = 512
BLOCK = 128
AT_ONCE = 4
VMEM_BYTES = 56 * 2**20
GELU = 0.7978845608


def dot(left, right, left_dim, right_dim):
    return lax.dot_general(
        left, right, (((left_dim,), (right_dim,)), ((), ())), preferred_element_type=F32
    )


def kernel_call(kernel, name, out_shape, prefetch=0, vmem=VMEM_BYTES, flops=1, **spec):
    if prefetch:
        spec = {
            "grid_spec": pltpu.PrefetchScalarGridSpec(
                num_scalar_prefetch=prefetch,
                grid=spec.pop("grid"),
                in_specs=spec.pop("in_specs"),
                out_specs=spec.pop("out_specs"),
                scratch_shapes=spec.pop("scratch_shapes", ()),
            ),
            **spec,
        }
    return pl.pallas_call(
        kernel,
        out_shape=out_shape,
        compiler_params=pltpu.CompilerParams(vmem_limit_bytes=vmem),
        cost_estimate=pl.CostEstimate(flops=flops, bytes_accessed=1, transcendentals=0),
        name=name,
        **spec,
    )


def made(rows, columns, kind=BF16):
    return jax.ShapeDtypeStruct((rows, columns), kind)


def kept(array):
    return pl.BlockSpec(array.shape, lambda *_: (0,) * array.ndim)


AWAY = pl.BlockSpec(memory_space=pltpu.HBM)
NEAR = pl.BlockSpec(memory_space=pltpu.VMEM)
SCALARS = pl.BlockSpec(memory_space=pltpu.SMEM)


def ends_of(lengths_ref):
    ends = [lengths_ref[0, 0]]
    for place in range(1, lengths_ref.shape[1]):
        ends.append(ends[-1] + lengths_ref[0, place])
    return ends


def starts_at(ends, places):
    start = jnp.zeros_like(places)
    for end in ends:
        start = jnp.maximum(start, jnp.where(places >= end, end, 0))
    return start


def turned_halves(columns):
    lane = lax.broadcasted_iota(jnp.int32, columns.shape, 1)
    return jnp.where(
        lane % ROTARY < ROTARY // 2, pltpu.roll(columns, 112, 1), pltpu.roll(columns, 16, 1)
    )


def span(part, size, first=0):
    at = part * size + first
    return pl.ds(at if isinstance(at, int) else pl.multiple_of(at, BLOCK if size % BLOCK == 0 else size), size)


class Copies:
    def __init__(self, sems):
        self.sems, self.made = sems, {}

    def start(self, name, source, target):
        copy = pltpu.make_async_copy(source, target, self.sems.at[len(self.made)])
        self.made[name] = copy
        copy.start()

    def numbered(self, names, count):
        first = len(self.made)
        for at in range(len(names) * count):
            self.made[("kept", first + at)] = None
        return {name: first + at * count for at, name in enumerate(names)}

    def at(self, source, target, number):
        return pltpu.make_async_copy(source, target, self.sems.at[number])

    def wait(self, *names):
        for name in names:
            self.made[name].wait()


OFFSETS = tuple((planes, places) for planes in range(2) for places in range(4))
FAR = (1, 2)
CUTS = (0, 48, 96, 128)
PARTS = tuple(zip(CUTS, CUTS[1:]))
BLOCK_NAMES = tuple(o for o in OFFSETS if o != FAR) + (0, 1, 2)


def block_shapes(width):
    return [made(BLOCK, width)] * 7 + [made(high - low, width) for low, high in PARTS]


def block_copy(copies, place_ref_of, which, total, ref, columns, number):
    name = BLOCK_NAMES[which]
    low, high = PARTS[name] if isinstance(name, int) else (0, BLOCK)
    place = place_ref_of[OFFSETS.index(FAR if isinstance(name, int) else name)]
    first = pl.multiple_of(place * BLOCK, BLOCK) + low
    return copies.at(
        total.at[pl.ds(first, high - low), columns], ref.at[:, columns], number
    )


def each_block_copy(copies, places_ref, total, refs, parts, size, first, do):
    for part in parts:
        columns = span(part, size)
        for which, ref in enumerate(refs):
            number = first + part * len(refs) + which
            do(block_copy(copies, places_ref, which, total, ref, columns, number))


def start(copy):
    copy.start()


def wait(copy):
    copy.wait()


def forward_kernel(
    lengths_ref,
    freq_ref,
    gain_ref,
    bias_ref,
    b_qkv_ref,
    b_fc1_ref,
    tokens_hbm,
    cot_hbm,
    w_qkv_hbm,
    w_fc1_hbm,
    w_dense_hbm,
    w_fc2_hbm,
    hidden_hbm,
    grad_hbm,
    act_hbm,
    slope_hbm,
    ctx_hbm,
    qkv_grad_hbm,
    stats_hbm,
    branch_hbm,
    tokens,
    grad,
    hidden,
    w_qkv,
    w_fc1,
    w_dense,
    w_fc2,
    qkv,
    act,
    slope,
    ctx_grad,
    ctx,
    qkv_grad,
    cosines,
    sines,
    stats,
    turn_sum,
    value_sum,
    both_ctx,
    both_grad,
    sems,
):
    slot_len, width = tokens.shape
    blocks = slot_len // ROWS
    copies = Copies(sems)
    ends = ends_of(lengths_ref)
    row_copies = {
        "tokens": (tokens_hbm, tokens),
        "cot": (cot_hbm, grad),
        "hidden": (hidden, hidden_hbm),
        "grad": (grad, grad_hbm),
        "act": (act, act_hbm),
        "slope": (slope, slope_hbm),
    }
    numbers = copies.numbered(tuple(row_copies), blocks)
    parts, size = 4, width // 4
    first_branch = copies.numbered(("branch",), parts)["branch"]
    w_fc2_number = copies.numbered(("w_fc2",), 1)["w_fc2"]

    def rows_at(block, part=0, height=ROWS):
        return span(part, height, block * ROWS)

    def row_copy(name, block):
        source, target = row_copies[name]
        at = rows_at(block)
        return copies.at(source.at[at, :], target.at[at, :], numbers[name] + block)

    def normalise(block, part, height):
        at = rows_at(block, part, height)
        places = block * ROWS + part * height
        places = places + lax.broadcasted_iota(jnp.int32, (height, 128), 0)
        lane = lax.broadcasted_iota(jnp.int32, (height, 128), 1)
        position = (places - starts_at(ends, places)).astype(F32)
        angle = position * freq_ref[...]
        cosines[at, :] = jnp.where(lane % HEAD_DIM < ROTARY, jnp.cos(angle), 1.0)
        sine = jnp.sin(angle)
        sines[at, :] = jnp.where(
            lane % HEAD_DIM < ROTARY // 2, -sine, jnp.where(lane % HEAD_DIM < ROTARY, sine, 0.0)
        )
        valid = (places < ends[-1])[:, :1]
        inputs = tokens[at, :].astype(F32)
        mean = jnp.mean(inputs, axis=1, keepdims=True)
        center = inputs - mean
        inv_sigma = lax.rsqrt(jnp.mean(center * center, axis=1, keepdims=True) + 1e-05)
        stats[at, :] = jnp.where(lane == 0, mean, inv_sigma)
        hidden[at, :] = (
            center * inv_sigma * gain_ref[...].astype(F32)[None]
            + bias_ref[...].astype(F32)[None]
        ).astype(BF16)
        grad[at, :] = jnp.where(valid, grad[at, :], jnp.zeros((height, width), BF16))

    def turn(at, projected):
        lane = lax.broadcasted_iota(jnp.int32, (ROWS, 128), 1)
        cosine, sine = cosines[at, :], sines[at, :]
        for block in range(qkv.shape[1] // 128):
            columns = slice(block * 128, block * 128 + 128)
            plain = projected[:, columns]
            turned = plain * cosine + turned_halves(plain) * sine
            if block % 3 == 1:
                turned = jnp.where(lane < HEAD_DIM, plain, turned)
            if block % 3 == 2:
                turned = jnp.where(lane < HEAD_DIM, turned, plain)
            qkv[at, columns] = turned.astype(BF16)

    def activate(at, up, columns):
        square = up * up
        share = 0.5 * jnp.tanh(up * (GELU + (GELU * 0.044715) * square)) + 0.5
        active = up * share
        act[at, columns] = active.astype(BF16)
        slope[at, columns] = (
            share + active * (1.0 - share) * (2 * GELU + (6 * GELU * 0.044715) * square)
        ).astype(BF16)

    def attend(pair, head):
        heads = pl.ds(pl.multiple_of(pair * 6 * HEAD_DIM, 6 * HEAD_DIM), 6 * HEAD_DIM)
        wide = pl.ds(pl.multiple_of(pair * 2 * HEAD_DIM, 2 * HEAD_DIM), 2 * HEAD_DIM)
        at = 3 * HEAD_DIM * head
        mine = slice(HEAD_DIM * head, HEAD_DIM * head + HEAD_DIM)
        all_heads = qkv[:, heads]
        for block in reversed(range(slot_len // QUERIES)):
            rows = slice(block * QUERIES, block * QUERIES + QUERIES)
            reach = (block + 1) * QUERIES
            query = all_heads[rows, at : at + 64] * BF16(HEAD_DIM**-0.5)
            key = all_heads[0:reach, at + 64 : at + 128]
            value = all_heads[0:reach, at + 128 : at + 192]
            upstream = ctx_grad[rows, wide][:, mine]
            scores = dot(key, query, 1, 1)
            place = block * QUERIES + lax.broadcasted_iota(jnp.int32, (1, QUERIES), 1)
            begin = starts_at(ends, place)
            key_place = lax.broadcasted_iota(jnp.int32, (reach, QUERIES), 0)
            scores = jnp.where((key_place >= begin) & (key_place <= place), scores, -1e30)
            raised = jnp.exp(scores - jnp.max(scores, axis=0, keepdims=True))
            prob = raised * (1.0 / jnp.sum(raised, axis=0, keepdims=True))
            prob_low = prob.astype(BF16)
            context = dot(value, prob_low, 0, 0)
            prob_grad = dot(value, upstream, 1, 1)
            row_dot = jnp.sum(prob_grad * prob, axis=0, keepdims=True)
            score_grad = (prob * (prob_grad - row_dot)).astype(BF16)
            query_grad = dot(key, score_grad, 0, 0)
            value_part = dot(prob_low, upstream, 1, 0)
            key_part = dot(score_grad, query, 1, 0)
            if reach == slot_len:
                value_sum[...] = value_part
                turn_sum[:, 64:128] = key_part
            else:
                value_sum[0:reach] += value_part
                turn_sum[0:reach, 64:128] += key_part
            turn_sum[rows, 0:64] = query_grad.T * HEAD_DIM**-0.5
            both_ctx[rows, mine] = context.T.astype(BF16)
        both = turn_sum[...]
        both = both * cosines[...] - turned_halves(both) * sines[...]
        both_grad[:, at : at + 128] = both.astype(BF16)
        both_grad[:, at + 128 : at + 192] = value_sum[...].astype(BF16)
        if head:
            ctx[:, wide] = both_ctx[...]
            qkv_grad[:, heads] = both_grad[...]

    def last_weights():
        return copies.at(w_fc2_hbm, w_fc2, w_fc2_number)

    def branch_copy(part):
        columns = span(part, size)
        return copies.at(
            tokens.at[:, columns], branch_hbm.at[:, columns], first_branch + part
        )

    for name in ("tokens", "cot"):
        row_copy(name, 0).start()
    copies.start("w_qkv", w_qkv_hbm, w_qkv)
    for name in ("tokens", "cot"):
        row_copy(name, 1).start()
    copies.start("w_fc1", w_fc1_hbm, w_fc1)
    copies.start("w_dense", w_dense_hbm, w_dense)

    def one_block(block, ready):
        for name in ("tokens", "cot"):
            row_copy(name, block).wait()
        for part in range(4):
            normalise(block, part, ROWS // 4)
        for name in ("hidden", "grad"):
            row_copy(name, block).start()
        ready("w_qkv")
        at = rows_at(block)
        turn(at, dot(hidden[at, :], w_qkv[...], 1, 0) + b_qkv_ref[...].astype(F32)[None])
        ready("w_fc1", "w_dense")
        half = w_fc1.shape[1] // 2
        for part in range(2):
            columns = slice(part * half, part * half + half)
            up = dot(hidden[at, :], w_fc1[:, columns], 1, 0)
            activate(at, up + b_fc1_ref[columns].astype(F32)[None], columns)
        ctx_grad[at, :] = dot(grad[at, :], w_dense[...], 1, 1).astype(BF16)
        for name in ("act", "slope"):
            row_copy(name, block).start()

    for later in range(2, blocks):
        for name in ("tokens", "cot"):
            row_copy(name, later).start()
    last_weights().start()
    one_block(0, copies.wait)

    @pl.loop(1, blocks)
    def _(block):
        one_block(block, lambda *names: None)

    copies.start("stats", stats, stats_hbm)

    @pl.loop(0, ctx.shape[1] // (2 * HEAD_DIM))
    def _(pair):
        for head in range(2):
            attend(pair, head)

    copies.start("ctx", ctx, ctx_hbm)
    copies.start("qkv_grad", qkv_grad, qkv_grad_hbm)
    last_weights().wait()

    @pl.loop(0, parts)
    def _(part):
        columns = span(part, size)
        tokens[:, columns] = (
            dot(ctx[...], w_dense[:, columns], 1, 0) + dot(act[...], w_fc2[:, columns], 1, 0)
        ).astype(BF16)
        branch_copy(part).start()

    for name in ("hidden", "grad", "act", "slope"):
        for block in range(blocks):
            row_copy(name, block).wait()
    copies.wait("stats", "ctx", "qkv_grad")
    for part in range(parts):
        branch_copy(part).wait()


def forward(lengths, freq, tokens, cot, gain, bias, b_qkv, b_fc1, w_qkv, w_fc1, w_dense, w_fc2):
    slot_len, width = tokens.shape
    units, heads, ctx_width = w_fc2.shape[0], w_qkv.shape[1], w_dense.shape[0]
    row_kinds = (width, width, units, units, ctx_width, heads)

    def room(rows, columns, kind=BF16):
        return pltpu.VMEM((rows, columns), kind)

    return kernel_call(
        forward_kernel,
        "forward",
        [made(slot_len, columns) for columns in row_kinds]
        + [made(slot_len, 128, F32), made(slot_len, width)],
        grid=(1,),
        in_specs=[SCALARS] + [kept(a) for a in (freq, gain, bias, b_qkv, b_fc1)] + [AWAY] * 6,
        out_specs=[AWAY] * 8,
        scratch_shapes=[room(slot_len, width)] * 3
        + [pltpu.VMEM(w.shape, BF16) for w in (w_qkv, w_fc1, w_dense, w_fc2)]
        + [
            room(slot_len, heads),
            room(slot_len, units),
            room(slot_len, units),
            room(slot_len, ctx_width),
            room(slot_len, ctx_width),
            room(slot_len, heads),
        ]
        + [room(slot_len, 128, F32)] * 4
        + [
            room(slot_len, HEAD_DIM, F32),
            room(slot_len, 2 * HEAD_DIM),
            room(slot_len, 6 * HEAD_DIM),
            pltpu.SemaphoreType.DMA((80,)),
        ],
    )(lengths, freq, gain, bias, b_qkv, b_fc1, tokens, cot, w_qkv, w_fc1, w_dense, w_fc2)


def backward_kernel(
    places_ref,
    grad_hbm,
    slope_hbm,
    qkv_grad_hbm,
    tokens_hbm,
    stats_hbm,
    w_fc2_hbm,
    w_fc1_hbm,
    w_qkv_hbm,
    norm_sum_ref,
    grad_sum_ref,
    head_sum_ref,
    unit_sum_ref,
    up_grad_hbm,
    *rest,
):
    blocks, scratch = rest[: len(BLOCK_NAMES)], rest[len(BLOCK_NAMES) :]
    grad, slope, qkv_grad, tokens, stats, w_fc2, w_fc1, w_qkv, *scratch = scratch
    up_grad, hidden, gain_sum, shift_sum, grad_sum, head_sum, unit_sum, sems = scratch
    copies = Copies(sems)
    slot_len, width = grad.shape
    units, size = w_fc2.shape[0], 512

    def part_of(part):
        return span(part, size)

    def bring_rows(name, part, source, target):
        at = part_of(part)
        copies.start((name, part), source.at[at, :], target.at[at, :])

    def add_to(ref, columns, array):
        ref[:, columns] += jnp.sum(array, axis=0, keepdims=True)

    def to_units(rows, part):
        at, columns = part_of(rows), part_of(part)
        up = dot(grad[at, :], w_fc2[columns, :], 1, 1) * slope[at, columns].astype(F32)
        up = up.astype(BF16)
        up_grad[at, columns] = up
        add_to(unit_sum, columns, up.astype(F32))

    def to_hidden(rows, part):
        at, columns = part_of(rows), part_of(part)
        result = dot(up_grad[at, :], w_fc1[columns, :], 1, 1) + dot(
            qkv_grad[at, :], w_qkv[columns, :], 1, 1
        )
        hidden[at, columns] = result.astype(BF16)
        normed = (tokens[at, columns].astype(F32) - stats[at, 0:1]) * stats[at, 1:2]
        add_to(gain_sum, columns, result * normed)
        add_to(shift_sum, columns, result)

    parts = width // size
    first_block = copies.numbered(("blocks",), parts * len(blocks))["blocks"]

    def blocks_of(which, do):
        each_block_copy(copies, places_ref, hidden, blocks, which, size, first_block, do)

    for part in range(2):
        bring_rows("grad", part, grad_hbm, grad)
        bring_rows("slope", part, slope_hbm, slope)
        bring_rows("w_fc2", part, w_fc2_hbm, w_fc2)
    for total in (gain_sum, shift_sum, grad_sum, head_sum, unit_sum):
        total[...] = jnp.zeros_like(total)
    copies.wait(("w_fc2", 0), ("grad", 0), ("slope", 0))
    copies.start("w_fc1", w_fc1_hbm, w_fc1)
    copies.start("w_qkv", w_qkv_hbm, w_qkv)
    copies.start("qkv_grad", qkv_grad_hbm, qkv_grad)
    copies.start("tokens", tokens_hbm, tokens)
    copies.start("stats", stats_hbm, stats)

    @pl.loop(0, 4)
    def _(turn):
        rows, part = turn // 2, turn % 2

        @pl.when(turn == 1)
        def _():
            copies.wait(("w_fc2", 1))

        @pl.when(turn == 2)
        def _():
            copies.wait(("grad", 1), ("slope", 1))

        to_units(rows, part)

        @pl.when(part == 0)
        def _():
            add_to(grad_sum, slice(0, width), grad[part_of(rows), :].astype(F32))

    copies.start("up_grad", up_grad, up_grad_hbm)
    copies.wait("w_fc1", "w_qkv", "qkv_grad", "tokens", "stats")
    add_to(head_sum, slice(0, qkv_grad.shape[1]), qkv_grad[...].astype(F32))

    @pl.loop(0, parts)
    def _(part):
        for rows in range(slot_len // size):
            to_hidden(rows, part)
        blocks_of((part,), start)

    for ref, first, total in (
        (norm_sum_ref, 0, gain_sum),
        (norm_sum_ref, 16, shift_sum),
        (grad_sum_ref, 0, grad_sum),
        (head_sum_ref, 0, head_sum),
        (unit_sum_ref, 0, unit_sum),
    ):
        share = total.shape[1] // 16
        if share < BLOCK:
            ref[...] = jnp.zeros_like(ref)
        for row in range(16):
            ref[first + row : first + row + 1, 0:share] = total[:, row * share : row * share + share]
    copies.wait("up_grad")
    blocks_of(range(parts), wait)


def backward(places, grad, slope, qkv_grad, tokens, stats, w_fc2, w_fc1, w_qkv):
    slot_len, width = tokens.shape
    units, heads = w_fc2.shape[0], w_qkv.shape[1]
    sizes = (width, width, width, heads, units)
    sums = [made(rows, BLOCK, F32) for rows in (32, 16, 16, 16)]
    arrays = (grad, slope, qkv_grad, tokens, stats, w_fc2, w_fc1, w_qkv)
    norm_sum, grad_sum, head_sum, unit_sum, up_grad, *blocks = kernel_call(
        backward_kernel,
        "backward",
        sums + [made(slot_len, units)] + block_shapes(width),
        grid=(1,),
        in_specs=[SCALARS] + [AWAY] * len(arrays),
        out_specs=[kept(array) for array in sums] + [AWAY] * (1 + len(BLOCK_NAMES)),
        scratch_shapes=[pltpu.VMEM(array.shape, array.dtype) for array in arrays]
        + [pltpu.VMEM((slot_len, units), BF16), pltpu.VMEM((slot_len, width), BF16)]
        + [pltpu.VMEM((1, size), F32) for size in sizes]
        + [pltpu.SemaphoreType.DMA((64,))],
    )(places, *arrays)
    sums = (norm_sum, grad_sum, head_sum, unit_sum)
    return up_grad, sums, dict(zip(BLOCK_NAMES, blocks))


def weight_kernel(order_ref, *refs):
    lefts, (first_ref, second_ref, *sums, out_ref) = refs[:AT_ONCE], refs[AT_ONCE:]
    cut, end = first_ref.shape[1], first_ref.shape[1] + second_ref.shape[1]
    left = jnp.concatenate([ref[...] for ref in lefts], axis=1)
    out_ref[:, 0:cut] = dot(left, first_ref[...], 0, 0).astype(BF16)
    out_ref[:, cut:end] = dot(left, second_ref[...], 0, 0).astype(BF16)
    if sums:
        for half in range(AT_ONCE):
            block = order_ref[AT_ONCE * pl.program_id(0) + half]
            lines = [
                ref[pl.ds(first + block, 1), :]
                for ref in sums
                for first in range(0, ref.shape[0], 16)
            ]
            lines.append(jnp.zeros((BLOCK - len(lines), BLOCK), F32))
            columns = jnp.concatenate(lines, axis=0).T
            out_ref[half * BLOCK : half * BLOCK + BLOCK, end:] = columns.astype(BF16)


def weight_blocks(order, left, first, second, *sums):
    slot_len = left.shape[0]
    width = first.shape[1] + second.shape[1] + (BLOCK if sums else 0)
    return kernel_call(
        weight_kernel,
        "weights",
        made(left.shape[1], width),
        prefetch=1,
        grid=(left.shape[1] // (AT_ONCE * BLOCK),),
        in_specs=[
            *[
                pl.BlockSpec(
                    (slot_len, BLOCK),
                    functools.partial(lambda at, i, order: (0, order[AT_ONCE * i + at]), at),
                )
                for at in range(AT_ONCE)
            ],
            kept(first),
            kept(second),
            *[kept(array) for array in sums],
        ],
        out_specs=pl.BlockSpec((AT_ONCE * BLOCK, width), lambda i, order: (i, 0)),
    )(order, *[left] * AT_ONCE, first, second, *sums)


def combine(name, *sums):
    arrays = [term[0] for terms in sums for term in terms]
    specs = [
        pl.BlockSpec((term[1], term[0].shape[1]), functools.partial(lambda at, _: (at, 0), term[2]))
        for terms in sums
        for term in terms
    ]
    heights = [max(term[4] for term in terms) for terms in sums]

    def kernel(*refs):
        ins, outs = list(refs[: len(arrays)]), refs[len(arrays) :]
        for terms, height, out in zip(sums, heights, outs):
            mine = [(ins.pop(0), term[3], term[4]) for term in terms]
            cuts = sorted({cut for _, low, high in mine for cut in (low, high)})
            for low, high in zip(cuts, cuts[1:]):
                parts = [
                    ref[low - first : high - first, :].astype(F32)
                    for ref, first, last in mine
                    if first <= low and high <= last
                ]
                out[low:high, :] = functools.reduce(lambda a, b: a + b, parts).astype(BF16)

    shapes = [made(height, terms[0][0].shape[1]) for height, terms in zip(heights, sums)]
    return kernel_call(
        kernel,
        name,
        shapes,
        grid=(1,),
        in_specs=specs,
        out_specs=[pl.BlockSpec(shape.shape, lambda _: (0, 0)) for shape in shapes],
    )(*arrays)


def whole_term(array, low=0):
    return (array, array.shape[0], 0, low, low + array.shape[0])


def output_kernel(lengths_ref, tokens_ref, branch_ref, b_dense_ref, b_fc2_ref, out_ref):
    bias = b_dense_ref[...].astype(F32) + b_fc2_ref[...].astype(F32)
    rows = tokens_ref.shape[0]
    place = pl.program_id(0) * rows + lax.broadcasted_iota(jnp.int32, (rows, 1), 0)
    total = jnp.where(
        place < ends_of(lengths_ref)[-1], branch_ref[...].astype(F32) + bias[None], 0.0
    )
    out_ref[...] = (tokens_ref[...].astype(F32) + total).astype(BF16)


def finish_output(lengths, tokens, branch_sum, b_dense, b_fc2):
    slot_len, width = tokens.shape
    row = pl.BlockSpec((ROWS, width), lambda i: (i, 0))
    return kernel_call(
        output_kernel,
        "output",
        made(slot_len, width),
        grid=(slot_len // ROWS,),
        in_specs=[SCALARS, row, row, kept(b_dense), kept(b_fc2)],
        out_specs=row,
    )(lengths, tokens, branch_sum, b_dense, b_fc2)


def input_kernel(places_ref, *refs):
    *terms, tokens_ref, cot_ref, stats_ref, gain_ref, out_ref = refs
    total = functools.reduce(lambda a, b: a + b, [t[...].astype(F32) for t in terms])
    inv_sigma = stats_ref[:, 1:2]
    normed = (tokens_ref[...].astype(F32) - stats_ref[:, 0:1]) * inv_sigma
    scaled = total * gain_ref[...].astype(F32)[None]
    out_ref[...] = (
        cot_ref[...].astype(F32)
        + inv_sigma
        * (
            scaled
            - jnp.mean(scaled, axis=1, keepdims=True)
            - normed * jnp.mean(scaled * normed, axis=1, keepdims=True)
        )
    ).astype(BF16)


def input_rows(places, terms, tokens, cot, stats, gain):
    width = tokens.shape[1]

    def mine(columns):
        return pl.BlockSpec((BLOCK, columns), lambda i, places: (places[0], 0))

    return kernel_call(
        input_kernel,
        "input",
        made(BLOCK, width),
        prefetch=1,
        grid=(1,),
        in_specs=[kept(t) for t in terms] + [mine(width), mine(width), mine(128), kept(gain)],
        out_specs=pl.BlockSpec((BLOCK, width), lambda *_: (0, 0)),
    )(places, *terms, tokens, cot, stats, gain)


def place_kernel(blocks, places_ref, *refs):
    pieces, out_ref, sems = refs[: len(blocks)], refs[-2], refs[-1]
    copies = []
    for i, ((offset, low, high), piece) in enumerate(zip(blocks, pieces)):
        first = pl.multiple_of(places_ref[OFFSETS.index(offset)] * BLOCK, BLOCK)
        copies.append(
            pltpu.make_async_copy(
                piece, out_ref.at[pl.ds(first + low, high - low), :], sems.at[i]
            )
        )
    for copy in copies:
        copy.start()
    for copy in copies:
        copy.wait()


def place_rows(places, blocks, pieces, whole=None):
    rest = {} if whole is None else {"input_output_aliases": {len(pieces) + 1: 0}}
    given = [] if whole is None else [whole]
    return kernel_call(
        functools.partial(place_kernel, blocks),
        "place",
        made(8 * BLOCK, pieces[0].shape[1]),
        in_specs=[SCALARS] + [NEAR] * len(pieces) + [AWAY] * len(given),
        out_specs=AWAY,
        scratch_shapes=[pltpu.SemaphoreType.DMA((len(pieces),))],
        **rest,
    )(places, *pieces, *given)


def up_kernel(near_ref, far_ref, first_ref, second_ref):
    total = near_ref[...].astype(F32) + far_ref[...].astype(F32)
    cut = first_ref.shape[1]
    first_ref[...] = total[:, :cut]
    second_ref[...] = total[:, cut:]


def down_kernel(near_ref, far_ref, first_ref, second_ref, sums_ref):
    total = near_ref[...].astype(F32) + far_ref[...].astype(F32)
    cut, end = first_ref.shape[0], first_ref.shape[0] + second_ref.shape[0]
    first_ref[...] = total[:, :cut].T
    second_ref[...] = total[:, cut:end].T
    sums_ref[...] = total[:, end:].T[: sums_ref.shape[0]]


def last_sum(kernel, name, shapes, near, far):
    return kernel_call(
        kernel,
        name,
        [made(*shape, F32) for shape in shapes],
        grid=(1,),
        in_specs=[pl.BlockSpec(far.shape, lambda _: (0, 0))] * 2,
        out_specs=[pl.BlockSpec(shape, lambda _: (0, 0)) for shape in shapes],
    )(near, far)


def shift(array, axis, size, by):
    return lax.ppermute(array, axis, [(i, (i + by) % size) for i in range(size)])


def y_up(array):
    return shift(array, "y", 4, 1)


def y_down(array):
    return shift(array, "y", 4, 3)


def across(array):
    return shift(array, "zl", 2, 1)


def after(arrays, *earlier):
    return lax.optimization_barrier((arrays, earlier))[0]


class TensorSum:
    def __init__(self, blocks):
        self.blocks = blocks

    def send_far(self):
        b = self.blocks
        self.far = across(b[0]), y_up(b[1]), y_down(b[2])

    def send_middle(self, earlier):
        b = self.blocks
        far = *self.far[:2], after(self.far[2], earlier)
        sent = combine(
            "middle",
            *[
                [whole_term(b[offset]), whole_term(part, low)]
                for offset, part, (low, _) in zip(((0, 2), (1, 1), (1, 3)), far, PARTS)
            ],
        )
        self.middle = y_up(sent[0]), across(sent[1]), y_down(sent[2])
        return sent

    def send_near(self, earlier):
        b = self.blocks
        two_on, diagonal, other = self.middle
        other = after(other, earlier)
        sent = combine(
            "near",
            [whole_term(b[(0, 1)]), whole_term(two_on), whole_term(diagonal)],
            [whole_term(b[(1, 0)]), whole_term(other)],
        )
        self.near = [y_up(sent[0]), across(sent[1]), y_down(after(b[(0, 3)], sent))]
        return sent

    def terms(self):
        return [self.blocks[(0, 0)], *self.near]


class TensorGather:
    def __init__(self, places, rows):
        self.places, self.rows = places, rows
        self.one = y_up(rows), y_down(rows), across(rows)

    def second(self, earlier):
        before, ahead, partner = self.one = after(self.one, earlier)
        self.two = y_down(ahead), across(ahead), y_up(partner)
        return self.one

    def third(self, earlier):
        two_on, diagonal, other = self.two = after(self.two, earlier)
        (a, b), (c, d), (e, f) = PARTS
        self.three = across(two_on[a:b]), y_down(diagonal[c:d]), y_up(other[e:f])
        blocks = [(0, 0), (0, 3), (0, 1), (1, 0), (0, 2), (1, 1), (1, 3)]
        self.whole = place_rows(
            self.places,
            [(offset, 0, BLOCK) for offset in blocks],
            [self.rows, *self.one, *self.two],
        )
        return self.whole

    def finish(self, earlier):
        parts = after(self.three, earlier)
        return place_rows(
            self.places, [(FAR, low, high) for low, high in PARTS], list(parts), self.whole
        )


class DataSum:
    def __init__(self, partial_sums, earlier):
        self.near = lax.psum_scatter(
            after(partial_sums, earlier), ("x", "core"), scatter_dimension=0, tiled=True
        )

    def send(self, earlier):
        self.near = after(self.near, earlier)
        self.far = shift(self.near[BLOCK:], "zh", 2, 1)

    def finish(self, kernel, name, shapes, earlier):
        return last_sum(kernel, name, shapes, self.near, after(self.far, earlier))


def dp_order():
    half = lax.axis_index("zh")
    return jnp.stack(
        [(half + part) % 2 * 8 + block for block in range(8) for part in range(2)]
    ).astype(jnp.int32)


def per_device(
    tokens,
    cotangent,
    seq_lengths,
    ln_gain,
    ln_bias,
    w_qkv,
    b_qkv,
    w_dense,
    b_dense,
    w_fc1,
    b_fc1,
    w_fc2,
    b_fc2,
):
    units = w_fc2.shape[0]
    plane, place = lax.axis_index("zl"), lax.axis_index("y")
    places = jnp.stack(
        [(plane + planes) % 2 * 4 + (place + steps) % 4 for planes, steps in OFFSETS]
    ).astype(jnp.int32)
    order = dp_order()
    frequency = 10000.0 ** (-jnp.arange(ROTARY // 2, dtype=F32) * 2.0 / ROTARY)
    frequency = jnp.tile(frequency, 8)[None]
    hidden, grad, activated, slope, context, qkv_grad, stats, branch_part = forward(
        seq_lengths,
        frequency,
        tokens,
        cotangent,
        ln_gain,
        ln_bias,
        b_qkv,
        b_fc1,
        w_qkv,
        w_fc1,
        w_dense,
        w_fc2,
    )
    branch_sum = lax.psum(branch_part, TENSOR)
    up_grad, sums, blocks = backward(
        after(places, branch_part), grad, slope, qkv_grad, tokens, stats, w_fc2, w_fc1, w_qkv
    )
    hidden_sum = TensorSum(blocks)
    hidden_sum.send_far()
    norm_sum, *sums = sums
    norm_across = across(norm_sum)
    up_part = weight_blocks(after(order, up_grad), hidden, up_grad, qkv_grad)
    done = hidden_sum.send_middle((up_part, norm_across))
    up = DataSum(up_part, done)
    norm_sum = norm_sum + norm_across
    around = [y_up(norm_sum), y_down(norm_sum), shift(norm_sum, "y", 4, 2)]
    done = hidden_sum.send_near((done, around))
    norm_sum = norm_sum + around[0] + around[1] + around[2]
    down_part = weight_blocks(after(order, done), grad, activated, context, norm_sum, *sums)
    rows = input_rows(
        after(places, down_part), hidden_sum.terms(), tokens, cotangent, stats, ln_gain
    )
    down = DataSum(down_part, rows)
    input_grad = TensorGather(places, rows)
    done = input_grad.second((rows, branch_sum))
    up.send(done)
    down.send(up.near)
    output = finish_output(after(seq_lengths, down.near), tokens, branch_sum, b_dense, b_fc2)
    done = input_grad.third(output)
    input_grad.three = after(input_grad.three, done)
    grad_fc1, grad_qkv = up.finish(
        up_kernel, "up", ((BLOCK, units), (BLOCK, w_qkv.shape[1])), input_grad.three[0]
    )
    grad_fc2, grad_dense, small = down.finish(
        down_kernel,
        "down",
        ((units, BLOCK), (w_dense.shape[0], BLOCK), (8, BLOCK)),
        grad_qkv,
    )
    input_grad = input_grad.finish(small)
    out_bias = small[2]
    return (
        output,
        input_grad,
        small[0],
        small[1],
        grad_qkv,
        small[3, :48],
        grad_dense,
        out_bias,
        grad_fc1,
        small[4, :64],
        grad_fc2,
        out_bias,
    )


def solution(mesh):
    parts = Mesh(mesh.devices.reshape(2, 4, 2, 2, 4), DP + TENSOR)
    rows = P(DP, None)
    placed = (
        rows,
        rows,
        rows,
        P(),
        P(),
        P(None, TENSOR),
        P(TENSOR),
        P(TENSOR, None),
        P(),
        P(None, TENSOR),
        P(TENSOR),
        P(TENSOR, None),
        P(),
    )
    return jax.shard_map(
        per_device,
        mesh=parts,
        in_specs=placed,
        out_specs=(
            rows,
            rows,
            P(DP),
            P(DP),
            P(DP, TENSOR),
            P(TENSOR + DP),
            P(TENSOR, DP),
            P(DP),
            P(DP, TENSOR),
            P(TENSOR + DP),
            P(TENSOR, DP),
            P(DP),
        ),
        check_vma=False,
    )
```

```python
import functools

import jax
import jax.numpy as jnp
from jax import lax
from jax.experimental import pallas as pl
from jax.experimental.pallas import tpu as pltpu
from jax.sharding import Mesh
from jax.sharding import PartitionSpec as P

HEAD_DIM = 64
ROTARY = 32
DP = ("zh", "x", "core")
TENSOR = ("zl", "y")
BF16 = jnp.bfloat16
F32 = jnp.float32
ROWS = 256
QUERIES = 512
BLOCK = 128
AT_ONCE = 4
VMEM_BYTES = 56 * 2**20
GELU = 0.7978845608


def dot(left, right, left_dim, right_dim):
    return lax.dot_general(
        left, right, (((left_dim,), (right_dim,)), ((), ())), preferred_element_type=F32
    )


def kernel_call(kernel, name, out_shape, prefetch=0, vmem=VMEM_BYTES, flops=1, **spec):
    if prefetch:
        spec = {
            "grid_spec": pltpu.PrefetchScalarGridSpec(
                num_scalar_prefetch=prefetch,
                grid=spec.pop("grid"),
                in_specs=spec.pop("in_specs"),
                out_specs=spec.pop("out_specs"),
                scratch_shapes=spec.pop("scratch_shapes", ()),
            ),
            **spec,
        }
    return pl.pallas_call(
        kernel,
        out_shape=out_shape,
        compiler_params=pltpu.CompilerParams(vmem_limit_bytes=vmem),
        cost_estimate=pl.CostEstimate(flops=flops, bytes_accessed=1, transcendentals=0),
        name=name,
        **spec,
    )


def made(rows, columns, kind=BF16):
    return jax.ShapeDtypeStruct((rows, columns), kind)


def kept(array):
    return pl.BlockSpec(array.shape, lambda *_: (0,) * array.ndim)


AWAY = pl.BlockSpec(memory_space=pltpu.HBM)
NEAR = pl.BlockSpec(memory_space=pltpu.VMEM)
SCALARS = pl.BlockSpec(memory_space=pltpu.SMEM)


def ends_of(lengths_ref):
    ends = [lengths_ref[0, 0]]
    for place in range(1, lengths_ref.shape[1]):
        ends.append(ends[-1] + lengths_ref[0, place])
    return ends


def starts_at(ends, places):
    start = jnp.zeros_like(places)
    for end in ends:
        start = jnp.maximum(start, jnp.where(places >= end, end, 0))
    return start


def turned_halves(columns):
    lane = lax.broadcasted_iota(jnp.int32, columns.shape, 1)
    return jnp.where(
        lane % ROTARY < ROTARY // 2, pltpu.roll(columns, 112, 1), pltpu.roll(columns, 16, 1)
    )


def span(part, size, first=0):
    at = part * size + first
    return pl.ds(at if isinstance(at, int) else pl.multiple_of(at, BLOCK if size % BLOCK == 0 else size), size)


class Copies:
    def __init__(self, sems):
        self.sems, self.made = sems, {}

    def start(self, name, source, target):
        copy = pltpu.make_async_copy(source, target, self.sems.at[len(self.made)])
        self.made[name] = copy
        copy.start()

    def numbered(self, names, count):
        first = len(self.made)
        for at in range(len(names) * count):
            self.made[("kept", first + at)] = None
        return {name: first + at * count for at, name in enumerate(names)}

    def at(self, source, target, number):
        return pltpu.make_async_copy(source, target, self.sems.at[number])

    def wait(self, *names):
        for name in names:
            self.made[name].wait()


OFFSETS = tuple((planes, places) for planes in range(2) for places in range(4))
FAR = (1, 2)
CUTS = (0, 48, 96, 128)
PARTS = tuple(zip(CUTS, CUTS[1:]))
BLOCK_NAMES = tuple(o for o in OFFSETS if o != FAR) + (0, 1, 2)


def block_shapes(width):
    return [made(BLOCK, width)] * 7 + [made(high - low, width) for low, high in PARTS]


def block_copy(copies, place_ref_of, which, total, ref, columns, number):
    name = BLOCK_NAMES[which]
    low, high = PARTS[name] if isinstance(name, int) else (0, BLOCK)
    place = place_ref_of[OFFSETS.index(FAR if isinstance(name, int) else name)]
    first = pl.multiple_of(place * BLOCK, BLOCK) + low
    return copies.at(
        total.at[pl.ds(first, high - low), columns], ref.at[:, columns], number
    )


def each_block_copy(copies, places_ref, total, refs, parts, size, first, do):
    for part in parts:
        columns = span(part, size)
        for which, ref in enumerate(refs):
            number = first + part * len(refs) + which
            do(block_copy(copies, places_ref, which, total, ref, columns, number))


def start(copy):
    copy.start()


def wait(copy):
    copy.wait()


def forward_kernel(
    lengths_ref,
    freq_ref,
    gain_ref,
    bias_ref,
    b_qkv_ref,
    b_fc1_ref,
    tokens_hbm,
    cot_hbm,
    w_qkv_hbm,
    w_fc1_hbm,
    w_dense_hbm,
    w_fc2_hbm,
    hidden_hbm,
    grad_hbm,
    act_hbm,
    slope_hbm,
    ctx_hbm,
    qkv_grad_hbm,
    stats_hbm,
    branch_hbm,
    tokens,
    grad,
    hidden,
    w_qkv,
    w_fc1,
    w_dense,
    w_fc2,
    qkv,
    act,
    slope,
    ctx_grad,
    ctx,
    qkv_grad,
    cosines,
    sines,
    stats,
    turn_sum,
    value_sum,
    both_ctx,
    both_grad,
    sems,
):
    slot_len, width = tokens.shape
    blocks = slot_len // ROWS
    copies = Copies(sems)
    ends = ends_of(lengths_ref)
    row_copies = {
        "tokens": (tokens_hbm, tokens),
        "cot": (cot_hbm, grad),
        "hidden": (hidden, hidden_hbm),
        "grad": (grad, grad_hbm),
        "act": (act, act_hbm),
        "slope": (slope, slope_hbm),
    }
    numbers = copies.numbered(tuple(row_copies), blocks)
    parts, size = 4, width // 4
    first_branch = copies.numbered(("branch",), parts)["branch"]
    w_fc2_number = copies.numbered(("w_fc2",), 1)["w_fc2"]

    def rows_at(block, part=0, height=ROWS):
        return span(part, height, block * ROWS)

    def row_copy(name, block):
        source, target = row_copies[name]
        at = rows_at(block)
        return copies.at(source.at[at, :], target.at[at, :], numbers[name] + block)

    def normalise(block, part, height):
        at = rows_at(block, part, height)
        places = block * ROWS + part * height
        places = places + lax.broadcasted_iota(jnp.int32, (height, 128), 0)
        lane = lax.broadcasted_iota(jnp.int32, (height, 128), 1)
        position = (places - starts_at(ends, places)).astype(F32)
        angle = position * freq_ref[...]
        cosines[at, :] = jnp.where(lane % HEAD_DIM < ROTARY, jnp.cos(angle), 1.0)
        sine = jnp.sin(angle)
        sines[at, :] = jnp.where(
            lane % HEAD_DIM < ROTARY // 2, -sine, jnp.where(lane % HEAD_DIM < ROTARY, sine, 0.0)
        )
        valid = (places < ends[-1])[:, :1]
        inputs = tokens[at, :].astype(F32)
        mean = jnp.mean(inputs, axis=1, keepdims=True)
        center = inputs - mean
        inv_sigma = lax.rsqrt(jnp.mean(center * center, axis=1, keepdims=True) + 1e-05)
        stats[at, :] = jnp.where(lane == 0, mean, inv_sigma)
        hidden[at, :] = (
            center * inv_sigma * gain_ref[...].astype(F32)[None]
            + bias_ref[...].astype(F32)[None]
        ).astype(BF16)
        grad[at, :] = jnp.where(valid, grad[at, :], jnp.zeros((height, width), BF16))

    def turn(at, projected):
        lane = lax.broadcasted_iota(jnp.int32, (ROWS, 128), 1)
        cosine, sine = cosines[at, :], sines[at, :]
        for block in range(qkv.shape[1] // 128):
            columns = slice(block * 128, block * 128 + 128)
            plain = projected[:, columns]
            turned = plain * cosine + turned_halves(plain) * sine
            if block % 3 == 1:
                turned = jnp.where(lane < HEAD_DIM, plain, turned)
            if block % 3 == 2:
                turned = jnp.where(lane < HEAD_DIM, turned, plain)
            qkv[at, columns] = turned.astype(BF16)

    def activate(at, up, columns):
        square = up * up
        share = 0.5 * jnp.tanh(up * (GELU + (GELU * 0.044715) * square)) + 0.5
        active = up * share
        act[at, columns] = active.astype(BF16)
        slope[at, columns] = (
            share + active * (1.0 - share) * (2 * GELU + (6 * GELU * 0.044715) * square)
        ).astype(BF16)

    def attend(pair, head):
        heads = pl.ds(pl.multiple_of(pair * 6 * HEAD_DIM, 6 * HEAD_DIM), 6 * HEAD_DIM)
        wide = pl.ds(pl.multiple_of(pair * 2 * HEAD_DIM, 2 * HEAD_DIM), 2 * HEAD_DIM)
        at = 3 * HEAD_DIM * head
        mine = slice(HEAD_DIM * head, HEAD_DIM * head + HEAD_DIM)
        all_heads = qkv[:, heads]
        for block in reversed(range(slot_len // QUERIES)):
            rows = slice(block * QUERIES, block * QUERIES + QUERIES)
            reach = (block + 1) * QUERIES
            query = all_heads[rows, at : at + 64] * BF16(HEAD_DIM**-0.5)
            key = all_heads[0:reach, at + 64 : at + 128]
            value = all_heads[0:reach, at + 128 : at + 192]
            upstream = ctx_grad[rows, wide][:, mine]
            scores = dot(key, query, 1, 1)
            place = block * QUERIES + lax.broadcasted_iota(jnp.int32, (1, QUERIES), 1)
            begin = starts_at(ends, place)
            key_place = lax.broadcasted_iota(jnp.int32, (reach, QUERIES), 0)
            scores = jnp.where((key_place >= begin) & (key_place <= place), scores, -1e30)
            raised = jnp.exp(scores - jnp.max(scores, axis=0, keepdims=True))
            prob = raised * (1.0 / jnp.sum(raised, axis=0, keepdims=True))
            prob_low = prob.astype(BF16)
            context = dot(value, prob_low, 0, 0)
            prob_grad = dot(value, upstream, 1, 1)
            row_dot = jnp.sum(prob_grad * prob, axis=0, keepdims=True)
            score_grad = (prob * (prob_grad - row_dot)).astype(BF16)
            query_grad = dot(key, score_grad, 0, 0)
            value_part = dot(prob_low, upstream, 1, 0)
            key_part = dot(score_grad, query, 1, 0)
            if reach == slot_len:
                value_sum[...] = value_part
                turn_sum[:, 64:128] = key_part
            else:
                value_sum[0:reach] += value_part
                turn_sum[0:reach, 64:128] += key_part
            turn_sum[rows, 0:64] = query_grad.T * HEAD_DIM**-0.5
            both_ctx[rows, mine] = context.T.astype(BF16)
        both = turn_sum[...]
        both = both * cosines[...] - turned_halves(both) * sines[...]
        both_grad[:, at : at + 128] = both.astype(BF16)
        both_grad[:, at + 128 : at + 192] = value_sum[...].astype(BF16)
        if head:
            ctx[:, wide] = both_ctx[...]
            qkv_grad[:, heads] = both_grad[...]

    def last_weights():
        return copies.at(w_fc2_hbm, w_fc2, w_fc2_number)

    def branch_copy(part):
        columns = span(part, size)
        return copies.at(
            tokens.at[:, columns], branch_hbm.at[:, columns], first_branch + part
        )

    for name in ("tokens", "cot"):
        row_copy(name, 0).start()
    copies.start("w_qkv", w_qkv_hbm, w_qkv)
    for name in ("tokens", "cot"):
        row_copy(name, 1).start()
    copies.start("w_fc1", w_fc1_hbm, w_fc1)
    copies.start("w_dense", w_dense_hbm, w_dense)

    def one_block(block, ready):
        for name in ("tokens", "cot"):
            row_copy(name, block).wait()
        for part in range(4):
            normalise(block, part, ROWS // 4)
        for name in ("hidden", "grad"):
            row_copy(name, block).start()
        ready("w_qkv")
        at = rows_at(block)
        turn(at, dot(hidden[at, :], w_qkv[...], 1, 0) + b_qkv_ref[...].astype(F32)[None])
        ready("w_fc1", "w_dense")
        half = w_fc1.shape[1] // 2
        for part in range(2):
            columns = slice(part * half, part * half + half)
            up = dot(hidden[at, :], w_fc1[:, columns], 1, 0)
            activate(at, up + b_fc1_ref[columns].astype(F32)[None], columns)
        ctx_grad[at, :] = dot(grad[at, :], w_dense[...], 1, 1).astype(BF16)
        for name in ("act", "slope"):
            row_copy(name, block).start()

    for later in range(2, blocks):
        for name in ("tokens", "cot"):
            row_copy(name, later).start()
    last_weights().start()
    one_block(0, copies.wait)

    @pl.loop(1, blocks)
    def _(block):
        one_block(block, lambda *names: None)

    copies.start("stats", stats, stats_hbm)

    @pl.loop(0, ctx.shape[1] // (2 * HEAD_DIM))
    def _(pair):
        for head in range(2):
            attend(pair, head)

    copies.start("ctx", ctx, ctx_hbm)
    copies.start("qkv_grad", qkv_grad, qkv_grad_hbm)
    last_weights().wait()

    @pl.loop(0, parts)
    def _(part):
        columns = span(part, size)
        tokens[:, columns] = (
            dot(ctx[...], w_dense[:, columns], 1, 0) + dot(act[...], w_fc2[:, columns], 1, 0)
        ).astype(BF16)
        branch_copy(part).start()

    for name in ("hidden", "grad", "act", "slope"):
        for block in range(blocks):
            row_copy(name, block).wait()
    copies.wait("stats", "ctx", "qkv_grad")
    for part in range(parts):
        branch_copy(part).wait()


def forward(lengths, freq, tokens, cot, gain, bias, b_qkv, b_fc1, w_qkv, w_fc1, w_dense, w_fc2):
    slot_len, width = tokens.shape
    units, heads, ctx_width = w_fc2.shape[0], w_qkv.shape[1], w_dense.shape[0]
    row_kinds = (width, width, units, units, ctx_width, heads)

    def room(rows, columns, kind=BF16):
        return pltpu.VMEM((rows, columns), kind)

    return kernel_call(
        forward_kernel,
        "forward",
        [made(slot_len, columns) for columns in row_kinds]
        + [made(slot_len, 128, F32), made(slot_len, width)],
        grid=(1,),
        in_specs=[SCALARS] + [kept(a) for a in (freq, gain, bias, b_qkv, b_fc1)] + [AWAY] * 6,
        out_specs=[AWAY] * 8,
        scratch_shapes=[room(slot_len, width)] * 3
        + [pltpu.VMEM(w.shape, BF16) for w in (w_qkv, w_fc1, w_dense, w_fc2)]
        + [
            room(slot_len, heads),
            room(slot_len, units),
            room(slot_len, units),
            room(slot_len, ctx_width),
            room(slot_len, ctx_width),
            room(slot_len, heads),
        ]
        + [room(slot_len, 128, F32)] * 4
        + [
            room(slot_len, HEAD_DIM, F32),
            room(slot_len, 2 * HEAD_DIM),
            room(slot_len, 6 * HEAD_DIM),
            pltpu.SemaphoreType.DMA((80,)),
        ],
    )(lengths, freq, gain, bias, b_qkv, b_fc1, tokens, cot, w_qkv, w_fc1, w_dense, w_fc2)


def backward_kernel(
    places_ref,
    grad_hbm,
    slope_hbm,
    qkv_grad_hbm,
    tokens_hbm,
    stats_hbm,
    w_fc2_hbm,
    w_fc1_hbm,
    w_qkv_hbm,
    norm_sum_ref,
    grad_sum_ref,
    head_sum_ref,
    unit_sum_ref,
    up_grad_hbm,
    *rest,
):
    blocks, scratch = rest[: len(BLOCK_NAMES)], rest[len(BLOCK_NAMES) :]
    grad, slope, qkv_grad, tokens, stats, w_fc2, w_fc1, w_qkv, *scratch = scratch
    up_grad, hidden, gain_sum, shift_sum, grad_sum, head_sum, unit_sum, sems = scratch
    copies = Copies(sems)
    slot_len, width = grad.shape
    units, size = w_fc2.shape[0], 512

    def part_of(part):
        return span(part, size)

    def bring_rows(name, part, source, target):
        at = part_of(part)
        copies.start((name, part), source.at[at, :], target.at[at, :])

    def add_to(ref, columns, array):
        ref[:, columns] += jnp.sum(array, axis=0, keepdims=True)

    def to_units(rows, part):
        at, columns = part_of(rows), part_of(part)
        up = dot(grad[at, :], w_fc2[columns, :], 1, 1) * slope[at, columns].astype(F32)
        up = up.astype(BF16)
        up_grad[at, columns] = up
        add_to(unit_sum, columns, up.astype(F32))

    def to_hidden(rows, part):
        at, columns = part_of(rows), part_of(part)
        result = dot(up_grad[at, :], w_fc1[columns, :], 1, 1) + dot(
            qkv_grad[at, :], w_qkv[columns, :], 1, 1
        )
        hidden[at, columns] = result.astype(BF16)
        normed = (tokens[at, columns].astype(F32) - stats[at, 0:1]) * stats[at, 1:2]
        add_to(gain_sum, columns, result * normed)
        add_to(shift_sum, columns, result)

    parts = width // size
    first_block = copies.numbered(("blocks",), parts * len(blocks))["blocks"]

    def blocks_of(which, do):
        each_block_copy(copies, places_ref, hidden, blocks, which, size, first_block, do)

    for part in range(2):
        bring_rows("grad", part, grad_hbm, grad)
        bring_rows("slope", part, slope_hbm, slope)
        bring_rows("w_fc2", part, w_fc2_hbm, w_fc2)
    for total in (gain_sum, shift_sum, grad_sum, head_sum, unit_sum):
        total[...] = jnp.zeros_like(total)
    copies.wait(("w_fc2", 0), ("grad", 0), ("slope", 0))
    copies.start("w_fc1", w_fc1_hbm, w_fc1)
    copies.start("w_qkv", w_qkv_hbm, w_qkv)
    copies.start("qkv_grad", qkv_grad_hbm, qkv_grad)
    copies.start("tokens", tokens_hbm, tokens)
    copies.start("stats", stats_hbm, stats)

    @pl.loop(0, 4)
    def _(turn):
        rows, part = turn // 2, turn % 2

        @pl.when(turn == 1)
        def _():
            copies.wait(("w_fc2", 1))

        @pl.when(turn == 2)
        def _():
            copies.wait(("grad", 1), ("slope", 1))

        to_units(rows, part)

        @pl.when(part == 0)
        def _():
            add_to(grad_sum, slice(0, width), grad[part_of(rows), :].astype(F32))

    copies.start("up_grad", up_grad, up_grad_hbm)
    copies.wait("w_fc1", "w_qkv", "qkv_grad", "tokens", "stats")
    add_to(head_sum, slice(0, qkv_grad.shape[1]), qkv_grad[...].astype(F32))

    @pl.loop(0, parts)
    def _(part):
        for rows in range(slot_len // size):
            to_hidden(rows, part)
        blocks_of((part,), start)

    for ref, first, total in (
        (norm_sum_ref, 0, gain_sum),
        (norm_sum_ref, 16, shift_sum),
        (grad_sum_ref, 0, grad_sum),
        (head_sum_ref, 0, head_sum),
        (unit_sum_ref, 0, unit_sum),
    ):
        share = total.shape[1] // 16
        if share < BLOCK:
            ref[...] = jnp.zeros_like(ref)
        for row in range(16):
            ref[first + row : first + row + 1, 0:share] = total[:, row * share : row * share + share]
    copies.wait("up_grad")
    blocks_of(range(parts), wait)


def backward(places, grad, slope, qkv_grad, tokens, stats, w_fc2, w_fc1, w_qkv):
    slot_len, width = tokens.shape
    units, heads = w_fc2.shape[0], w_qkv.shape[1]
    sizes = (width, width, width, heads, units)
    sums = [made(rows, BLOCK, F32) for rows in (32, 16, 16, 16)]
    arrays = (grad, slope, qkv_grad, tokens, stats, w_fc2, w_fc1, w_qkv)
    norm_sum, grad_sum, head_sum, unit_sum, up_grad, *blocks = kernel_call(
        backward_kernel,
        "backward",
        sums + [made(slot_len, units)] + block_shapes(width),
        grid=(1,),
        in_specs=[SCALARS] + [AWAY] * len(arrays),
        out_specs=[kept(array) for array in sums] + [AWAY] * (1 + len(BLOCK_NAMES)),
        scratch_shapes=[pltpu.VMEM(array.shape, array.dtype) for array in arrays]
        + [pltpu.VMEM((slot_len, units), BF16), pltpu.VMEM((slot_len, width), BF16)]
        + [pltpu.VMEM((1, size), F32) for size in sizes]
        + [pltpu.SemaphoreType.DMA((64,))],
    )(places, *arrays)
    sums = (norm_sum, grad_sum, head_sum, unit_sum)
    return up_grad, sums, dict(zip(BLOCK_NAMES, blocks))


def weight_kernel(order_ref, *refs):
    lefts, (first_ref, second_ref, *sums, out_ref) = refs[:AT_ONCE], refs[AT_ONCE:]
    cut, end = first_ref.shape[1], first_ref.shape[1] + second_ref.shape[1]
    left = jnp.concatenate([ref[...] for ref in lefts], axis=1)
    out_ref[:, 0:cut] = dot(left, first_ref[...], 0, 0).astype(BF16)
    out_ref[:, cut:end] = dot(left, second_ref[...], 0, 0).astype(BF16)
    if sums:
        for half in range(AT_ONCE):
            block = order_ref[AT_ONCE * pl.program_id(0) + half]
            lines = [
                ref[pl.ds(first + block, 1), :]
                for ref in sums
                for first in range(0, ref.shape[0], 16)
            ]
            lines.append(jnp.zeros((BLOCK - len(lines), BLOCK), F32))
            columns = jnp.concatenate(lines, axis=0).T
            out_ref[half * BLOCK : half * BLOCK + BLOCK, end:] = columns.astype(BF16)


def weight_blocks(order, left, first, second, *sums):
    slot_len = left.shape[0]
    width = first.shape[1] + second.shape[1] + (BLOCK if sums else 0)
    return kernel_call(
        weight_kernel,
        "weights",
        made(left.shape[1], width),
        prefetch=1,
        grid=(left.shape[1] // (AT_ONCE * BLOCK),),
        in_specs=[
            *[
                pl.BlockSpec(
                    (slot_len, BLOCK),
                    functools.partial(lambda at, i, order: (0, order[AT_ONCE * i + at]), at),
                )
                for at in range(AT_ONCE)
            ],
            kept(first),
            kept(second),
            *[kept(array) for array in sums],
        ],
        out_specs=pl.BlockSpec((AT_ONCE * BLOCK, width), lambda i, order: (i, 0)),
    )(order, *[left] * AT_ONCE, first, second, *sums)


def combine(name, *sums):
    arrays = [term[0] for terms in sums for term in terms]
    specs = [
        pl.BlockSpec((term[1], term[0].shape[1]), functools.partial(lambda at, _: (at, 0), term[2]))
        for terms in sums
        for term in terms
    ]
    heights = [max(term[4] for term in terms) for terms in sums]

    def kernel(*refs):
        ins, outs = list(refs[: len(arrays)]), refs[len(arrays) :]
        for terms, height, out in zip(sums, heights, outs):
            mine = [(ins.pop(0), term[3], term[4]) for term in terms]
            cuts = sorted({cut for _, low, high in mine for cut in (low, high)})
            for low, high in zip(cuts, cuts[1:]):
                parts = [
                    ref[low - first : high - first, :].astype(F32)
                    for ref, first, last in mine
                    if first <= low and high <= last
                ]
                out[low:high, :] = functools.reduce(lambda a, b: a + b, parts).astype(BF16)

    shapes = [made(height, terms[0][0].shape[1]) for height, terms in zip(heights, sums)]
    return kernel_call(
        kernel,
        name,
        shapes,
        grid=(1,),
        in_specs=specs,
        out_specs=[pl.BlockSpec(shape.shape, lambda _: (0, 0)) for shape in shapes],
    )(*arrays)


def whole_term(array, low=0):
    return (array, array.shape[0], 0, low, low + array.shape[0])


def output_kernel(lengths_ref, tokens_ref, branch_ref, b_dense_ref, b_fc2_ref, out_ref):
    bias = b_dense_ref[...].astype(F32) + b_fc2_ref[...].astype(F32)
    rows = tokens_ref.shape[0]
    place = pl.program_id(0) * rows + lax.broadcasted_iota(jnp.int32, (rows, 1), 0)
    total = jnp.where(
        place < ends_of(lengths_ref)[-1], branch_ref[...].astype(F32) + bias[None], 0.0
    )
    out_ref[...] = (tokens_ref[...].astype(F32) + total).astype(BF16)


def finish_output(lengths, tokens, branch_sum, b_dense, b_fc2):
    slot_len, width = tokens.shape
    row = pl.BlockSpec((ROWS, width), lambda i: (i, 0))
    return kernel_call(
        output_kernel,
        "output",
        made(slot_len, width),
        grid=(slot_len // ROWS,),
        in_specs=[SCALARS, row, row, kept(b_dense), kept(b_fc2)],
        out_specs=row,
    )(lengths, tokens, branch_sum, b_dense, b_fc2)


def input_kernel(places_ref, *refs):
    *terms, tokens_ref, cot_ref, stats_ref, gain_ref, out_ref = refs
    total = functools.reduce(lambda a, b: a + b, [t[...].astype(F32) for t in terms])
    inv_sigma = stats_ref[:, 1:2]
    normed = (tokens_ref[...].astype(F32) - stats_ref[:, 0:1]) * inv_sigma
    scaled = total * gain_ref[...].astype(F32)[None]
    out_ref[...] = (
        cot_ref[...].astype(F32)
        + inv_sigma
        * (
            scaled
            - jnp.mean(scaled, axis=1, keepdims=True)
            - normed * jnp.mean(scaled * normed, axis=1, keepdims=True)
        )
    ).astype(BF16)


def input_rows(places, terms, tokens, cot, stats, gain):
    width = tokens.shape[1]

    def mine(columns):
        return pl.BlockSpec((BLOCK, columns), lambda i, places: (places[0], 0))

    return kernel_call(
        input_kernel,
        "input",
        made(BLOCK, width),
        prefetch=1,
        grid=(1,),
        in_specs=[kept(t) for t in terms] + [mine(width), mine(width), mine(128), kept(gain)],
        out_specs=pl.BlockSpec((BLOCK, width), lambda *_: (0, 0)),
    )(places, *terms, tokens, cot, stats, gain)


def place_kernel(blocks, places_ref, *refs):
    pieces, out_ref, sems = refs[: len(blocks)], refs[-2], refs[-1]
    copies = []
    for i, ((offset, low, high), piece) in enumerate(zip(blocks, pieces)):
        first = pl.multiple_of(places_ref[OFFSETS.index(offset)] * BLOCK, BLOCK)
        copies.append(
            pltpu.make_async_copy(
                piece, out_ref.at[pl.ds(first + low, high - low), :], sems.at[i]
            )
        )
    for copy in copies:
        copy.start()
    for copy in copies:
        copy.wait()


def place_rows(places, blocks, pieces, whole=None):
    rest = {} if whole is None else {"input_output_aliases": {len(pieces) + 1: 0}}
    given = [] if whole is None else [whole]
    return kernel_call(
        functools.partial(place_kernel, blocks),
        "place",
        made(8 * BLOCK, pieces[0].shape[1]),
        in_specs=[SCALARS] + [NEAR] * len(pieces) + [AWAY] * len(given),
        out_specs=AWAY,
        scratch_shapes=[pltpu.SemaphoreType.DMA((len(pieces),))],
        **rest,
    )(places, *pieces, *given)


def up_kernel(near_ref, far_ref, first_ref, second_ref):
    total = near_ref[...].astype(F32) + far_ref[...].astype(F32)
    cut = first_ref.shape[1]
    first_ref[...] = total[:, :cut]
    second_ref[...] = total[:, cut:]


def down_kernel(near_ref, far_ref, first_ref, second_ref, sums_ref):
    total = near_ref[...].astype(F32) + far_ref[...].astype(F32)
    cut, end = first_ref.shape[0], first_ref.shape[0] + second_ref.shape[0]
    first_ref[...] = total[:, :cut].T
    second_ref[...] = total[:, cut:end].T
    sums_ref[...] = total[:, end:].T[: sums_ref.shape[0]]


def last_sum(kernel, name, shapes, near, far):
    return kernel_call(
        kernel,
        name,
        [made(*shape, F32) for shape in shapes],
        grid=(1,),
        in_specs=[pl.BlockSpec(far.shape, lambda _: (0, 0))] * 2,
        out_specs=[pl.BlockSpec(shape, lambda _: (0, 0)) for shape in shapes],
    )(near, far)


def shift(array, axis, size, by):
    return lax.ppermute(array, axis, [(i, (i + by) % size) for i in range(size)])


def y_up(array):
    return shift(array, "y", 4, 1)


def y_down(array):
    return shift(array, "y", 4, 3)


def across(array):
    return shift(array, "zl", 2, 1)


def after(arrays, *earlier):
    return lax.optimization_barrier((arrays, earlier))[0]


class TensorSum:
    def __init__(self, blocks):
        self.blocks = blocks

    def send_far(self):
        b = self.blocks
        self.far = across(b[0]), y_up(b[1]), y_down(b[2])

    def send_middle(self, earlier):
        b = self.blocks
        far = *self.far[:2], after(self.far[2], earlier)
        sent = combine(
            "middle",
            *[
                [whole_term(b[offset]), whole_term(part, low)]
                for offset, part, (low, _) in zip(((0, 2), (1, 1), (1, 3)), far, PARTS)
            ],
        )
        self.middle = y_up(sent[0]), across(sent[1]), y_down(sent[2])
        return sent

    def send_near(self, earlier):
        b = self.blocks
        two_on, diagonal, other = self.middle
        other = after(other, earlier)
        sent = combine(
            "near",
            [whole_term(b[(0, 1)]), whole_term(two_on), whole_term(diagonal)],
            [whole_term(b[(1, 0)]), whole_term(other)],
        )
        self.near = [y_up(sent[0]), across(sent[1]), y_down(after(b[(0, 3)], sent))]
        return sent

    def terms(self):
        return [self.blocks[(0, 0)], *self.near]


class TensorGather:
    def __init__(self, places, rows):
        self.places, self.rows = places, rows
        self.one = y_up(rows), y_down(rows), across(rows)

    def second(self, earlier):
        before, ahead, partner = self.one = after(self.one, earlier)
        self.two = y_down(ahead), across(ahead), y_up(partner)
        return self.one

    def third(self, earlier):
        two_on, diagonal, other = self.two = after(self.two, earlier)
        (a, b), (c, d), (e, f) = PARTS
        self.three = across(two_on[a:b]), y_down(diagonal[c:d]), y_up(other[e:f])
        blocks = [(0, 0), (0, 3), (0, 1), (1, 0), (0, 2), (1, 1), (1, 3)]
        self.whole = place_rows(
            self.places,
            [(offset, 0, BLOCK) for offset in blocks],
            [self.rows, *self.one, *self.two],
        )
        return self.whole

    def finish(self, earlier):
        parts = after(self.three, earlier)
        return place_rows(
            self.places, [(FAR, low, high) for low, high in PARTS], list(parts), self.whole
        )


class DataSum:
    def __init__(self, partial_sums, earlier):
        self.near = lax.psum_scatter(
            after(partial_sums, earlier), ("x", "core"), scatter_dimension=0, tiled=True
        )

    def send(self, earlier):
        self.near = after(self.near, earlier)
        self.far = shift(self.near[BLOCK:], "zh", 2, 1)

    def finish(self, kernel, name, shapes, earlier):
        return last_sum(kernel, name, shapes, self.near, after(self.far, earlier))


def dp_order():
    half = lax.axis_index("zh")
    return jnp.stack(
        [(half + part) % 2 * 8 + block for block in range(8) for part in range(2)]
    ).astype(jnp.int32)


def per_device(
    tokens,
    cotangent,
    seq_lengths,
    ln_gain,
    ln_bias,
    w_qkv,
    b_qkv,
    w_dense,
    b_dense,
    w_fc1,
    b_fc1,
    w_fc2,
    b_fc2,
):
    units = w_fc2.shape[0]
    plane, place = lax.axis_index("zl"), lax.axis_index("y")
    places = jnp.stack(
        [(plane + planes) % 2 * 4 + (place + steps) % 4 for planes, steps in OFFSETS]
    ).astype(jnp.int32)
    order = dp_order()
    frequency = 10000.0 ** (-jnp.arange(ROTARY // 2, dtype=F32) * 2.0 / ROTARY)
    frequency = jnp.tile(frequency, 8)[None]
    hidden, grad, activated, slope, context, qkv_grad, stats, branch_part = forward(
        seq_lengths,
        frequency,
        tokens,
        cotangent,
        ln_gain,
        ln_bias,
        b_qkv,
        b_fc1,
        w_qkv,
        w_fc1,
        w_dense,
        w_fc2,
    )
    branch_sum = lax.psum(branch_part, TENSOR)
    up_grad, sums, blocks = backward(
        after(places, branch_part), grad, slope, qkv_grad, tokens, stats, w_fc2, w_fc1, w_qkv
    )
    hidden_sum = TensorSum(blocks)
    hidden_sum.send_far()
    down_part = weight_blocks(after(order, up_grad), grad, activated, context, *sums)
    done = hidden_sum.send_middle(down_part)
    down = DataSum(down_part, done)
    up_part = weight_blocks(after(order, done), hidden, up_grad, qkv_grad)
    done = hidden_sum.send_near(up_part)
    up = DataSum(up_part, done)
    rows = input_rows(
        after(places, done), hidden_sum.terms(), tokens, cotangent, stats, ln_gain
    )
    input_grad = TensorGather(places, rows)
    done = input_grad.second((rows, branch_sum))
    down.send(done)
    up.send(down.near)
    output = finish_output(after(seq_lengths, up.near), tokens, branch_sum, b_dense, b_fc2)
    done = input_grad.third(output)
    input_grad.three = after(input_grad.three, done)
    grad_fc2, grad_dense, small = down.finish(
        down_kernel,
        "down",
        ((units, BLOCK), (w_dense.shape[0], BLOCK), (8, BLOCK)),
        input_grad.three[0],
    )
    norm_sum = small[:2] + across(small[:2])
    grad_fc1, grad_qkv = up.finish(
        up_kernel, "up", ((BLOCK, units), (BLOCK, w_qkv.shape[1])), small
    )
    norm_sum = norm_sum + y_up(norm_sum) + y_down(norm_sum) + shift(norm_sum, "y", 4, 2)
    input_grad = input_grad.finish(grad_qkv)
    out_bias = small[2]
    return (
        output,
        input_grad,
        norm_sum[0],
        norm_sum[1],
        grad_qkv,
        small[3, :48],
        grad_dense,
        out_bias,
        grad_fc1,
        small[4, :64],
        grad_fc2,
        out_bias,
    )


def solution(mesh):
    parts = Mesh(mesh.devices.reshape(2, 4, 2, 2, 4), DP + TENSOR)
    rows = P(DP, None)
    placed = (
        rows,
        rows,
        rows,
        P(),
        P(),
        P(None, TENSOR),
        P(TENSOR),
        P(TENSOR, None),
        P(),
        P(None, TENSOR),
        P(TENSOR),
        P(TENSOR, None),
        P(),
    )
    return jax.shard_map(
        per_device,
        mesh=parts,
        in_specs=placed,
        out_specs=(
            rows,
            rows,
            P(DP),
            P(DP),
            P(DP, TENSOR),
            P(TENSOR + DP),
            P(TENSOR, DP),
            P(DP),
            P(DP, TENSOR),
            P(TENSOR + DP),
            P(TENSOR, DP),
            P(DP),
        ),
        check_vma=False,
    )
```

```python
import functools

import jax
import jax.numpy as jnp
from jax import lax
from jax.experimental import pallas as pl
from jax.experimental.pallas import tpu as pltpu
from jax.sharding import Mesh
from jax.sharding import PartitionSpec as P

HEAD_DIM = 64
ROTARY = 32
DP = ("zh", "x", "core")
TENSOR = ("zl", "y")
BF16 = jnp.bfloat16
F32 = jnp.float32
ROWS = 256
QUERIES = 512
BLOCK = 128
AT_ONCE = 4
VMEM_BYTES = 56 * 2**20
GELU = 0.7978845608


def dot(left, right, left_dim, right_dim):
    return lax.dot_general(
        left, right, (((left_dim,), (right_dim,)), ((), ())), preferred_element_type=F32
    )


def kernel_call(kernel, name, out_shape, prefetch=0, vmem=VMEM_BYTES, flops=1, **spec):
    if prefetch:
        spec = {
            "grid_spec": pltpu.PrefetchScalarGridSpec(
                num_scalar_prefetch=prefetch,
                grid=spec.pop("grid"),
                in_specs=spec.pop("in_specs"),
                out_specs=spec.pop("out_specs"),
                scratch_shapes=spec.pop("scratch_shapes", ()),
            ),
            **spec,
        }
    return pl.pallas_call(
        kernel,
        out_shape=out_shape,
        compiler_params=pltpu.CompilerParams(vmem_limit_bytes=vmem),
        cost_estimate=pl.CostEstimate(flops=flops, bytes_accessed=1, transcendentals=0),
        name=name,
        **spec,
    )


def made(rows, columns, kind=BF16):
    return jax.ShapeDtypeStruct((rows, columns), kind)


def kept(array):
    return pl.BlockSpec(array.shape, lambda *_: (0,) * array.ndim)


AWAY = pl.BlockSpec(memory_space=pltpu.HBM)
NEAR = pl.BlockSpec(memory_space=pltpu.VMEM)
SCALARS = pl.BlockSpec(memory_space=pltpu.SMEM)


def ends_of(lengths_ref):
    ends = [lengths_ref[0, 0]]
    for place in range(1, lengths_ref.shape[1]):
        ends.append(ends[-1] + lengths_ref[0, place])
    return ends


def starts_at(ends, places):
    start = jnp.zeros_like(places)
    for end in ends:
        start = jnp.maximum(start, jnp.where(places >= end, end, 0))
    return start


def turned_halves(columns):
    lane = lax.broadcasted_iota(jnp.int32, columns.shape, 1)
    return jnp.where(
        lane % ROTARY < ROTARY // 2, pltpu.roll(columns, 112, 1), pltpu.roll(columns, 16, 1)
    )


def span(part, size, first=0):
    at = part * size + first
    return pl.ds(at if isinstance(at, int) else pl.multiple_of(at, BLOCK if size % BLOCK == 0 else size), size)


class Copies:
    def __init__(self, sems):
        self.sems, self.made = sems, {}

    def start(self, name, source, target):
        copy = pltpu.make_async_copy(source, target, self.sems.at[len(self.made)])
        self.made[name] = copy
        copy.start()

    def numbered(self, names, count):
        first = len(self.made)
        for at in range(len(names) * count):
            self.made[("kept", first + at)] = None
        return {name: first + at * count for at, name in enumerate(names)}

    def at(self, source, target, number):
        return pltpu.make_async_copy(source, target, self.sems.at[number])

    def wait(self, *names):
        for name in names:
            self.made[name].wait()


OFFSETS = tuple((planes, places) for planes in range(2) for places in range(4))
FAR = (1, 2)
CUTS = (0, 48, 96, 128)
PARTS = tuple(zip(CUTS, CUTS[1:]))
BLOCK_NAMES = tuple(o for o in OFFSETS if o != FAR) + (0, 1, 2)


def block_shapes(width):
    return [made(BLOCK, width)] * 7 + [made(high - low, width) for low, high in PARTS]


def block_copy(copies, place_ref_of, which, total, ref, columns, number):
    name = BLOCK_NAMES[which]
    low, high = PARTS[name] if isinstance(name, int) else (0, BLOCK)
    place = place_ref_of[OFFSETS.index(FAR if isinstance(name, int) else name)]
    first = pl.multiple_of(place * BLOCK, BLOCK) + low
    return copies.at(
        total.at[pl.ds(first, high - low), columns], ref.at[:, columns], number
    )


def each_block_copy(copies, places_ref, total, refs, parts, size, first, do):
    for part in parts:
        columns = span(part, size)
        for which, ref in enumerate(refs):
            number = first + part * len(refs) + which
            do(block_copy(copies, places_ref, which, total, ref, columns, number))


def start(copy):
    copy.start()


def wait(copy):
    copy.wait()


def forward_kernel(
    lengths_ref,
    freq_ref,
    gain_ref,
    bias_ref,
    b_qkv_ref,
    b_fc1_ref,
    tokens_hbm,
    cot_hbm,
    w_qkv_hbm,
    w_fc1_hbm,
    w_dense_hbm,
    w_fc2_hbm,
    hidden_hbm,
    grad_hbm,
    act_hbm,
    slope_hbm,
    ctx_hbm,
    qkv_grad_hbm,
    stats_hbm,
    branch_hbm,
    tokens,
    grad,
    hidden,
    w_qkv,
    w_fc1,
    w_dense,
    w_fc2,
    qkv,
    act,
    slope,
    ctx_grad,
    ctx,
    qkv_grad,
    cosines,
    sines,
    stats,
    turn_sum,
    value_sum,
    both_ctx,
    both_grad,
    sems,
):
    slot_len, width = tokens.shape
    blocks = slot_len // ROWS
    copies = Copies(sems)
    ends = ends_of(lengths_ref)
    row_copies = {
        "tokens": (tokens_hbm, tokens),
        "cot": (cot_hbm, grad),
        "hidden": (hidden, hidden_hbm),
        "grad": (grad, grad_hbm),
        "act": (act, act_hbm),
        "slope": (slope, slope_hbm),
    }
    numbers = copies.numbered(tuple(row_copies), blocks)
    parts, size = 4, width // 4
    first_branch = copies.numbered(("branch",), parts)["branch"]
    w_fc2_number = copies.numbered(("w_fc2",), 1)["w_fc2"]

    def rows_at(block, part=0, height=ROWS):
        return span(part, height, block * ROWS)

    def row_copy(name, block):
        source, target = row_copies[name]
        at = rows_at(block)
        return copies.at(source.at[at, :], target.at[at, :], numbers[name] + block)

    def normalise(block, part, height):
        at = rows_at(block, part, height)
        places = block * ROWS + part * height
        places = places + lax.broadcasted_iota(jnp.int32, (height, 128), 0)
        lane = lax.broadcasted_iota(jnp.int32, (height, 128), 1)
        position = (places - starts_at(ends, places)).astype(F32)
        angle = position * freq_ref[...]
        cosines[at, :] = jnp.where(lane % HEAD_DIM < ROTARY, jnp.cos(angle), 1.0)
        sine = jnp.sin(angle)
        sines[at, :] = jnp.where(
            lane % HEAD_DIM < ROTARY // 2, -sine, jnp.where(lane % HEAD_DIM < ROTARY, sine, 0.0)
        )
        valid = (places < ends[-1])[:, :1]
        inputs = tokens[at, :].astype(F32)
        mean = jnp.mean(inputs, axis=1, keepdims=True)
        center = inputs - mean
        inv_sigma = lax.rsqrt(jnp.mean(center * center, axis=1, keepdims=True) + 1e-05)
        stats[at, :] = jnp.where(lane == 0, mean, inv_sigma)
        hidden[at, :] = (
            center * inv_sigma * gain_ref[...].astype(F32)[None]
            + bias_ref[...].astype(F32)[None]
        ).astype(BF16)
        grad[at, :] = jnp.where(valid, grad[at, :], jnp.zeros((height, width), BF16))

    def turn(at, projected):
        lane = lax.broadcasted_iota(jnp.int32, (ROWS, 128), 1)
        cosine, sine = cosines[at, :], sines[at, :]
        for block in range(qkv.shape[1] // 128):
            columns = slice(block * 128, block * 128 + 128)
            plain = projected[:, columns]
            turned = plain * cosine + turned_halves(plain) * sine
            if block % 3 == 1:
                turned = jnp.where(lane < HEAD_DIM, plain, turned)
            if block % 3 == 2:
                turned = jnp.where(lane < HEAD_DIM, turned, plain)
            qkv[at, columns] = turned.astype(BF16)

    def activate(at, up, columns):
        square = up * up
        share = 0.5 * jnp.tanh(up * (GELU + (GELU * 0.044715) * square)) + 0.5
        active = up * share
        act[at, columns] = active.astype(BF16)
        slope[at, columns] = (
            share + active * (1.0 - share) * (2 * GELU + (6 * GELU * 0.044715) * square)
        ).astype(BF16)

    def attend(pair, head):
        heads = pl.ds(pl.multiple_of(pair * 6 * HEAD_DIM, 6 * HEAD_DIM), 6 * HEAD_DIM)
        wide = pl.ds(pl.multiple_of(pair * 2 * HEAD_DIM, 2 * HEAD_DIM), 2 * HEAD_DIM)
        at = 3 * HEAD_DIM * head
        mine = slice(HEAD_DIM * head, HEAD_DIM * head + HEAD_DIM)
        all_heads = qkv[:, heads]
        for block in reversed(range(slot_len // QUERIES)):
            rows = slice(block * QUERIES, block * QUERIES + QUERIES)
            reach = (block + 1) * QUERIES
            query = all_heads[rows, at : at + 64] * BF16(HEAD_DIM**-0.5)
            key = all_heads[0:reach, at + 64 : at + 128]
            value = all_heads[0:reach, at + 128 : at + 192]
            upstream = ctx_grad[rows, wide][:, mine]
            scores = dot(key, query, 1, 1)
            place = block * QUERIES + lax.broadcasted_iota(jnp.int32, (1, QUERIES), 1)
            begin = starts_at(ends, place)
            key_place = lax.broadcasted_iota(jnp.int32, (reach, QUERIES), 0)
            scores = jnp.where((key_place >= begin) & (key_place <= place), scores, -1e30)
            raised = jnp.exp(scores - jnp.max(scores, axis=0, keepdims=True))
            prob = raised * (1.0 / jnp.sum(raised, axis=0, keepdims=True))
            prob_low = prob.astype(BF16)
            context = dot(value, prob_low, 0, 0)
            prob_grad = dot(value, upstream, 1, 1)
            row_dot = jnp.sum(prob_grad * prob, axis=0, keepdims=True)
            score_grad = (prob * (prob_grad - row_dot)).astype(BF16)
            query_grad = dot(key, score_grad, 0, 0)
            value_part = dot(prob_low, upstream, 1, 0)
            key_part = dot(score_grad, query, 1, 0)
            if reach == slot_len:
                value_sum[...] = value_part
                turn_sum[:, 64:128] = key_part
            else:
                value_sum[0:reach] += value_part
                turn_sum[0:reach, 64:128] += key_part
            turn_sum[rows, 0:64] = query_grad.T * HEAD_DIM**-0.5
            both_ctx[rows, mine] = context.T.astype(BF16)
        both = turn_sum[...]
        both = both * cosines[...] - turned_halves(both) * sines[...]
        both_grad[:, at : at + 128] = both.astype(BF16)
        both_grad[:, at + 128 : at + 192] = value_sum[...].astype(BF16)
        if head:
            ctx[:, wide] = both_ctx[...]
            qkv_grad[:, heads] = both_grad[...]

    def last_weights():
        return copies.at(w_fc2_hbm, w_fc2, w_fc2_number)

    def branch_copy(part):
        columns = span(part, size)
        return copies.at(
            tokens.at[:, columns], branch_hbm.at[:, columns], first_branch + part
        )

    for name in ("tokens", "cot"):
        row_copy(name, 0).start()
    copies.start("w_qkv", w_qkv_hbm, w_qkv)
    for name in ("tokens", "cot"):
        row_copy(name, 1).start()
    copies.start("w_fc1", w_fc1_hbm, w_fc1)
    copies.start("w_dense", w_dense_hbm, w_dense)

    def one_block(block, ready):
        for name in ("tokens", "cot"):
            row_copy(name, block).wait()
        for part in range(4):
            normalise(block, part, ROWS // 4)
        for name in ("hidden", "grad"):
            row_copy(name, block).start()
        ready("w_qkv")
        at = rows_at(block)
        turn(at, dot(hidden[at, :], w_qkv[...], 1, 0) + b_qkv_ref[...].astype(F32)[None])
        ready("w_fc1", "w_dense")
        half = w_fc1.shape[1] // 2
        for part in range(2):
            columns = slice(part * half, part * half + half)
            up = dot(hidden[at, :], w_fc1[:, columns], 1, 0)
            activate(at, up + b_fc1_ref[columns].astype(F32)[None], columns)
        ctx_grad[at, :] = dot(grad[at, :], w_dense[...], 1, 1).astype(BF16)
        for name in ("act", "slope"):
            row_copy(name, block).start()

    for later in range(2, blocks):
        for name in ("tokens", "cot"):
            row_copy(name, later).start()
    last_weights().start()
    one_block(0, copies.wait)

    @pl.loop(1, blocks)
    def _(block):
        one_block(block, lambda *names: None)

    copies.start("stats", stats, stats_hbm)

    @pl.loop(0, ctx.shape[1] // (2 * HEAD_DIM))
    def _(pair):
        for head in range(2):
            attend(pair, head)

    copies.start("ctx", ctx, ctx_hbm)
    copies.start("qkv_grad", qkv_grad, qkv_grad_hbm)
    last_weights().wait()

    @pl.loop(0, parts)
    def _(part):
        columns = span(part, size)
        tokens[:, columns] = (
            dot(ctx[...], w_dense[:, columns], 1, 0) + dot(act[...], w_fc2[:, columns], 1, 0)
        ).astype(BF16)
        branch_copy(part).start()

    for name in ("hidden", "grad", "act", "slope"):
        for block in range(blocks):
            row_copy(name, block).wait()
    copies.wait("stats", "ctx", "qkv_grad")
    for part in range(parts):
        branch_copy(part).wait()


def forward(lengths, freq, tokens, cot, gain, bias, b_qkv, b_fc1, w_qkv, w_fc1, w_dense, w_fc2):
    slot_len, width = tokens.shape
    units, heads, ctx_width = w_fc2.shape[0], w_qkv.shape[1], w_dense.shape[0]
    row_kinds = (width, width, units, units, ctx_width, heads)

    def room(rows, columns, kind=BF16):
        return pltpu.VMEM((rows, columns), kind)

    return kernel_call(
        forward_kernel,
        "forward",
        [made(slot_len, columns) for columns in row_kinds]
        + [made(slot_len, 128, F32), made(slot_len, width)],
        grid=(1,),
        in_specs=[SCALARS] + [kept(a) for a in (freq, gain, bias, b_qkv, b_fc1)] + [AWAY] * 6,
        out_specs=[AWAY] * 8,
        scratch_shapes=[room(slot_len, width)] * 3
        + [pltpu.VMEM(w.shape, BF16) for w in (w_qkv, w_fc1, w_dense, w_fc2)]
        + [
            room(slot_len, heads),
            room(slot_len, units),
            room(slot_len, units),
            room(slot_len, ctx_width),
            room(slot_len, ctx_width),
            room(slot_len, heads),
        ]
        + [room(slot_len, 128, F32)] * 4
        + [
            room(slot_len, HEAD_DIM, F32),
            room(slot_len, 2 * HEAD_DIM),
            room(slot_len, 6 * HEAD_DIM),
            pltpu.SemaphoreType.DMA((80,)),
        ],
    )(lengths, freq, gain, bias, b_qkv, b_fc1, tokens, cot, w_qkv, w_fc1, w_dense, w_fc2)


def backward_kernel(
    places_ref,
    grad_hbm,
    slope_hbm,
    qkv_grad_hbm,
    tokens_hbm,
    stats_hbm,
    w_fc2_hbm,
    w_fc1_hbm,
    w_qkv_hbm,
    norm_sum_ref,
    grad_sum_ref,
    head_sum_ref,
    unit_sum_ref,
    up_grad_hbm,
    *rest,
):
    blocks, scratch = rest[: len(BLOCK_NAMES)], rest[len(BLOCK_NAMES) :]
    grad, slope, qkv_grad, tokens, stats, w_fc2, w_fc1, w_qkv, *scratch = scratch
    up_grad, hidden, gain_sum, shift_sum, grad_sum, head_sum, unit_sum, sems = scratch
    copies = Copies(sems)
    slot_len, width = grad.shape
    units, size = w_fc2.shape[0], 512

    def part_of(part):
        return span(part, size)

    def bring_rows(name, part, source, target):
        at = part_of(part)
        copies.start((name, part), source.at[at, :], target.at[at, :])

    def add_to(ref, columns, array):
        ref[:, columns] += jnp.sum(array, axis=0, keepdims=True)

    def to_units(rows, part):
        at, columns = part_of(rows), part_of(part)
        up = dot(grad[at, :], w_fc2[columns, :], 1, 1) * slope[at, columns].astype(F32)
        up = up.astype(BF16)
        up_grad[at, columns] = up
        add_to(unit_sum, columns, up.astype(F32))

    def to_hidden(rows, part):
        at, columns = part_of(rows), part_of(part)
        result = dot(up_grad[at, :], w_fc1[columns, :], 1, 1) + dot(
            qkv_grad[at, :], w_qkv[columns, :], 1, 1
        )
        hidden[at, columns] = result.astype(BF16)
        normed = (tokens[at, columns].astype(F32) - stats[at, 0:1]) * stats[at, 1:2]
        add_to(gain_sum, columns, result * normed)
        add_to(shift_sum, columns, result)

    parts = width // size
    first_block = copies.numbered(("blocks",), parts * len(blocks))["blocks"]

    def blocks_of(which, do):
        each_block_copy(copies, places_ref, hidden, blocks, which, size, first_block, do)

    for part in range(2):
        bring_rows("grad", part, grad_hbm, grad)
        bring_rows("slope", part, slope_hbm, slope)
        bring_rows("w_fc2", part, w_fc2_hbm, w_fc2)
    for total in (gain_sum, shift_sum, grad_sum, head_sum, unit_sum):
        total[...] = jnp.zeros_like(total)
    copies.wait(("w_fc2", 0), ("grad", 0), ("slope", 0))
    copies.start("w_fc1", w_fc1_hbm, w_fc1)
    copies.start("w_qkv", w_qkv_hbm, w_qkv)
    copies.start("qkv_grad", qkv_grad_hbm, qkv_grad)
    copies.start("tokens", tokens_hbm, tokens)
    copies.start("stats", stats_hbm, stats)

    @pl.loop(0, 4)
    def _(turn):
        rows, part = turn // 2, turn % 2

        @pl.when(turn == 1)
        def _():
            copies.wait(("w_fc2", 1))

        @pl.when(turn == 2)
        def _():
            copies.wait(("grad", 1), ("slope", 1))

        to_units(rows, part)

        @pl.when(part == 0)
        def _():
            add_to(grad_sum, slice(0, width), grad[part_of(rows), :].astype(F32))

    copies.start("up_grad", up_grad, up_grad_hbm)
    copies.wait("w_fc1", "w_qkv", "qkv_grad", "tokens", "stats")
    add_to(head_sum, slice(0, qkv_grad.shape[1]), qkv_grad[...].astype(F32))

    @pl.loop(0, parts)
    def _(part):
        for rows in range(slot_len // size):
            to_hidden(rows, part)
        blocks_of((part,), start)

    for ref, first, total in (
        (norm_sum_ref, 0, gain_sum),
        (norm_sum_ref, 16, shift_sum),
        (grad_sum_ref, 0, grad_sum),
        (head_sum_ref, 0, head_sum),
        (unit_sum_ref, 0, unit_sum),
    ):
        share = total.shape[1] // 16
        if share < BLOCK:
            ref[...] = jnp.zeros_like(ref)
        for row in range(16):
            ref[first + row : first + row + 1, 0:share] = total[:, row * share : row * share + share]
    copies.wait("up_grad")
    blocks_of(range(parts), wait)


def backward(places, grad, slope, qkv_grad, tokens, stats, w_fc2, w_fc1, w_qkv):
    slot_len, width = tokens.shape
    units, heads = w_fc2.shape[0], w_qkv.shape[1]
    sizes = (width, width, width, heads, units)
    sums = [made(rows, BLOCK, F32) for rows in (32, 16, 16, 16)]
    arrays = (grad, slope, qkv_grad, tokens, stats, w_fc2, w_fc1, w_qkv)
    norm_sum, grad_sum, head_sum, unit_sum, up_grad, *blocks = kernel_call(
        backward_kernel,
        "backward",
        sums + [made(slot_len, units)] + block_shapes(width),
        grid=(1,),
        in_specs=[SCALARS] + [AWAY] * len(arrays),
        out_specs=[kept(array) for array in sums] + [AWAY] * (1 + len(BLOCK_NAMES)),
        scratch_shapes=[pltpu.VMEM(array.shape, array.dtype) for array in arrays]
        + [pltpu.VMEM((slot_len, units), BF16), pltpu.VMEM((slot_len, width), BF16)]
        + [pltpu.VMEM((1, size), F32) for size in sizes]
        + [pltpu.SemaphoreType.DMA((64,))],
    )(places, *arrays)
    sums = (norm_sum, grad_sum, head_sum, unit_sum)
    return up_grad, sums, dict(zip(BLOCK_NAMES, blocks))


def weight_kernel(order_ref, *refs):
    lefts, (first_ref, second_ref, *sums, out_ref) = refs[:AT_ONCE], refs[AT_ONCE:]
    cut, end = first_ref.shape[1], first_ref.shape[1] + second_ref.shape[1]
    left = jnp.concatenate([ref[...] for ref in lefts], axis=1)
    out_ref[:, 0:cut] = dot(left, first_ref[...], 0, 0).astype(BF16)
    out_ref[:, cut:end] = dot(left, second_ref[...], 0, 0).astype(BF16)
    if sums:
        for half in range(AT_ONCE):
            block = order_ref[AT_ONCE * pl.program_id(0) + half]
            lines = [
                ref[pl.ds(first + block, 1), :]
                for ref in sums
                for first in range(0, ref.shape[0], 16)
            ]
            lines.append(jnp.zeros((BLOCK - len(lines), BLOCK), F32))
            columns = jnp.concatenate(lines, axis=0).T
            out_ref[half * BLOCK : half * BLOCK + BLOCK, end:] = columns.astype(BF16)


def weight_blocks(order, left, first, second, *sums):
    slot_len = left.shape[0]
    width = first.shape[1] + second.shape[1] + (BLOCK if sums else 0)
    return kernel_call(
        weight_kernel,
        "weights",
        made(left.shape[1], width),
        prefetch=1,
        grid=(left.shape[1] // (AT_ONCE * BLOCK),),
        in_specs=[
            *[
                pl.BlockSpec(
                    (slot_len, BLOCK),
                    functools.partial(lambda at, i, order: (0, order[AT_ONCE * i + at]), at),
                )
                for at in range(AT_ONCE)
            ],
            kept(first),
            kept(second),
            *[kept(array) for array in sums],
        ],
        out_specs=pl.BlockSpec((AT_ONCE * BLOCK, width), lambda i, order: (i, 0)),
    )(order, *[left] * AT_ONCE, first, second, *sums)


def combine(name, *sums):
    arrays = [term[0] for terms in sums for term in terms]
    specs = [
        pl.BlockSpec((term[1], term[0].shape[1]), functools.partial(lambda at, _: (at, 0), term[2]))
        for terms in sums
        for term in terms
    ]
    heights = [max(term[4] for term in terms) for terms in sums]

    def kernel(*refs):
        ins, outs = list(refs[: len(arrays)]), refs[len(arrays) :]
        for terms, height, out in zip(sums, heights, outs):
            mine = [(ins.pop(0), term[3], term[4]) for term in terms]
            cuts = sorted({cut for _, low, high in mine for cut in (low, high)})
            for low, high in zip(cuts, cuts[1:]):
                parts = [
                    ref[low - first : high - first, :].astype(F32)
                    for ref, first, last in mine
                    if first <= low and high <= last
                ]
                out[low:high, :] = functools.reduce(lambda a, b: a + b, parts).astype(BF16)

    shapes = [made(height, terms[0][0].shape[1]) for height, terms in zip(heights, sums)]
    return kernel_call(
        kernel,
        name,
        shapes,
        grid=(1,),
        in_specs=specs,
        out_specs=[pl.BlockSpec(shape.shape, lambda _: (0, 0)) for shape in shapes],
    )(*arrays)


def whole_term(array, low=0):
    return (array, array.shape[0], 0, low, low + array.shape[0])


def output_kernel(lengths_ref, tokens_ref, branch_ref, b_dense_ref, b_fc2_ref, out_ref):
    bias = b_dense_ref[...].astype(F32) + b_fc2_ref[...].astype(F32)
    rows = tokens_ref.shape[0]
    place = pl.program_id(0) * rows + lax.broadcasted_iota(jnp.int32, (rows, 1), 0)
    total = jnp.where(
        place < ends_of(lengths_ref)[-1], branch_ref[...].astype(F32) + bias[None], 0.0
    )
    out_ref[...] = (tokens_ref[...].astype(F32) + total).astype(BF16)


def finish_output(lengths, tokens, branch_sum, b_dense, b_fc2):
    slot_len, width = tokens.shape
    row = pl.BlockSpec((ROWS, width), lambda i: (i, 0))
    return kernel_call(
        output_kernel,
        "output",
        made(slot_len, width),
        grid=(slot_len // ROWS,),
        in_specs=[SCALARS, row, row, kept(b_dense), kept(b_fc2)],
        out_specs=row,
    )(lengths, tokens, branch_sum, b_dense, b_fc2)


def input_kernel(places_ref, *refs):
    *terms, tokens_ref, cot_ref, stats_ref, gain_ref, out_ref = refs
    total = functools.reduce(lambda a, b: a + b, [t[...].astype(F32) for t in terms])
    inv_sigma = stats_ref[:, 1:2]
    normed = (tokens_ref[...].astype(F32) - stats_ref[:, 0:1]) * inv_sigma
    scaled = total * gain_ref[...].astype(F32)[None]
    out_ref[...] = (
        cot_ref[...].astype(F32)
        + inv_sigma
        * (
            scaled
            - jnp.mean(scaled, axis=1, keepdims=True)
            - normed * jnp.mean(scaled * normed, axis=1, keepdims=True)
        )
    ).astype(BF16)


def input_rows(places, terms, tokens, cot, stats, gain):
    width = tokens.shape[1]

    def mine(columns):
        return pl.BlockSpec((BLOCK, columns), lambda i, places: (places[0], 0))

    return kernel_call(
        input_kernel,
        "input",
        made(BLOCK, width),
        prefetch=1,
        grid=(1,),
        in_specs=[kept(t) for t in terms] + [mine(width), mine(width), mine(128), kept(gain)],
        out_specs=pl.BlockSpec((BLOCK, width), lambda *_: (0, 0)),
    )(places, *terms, tokens, cot, stats, gain)


def place_kernel(blocks, places_ref, *refs):
    pieces, out_ref, sems = refs[: len(blocks)], refs[-2], refs[-1]
    copies = []
    for i, ((offset, low, high), piece) in enumerate(zip(blocks, pieces)):
        first = pl.multiple_of(places_ref[OFFSETS.index(offset)] * BLOCK, BLOCK)
        copies.append(
            pltpu.make_async_copy(
                piece, out_ref.at[pl.ds(first + low, high - low), :], sems.at[i]
            )
        )
    for copy in copies:
        copy.start()
    for copy in copies:
        copy.wait()


def place_rows(places, blocks, pieces, whole=None):
    rest = {} if whole is None else {"input_output_aliases": {len(pieces) + 1: 0}}
    given = [] if whole is None else [whole]
    return kernel_call(
        functools.partial(place_kernel, blocks),
        "place",
        made(8 * BLOCK, pieces[0].shape[1]),
        in_specs=[SCALARS] + [NEAR] * len(pieces) + [AWAY] * len(given),
        out_specs=AWAY,
        scratch_shapes=[pltpu.SemaphoreType.DMA((len(pieces),))],
        **rest,
    )(places, *pieces, *given)


def up_kernel(near_ref, far_ref, first_ref, second_ref):
    total = near_ref[...].astype(F32) + far_ref[...].astype(F32)
    cut = first_ref.shape[1]
    first_ref[...] = total[:, :cut]
    second_ref[...] = total[:, cut:]


def down_kernel(near_ref, far_ref, first_ref, second_ref, sums_ref):
    total = near_ref[...].astype(F32) + far_ref[...].astype(F32)
    cut, end = first_ref.shape[0], first_ref.shape[0] + second_ref.shape[0]
    first_ref[...] = total[:, :cut].T
    second_ref[...] = total[:, cut:end].T
    sums_ref[...] = total[:, end:].T[: sums_ref.shape[0]]


def last_sum(kernel, name, shapes, near, far):
    return kernel_call(
        kernel,
        name,
        [made(*shape, F32) for shape in shapes],
        grid=(1,),
        in_specs=[pl.BlockSpec(far.shape, lambda _: (0, 0))] * 2,
        out_specs=[pl.BlockSpec(shape, lambda _: (0, 0)) for shape in shapes],
    )(near, far)


def shift(array, axis, size, by):
    return lax.ppermute(array, axis, [(i, (i + by) % size) for i in range(size)])


def y_up(array):
    return shift(array, "y", 4, 1)


def y_down(array):
    return shift(array, "y", 4, 3)


def across(array):
    return shift(array, "zl", 2, 1)


def after(arrays, *earlier):
    return lax.optimization_barrier((arrays, earlier))[0]


class TensorSum:
    def __init__(self, blocks):
        self.blocks = blocks

    def send_far(self):
        b = self.blocks
        self.far = across(b[0]), y_up(b[1]), y_down(b[2])

    def send_middle(self, earlier):
        b = self.blocks
        far = *self.far[:2], after(self.far[2], earlier)
        sent = combine(
            "middle",
            *[
                [whole_term(b[offset]), whole_term(part, low)]
                for offset, part, (low, _) in zip(((0, 2), (1, 1), (1, 3)), far, PARTS)
            ],
        )
        self.middle = y_up(sent[0]), across(sent[1]), y_down(sent[2])
        return sent

    def send_near(self, earlier):
        b = self.blocks
        two_on, diagonal, other = self.middle
        other = after(other, earlier)
        sent = combine(
            "near",
            [whole_term(b[(0, 1)]), whole_term(two_on), whole_term(diagonal)],
            [whole_term(b[(1, 0)]), whole_term(other)],
        )
        self.near = [y_up(sent[0]), across(sent[1]), y_down(after(b[(0, 3)], sent))]
        return sent

    def terms(self):
        return [self.blocks[(0, 0)], *self.near]


class TensorGather:
    def __init__(self, places, rows):
        self.places, self.rows = places, rows
        self.one = y_up(rows), y_down(rows), across(rows)

    def second(self, earlier):
        before, ahead, partner = self.one = after(self.one, earlier)
        self.two = y_down(ahead), across(ahead), y_up(partner)
        return self.one

    def third(self, earlier):
        two_on, diagonal, other = self.two = after(self.two, earlier)
        (a, b), (c, d), (e, f) = PARTS
        self.three = across(two_on[a:b]), y_down(diagonal[c:d]), y_up(other[e:f])
        blocks = [(0, 0), (0, 3), (0, 1), (1, 0), (0, 2), (1, 1), (1, 3)]
        self.whole = place_rows(
            self.places,
            [(offset, 0, BLOCK) for offset in blocks],
            [self.rows, *self.one, *self.two],
        )
        return self.whole

    def finish(self, earlier):
        parts = after(self.three, earlier)
        return place_rows(
            self.places, [(FAR, low, high) for low, high in PARTS], list(parts), self.whole
        )


class DataSum:
    def __init__(self, partial_sums, earlier):
        self.near = lax.psum_scatter(
            after(partial_sums, earlier), ("x", "core"), scatter_dimension=0, tiled=True
        )

    def send(self, earlier):
        self.near = after(self.near, earlier)
        self.far = shift(self.near[BLOCK:], "zh", 2, 1)

    def finish(self, kernel, name, shapes, earlier):
        return last_sum(kernel, name, shapes, self.near, after(self.far, earlier))


def dp_order():
    half = lax.axis_index("zh")
    return jnp.stack(
        [(half + part) % 2 * 8 + block for block in range(8) for part in range(2)]
    ).astype(jnp.int32)


def per_device(
    tokens,
    cotangent,
    seq_lengths,
    ln_gain,
    ln_bias,
    w_qkv,
    b_qkv,
    w_dense,
    b_dense,
    w_fc1,
    b_fc1,
    w_fc2,
    b_fc2,
):
    units = w_fc2.shape[0]
    plane, place = lax.axis_index("zl"), lax.axis_index("y")
    places = jnp.stack(
        [(plane + planes) % 2 * 4 + (place + steps) % 4 for planes, steps in OFFSETS]
    ).astype(jnp.int32)
    order = dp_order()
    frequency = 10000.0 ** (-jnp.arange(ROTARY // 2, dtype=F32) * 2.0 / ROTARY)
    frequency = jnp.tile(frequency, 8)[None]
    hidden, grad, activated, slope, context, qkv_grad, stats, branch_part = forward(
        seq_lengths,
        frequency,
        tokens,
        cotangent,
        ln_gain,
        ln_bias,
        b_qkv,
        b_fc1,
        w_qkv,
        w_fc1,
        w_dense,
        w_fc2,
    )
    branch_sum = lax.psum(branch_part, TENSOR)
    up_grad, sums, blocks = backward(
        after(places, branch_part), grad, slope, qkv_grad, tokens, stats, w_fc2, w_fc1, w_qkv
    )
    hidden_sum = TensorSum(blocks)
    hidden_sum.send_far()
    down_part = weight_blocks(after(order, up_grad), grad, activated, context, *sums)
    done = hidden_sum.send_middle(down_part)
    down = DataSum(down_part, done)
    up_part = weight_blocks(after(order, done), hidden, up_grad, qkv_grad)
    done = hidden_sum.send_near(up_part)
    up = DataSum(up_part, done)
    rows = input_rows(
        after(places, done), hidden_sum.terms(), tokens, cotangent, stats, ln_gain
    )
    input_grad = TensorGather(places, rows)
    down.send((rows, branch_sum))
    done = input_grad.second(down.near)
    grad_fc2, grad_dense, small = down.finish(
        down_kernel,
        "down",
        ((units, BLOCK), (w_dense.shape[0], BLOCK), (8, BLOCK)),
        done,
    )
    norm_sum = small[:2]
    norm_across = across(norm_sum)
    output = finish_output(after(seq_lengths, small), tokens, branch_sum, b_dense, b_fc2)
    up.send(output)
    input_grad.third((output, up.near))
    *three, up.far = after([*input_grad.three, up.far], input_grad.whole)
    input_grad.three = three
    norm_sum = norm_sum + after(norm_across, three[0])
    grad_fc1, grad_qkv = up.finish(
        up_kernel, "up", ((BLOCK, units), (BLOCK, w_qkv.shape[1])), input_grad.three[0]
    )
    norm_sum = norm_sum + y_up(norm_sum) + y_down(norm_sum) + shift(norm_sum, "y", 4, 2)
    input_grad = input_grad.finish(grad_qkv)
    out_bias = small[2]
    return (
        output,
        input_grad,
        norm_sum[0],
        norm_sum[1],
        grad_qkv,
        small[3, :48],
        grad_dense,
        out_bias,
        grad_fc1,
        small[4, :64],
        grad_fc2,
        out_bias,
    )


def solution(mesh):
    parts = Mesh(mesh.devices.reshape(2, 4, 2, 2, 4), DP + TENSOR)
    rows = P(DP, None)
    placed = (
        rows,
        rows,
        rows,
        P(),
        P(),
        P(None, TENSOR),
        P(TENSOR),
        P(TENSOR, None),
        P(),
        P(None, TENSOR),
        P(TENSOR),
        P(TENSOR, None),
        P(),
    )
    return jax.shard_map(
        per_device,
        mesh=parts,
        in_specs=placed,
        out_specs=(
            rows,
            rows,
            P(DP),
            P(DP),
            P(DP, TENSOR),
            P(TENSOR + DP),
            P(TENSOR, DP),
            P(DP),
            P(DP, TENSOR),
            P(TENSOR + DP),
            P(TENSOR, DP),
            P(DP),
        ),
        check_vma=False,
    )
```

```python
import functools

import jax
import jax.numpy as jnp
from jax import lax
from jax.experimental import pallas as pl
from jax.experimental.pallas import tpu as pltpu
from jax.sharding import Mesh
from jax.sharding import PartitionSpec as P

HEAD_DIM = 64
ROTARY = 32
DP = ("zh", "x", "core")
TENSOR = ("zl", "y")
BF16 = jnp.bfloat16
F32 = jnp.float32
ROWS = 256
QUERIES = 512
BLOCK = 128
AT_ONCE = 4
VMEM_BYTES = 56 * 2**20
GELU = 0.7978845608


def dot(left, right, left_dim, right_dim):
    return lax.dot_general(
        left, right, (((left_dim,), (right_dim,)), ((), ())), preferred_element_type=F32
    )


def kernel_call(kernel, name, out_shape, prefetch=0, vmem=VMEM_BYTES, flops=1, **spec):
    if prefetch:
        spec = {
            "grid_spec": pltpu.PrefetchScalarGridSpec(
                num_scalar_prefetch=prefetch,
                grid=spec.pop("grid"),
                in_specs=spec.pop("in_specs"),
                out_specs=spec.pop("out_specs"),
                scratch_shapes=spec.pop("scratch_shapes", ()),
            ),
            **spec,
        }
    return pl.pallas_call(
        kernel,
        out_shape=out_shape,
        compiler_params=pltpu.CompilerParams(vmem_limit_bytes=vmem),
        cost_estimate=pl.CostEstimate(flops=flops, bytes_accessed=1, transcendentals=0),
        name=name,
        **spec,
    )


def made(rows, columns, kind=BF16):
    return jax.ShapeDtypeStruct((rows, columns), kind)


def kept(array):
    return pl.BlockSpec(array.shape, lambda *_: (0,) * array.ndim)


AWAY = pl.BlockSpec(memory_space=pltpu.HBM)
NEAR = pl.BlockSpec(memory_space=pltpu.VMEM)
SCALARS = pl.BlockSpec(memory_space=pltpu.SMEM)


def ends_of(lengths_ref):
    ends = [lengths_ref[0, 0]]
    for place in range(1, lengths_ref.shape[1]):
        ends.append(ends[-1] + lengths_ref[0, place])
    return ends


def starts_at(ends, places):
    start = jnp.zeros_like(places)
    for end in ends:
        start = jnp.maximum(start, jnp.where(places >= end, end, 0))
    return start


def turned_halves(columns):
    lane = lax.broadcasted_iota(jnp.int32, columns.shape, 1)
    return jnp.where(
        lane % ROTARY < ROTARY // 2, pltpu.roll(columns, 112, 1), pltpu.roll(columns, 16, 1)
    )


def span(part, size, first=0):
    at = part * size + first
    return pl.ds(at if isinstance(at, int) else pl.multiple_of(at, BLOCK if size % BLOCK == 0 else size), size)


class Copies:
    def __init__(self, sems):
        self.sems, self.made = sems, {}

    def start(self, name, source, target):
        copy = pltpu.make_async_copy(source, target, self.sems.at[len(self.made)])
        self.made[name] = copy
        copy.start()

    def numbered(self, names, count):
        first = len(self.made)
        for at in range(len(names) * count):
            self.made[("kept", first + at)] = None
        return {name: first + at * count for at, name in enumerate(names)}

    def at(self, source, target, number):
        return pltpu.make_async_copy(source, target, self.sems.at[number])

    def wait(self, *names):
        for name in names:
            self.made[name].wait()


OFFSETS = tuple((planes, places) for planes in range(2) for places in range(4))
FAR = (1, 2)
CUTS = (0, 48, 96, 128)
PARTS = tuple(zip(CUTS, CUTS[1:]))
BLOCK_NAMES = tuple(o for o in OFFSETS if o != FAR) + (0, 1, 2)


def block_shapes(width):
    return [made(BLOCK, width)] * 7 + [made(high - low, width) for low, high in PARTS]


def block_copy(copies, place_ref_of, which, total, ref, columns, number):
    name = BLOCK_NAMES[which]
    low, high = PARTS[name] if isinstance(name, int) else (0, BLOCK)
    place = place_ref_of[OFFSETS.index(FAR if isinstance(name, int) else name)]
    first = pl.multiple_of(place * BLOCK, BLOCK) + low
    return copies.at(
        total.at[pl.ds(first, high - low), columns], ref.at[:, columns], number
    )


def each_block_copy(copies, places_ref, total, refs, parts, size, first, do):
    for part in parts:
        columns = span(part, size)
        for which, ref in enumerate(refs):
            number = first + part * len(refs) + which
            do(block_copy(copies, places_ref, which, total, ref, columns, number))


def start(copy):
    copy.start()


def wait(copy):
    copy.wait()


def forward_kernel(
    lengths_ref,
    freq_ref,
    gain_ref,
    bias_ref,
    b_qkv_ref,
    b_fc1_ref,
    tokens_hbm,
    cot_hbm,
    w_qkv_hbm,
    w_fc1_hbm,
    w_dense_hbm,
    w_fc2_hbm,
    hidden_hbm,
    grad_hbm,
    act_hbm,
    slope_hbm,
    ctx_hbm,
    qkv_grad_hbm,
    stats_hbm,
    branch_hbm,
    tokens,
    grad,
    hidden,
    w_qkv,
    w_fc1,
    w_dense,
    w_fc2,
    qkv,
    act,
    slope,
    ctx_grad,
    ctx,
    qkv_grad,
    cosines,
    sines,
    stats,
    turn_sum,
    value_sum,
    both_ctx,
    both_grad,
    sems,
):
    slot_len, width = tokens.shape
    blocks = slot_len // ROWS
    copies = Copies(sems)
    ends = ends_of(lengths_ref)
    row_copies = {
        "tokens": (tokens_hbm, tokens),
        "cot": (cot_hbm, grad),
        "hidden": (hidden, hidden_hbm),
        "grad": (grad, grad_hbm),
        "act": (act, act_hbm),
        "slope": (slope, slope_hbm),
    }
    numbers = copies.numbered(tuple(row_copies), blocks)
    parts, size = 4, width // 4
    first_branch = copies.numbered(("branch",), parts)["branch"]
    w_fc2_number = copies.numbered(("w_fc2",), 1)["w_fc2"]

    def rows_at(block, part=0, height=ROWS):
        return span(part, height, block * ROWS)

    def row_copy(name, block):
        source, target = row_copies[name]
        at = rows_at(block)
        return copies.at(source.at[at, :], target.at[at, :], numbers[name] + block)

    def normalise(block, part, height):
        at = rows_at(block, part, height)
        places = block * ROWS + part * height
        places = places + lax.broadcasted_iota(jnp.int32, (height, 128), 0)
        lane = lax.broadcasted_iota(jnp.int32, (height, 128), 1)
        position = (places - starts_at(ends, places)).astype(F32)
        angle = position * freq_ref[...]
        cosines[at, :] = jnp.where(lane % HEAD_DIM < ROTARY, jnp.cos(angle), 1.0)
        sine = jnp.sin(angle)
        sines[at, :] = jnp.where(
            lane % HEAD_DIM < ROTARY // 2, -sine, jnp.where(lane % HEAD_DIM < ROTARY, sine, 0.0)
        )
        valid = (places < ends[-1])[:, :1]
        inputs = tokens[at, :].astype(F32)
        mean = jnp.mean(inputs, axis=1, keepdims=True)
        center = inputs - mean
        inv_sigma = lax.rsqrt(jnp.mean(center * center, axis=1, keepdims=True) + 1e-05)
        stats[at, :] = jnp.where(lane == 0, mean, inv_sigma)
        hidden[at, :] = (
            center * inv_sigma * gain_ref[...].astype(F32)[None]
            + bias_ref[...].astype(F32)[None]
        ).astype(BF16)
        grad[at, :] = jnp.where(valid, grad[at, :], jnp.zeros((height, width), BF16))

    def turn(at, projected):
        lane = lax.broadcasted_iota(jnp.int32, (ROWS, 128), 1)
        cosine, sine = cosines[at, :], sines[at, :]
        for block in range(qkv.shape[1] // 128):
            columns = slice(block * 128, block * 128 + 128)
            plain = projected[:, columns]
            turned = plain * cosine + turned_halves(plain) * sine
            if block % 3 == 1:
                turned = jnp.where(lane < HEAD_DIM, plain, turned)
            if block % 3 == 2:
                turned = jnp.where(lane < HEAD_DIM, turned, plain)
            qkv[at, columns] = turned.astype(BF16)

    def activate(at, up, columns):
        square = up * up
        share = 0.5 * jnp.tanh(up * (GELU + (GELU * 0.044715) * square)) + 0.5
        active = up * share
        act[at, columns] = active.astype(BF16)
        slope[at, columns] = (
            share + active * (1.0 - share) * (2 * GELU + (6 * GELU * 0.044715) * square)
        ).astype(BF16)

    def attend(pair, head):
        heads = pl.ds(pl.multiple_of(pair * 6 * HEAD_DIM, 6 * HEAD_DIM), 6 * HEAD_DIM)
        wide = pl.ds(pl.multiple_of(pair * 2 * HEAD_DIM, 2 * HEAD_DIM), 2 * HEAD_DIM)
        at = 3 * HEAD_DIM * head
        mine = slice(HEAD_DIM * head, HEAD_DIM * head + HEAD_DIM)
        all_heads = qkv[:, heads]
        for block in reversed(range(slot_len // QUERIES)):
            rows = slice(block * QUERIES, block * QUERIES + QUERIES)
            reach = (block + 1) * QUERIES
            query = all_heads[rows, at : at + 64] * BF16(HEAD_DIM**-0.5)
            key = all_heads[0:reach, at + 64 : at + 128]
            value = all_heads[0:reach, at + 128 : at + 192]
            upstream = ctx_grad[rows, wide][:, mine]
            scores = dot(key, query, 1, 1)
            place = block * QUERIES + lax.broadcasted_iota(jnp.int32, (1, QUERIES), 1)
            begin = starts_at(ends, place)
            key_place = lax.broadcasted_iota(jnp.int32, (reach, QUERIES), 0)
            scores = jnp.where((key_place >= begin) & (key_place <= place), scores, -1e30)
            raised = jnp.exp(scores - jnp.max(scores, axis=0, keepdims=True))
            prob = raised * (1.0 / jnp.sum(raised, axis=0, keepdims=True))
            prob_low = prob.astype(BF16)
            context = dot(value, prob_low, 0, 0)
            prob_grad = dot(value, upstream, 1, 1)
            row_dot = jnp.sum(prob_grad * prob, axis=0, keepdims=True)
            score_grad = (prob * (prob_grad - row_dot)).astype(BF16)
            query_grad = dot(key, score_grad, 0, 0)
            value_part = dot(prob_low, upstream, 1, 0)
            key_part = dot(score_grad, query, 1, 0)
            if reach == slot_len:
                value_sum[...] = value_part
                turn_sum[:, 64:128] = key_part
            else:
                value_sum[0:reach] += value_part
                turn_sum[0:reach, 64:128] += key_part
            turn_sum[rows, 0:64] = query_grad.T * HEAD_DIM**-0.5
            both_ctx[rows, mine] = context.T.astype(BF16)
        both = turn_sum[...]
        both = both * cosines[...] - turned_halves(both) * sines[...]
        both_grad[:, at : at + 128] = both.astype(BF16)
        both_grad[:, at + 128 : at + 192] = value_sum[...].astype(BF16)
        if head:
            ctx[:, wide] = both_ctx[...]
            qkv_grad[:, heads] = both_grad[...]

    def last_weights():
        return copies.at(w_fc2_hbm, w_fc2, w_fc2_number)

    def branch_copy(part):
        columns = span(part, size)
        return copies.at(
            tokens.at[:, columns], branch_hbm.at[:, columns], first_branch + part
        )

    for name in ("tokens", "cot"):
        row_copy(name, 0).start()
    copies.start("w_qkv", w_qkv_hbm, w_qkv)
    for name in ("tokens", "cot"):
        row_copy(name, 1).start()
    copies.start("w_fc1", w_fc1_hbm, w_fc1)
    copies.start("w_dense", w_dense_hbm, w_dense)

    def one_block(block, ready):
        for name in ("tokens", "cot"):
            row_copy(name, block).wait()
        for part in range(4):
            normalise(block, part, ROWS // 4)
        for name in ("hidden", "grad"):
            row_copy(name, block).start()
        ready("w_qkv")
        at = rows_at(block)
        turn(at, dot(hidden[at, :], w_qkv[...], 1, 0) + b_qkv_ref[...].astype(F32)[None])
        ready("w_fc1", "w_dense")
        half = w_fc1.shape[1] // 2
        for part in range(2):
            columns = slice(part * half, part * half + half)
            up = dot(hidden[at, :], w_fc1[:, columns], 1, 0)
            activate(at, up + b_fc1_ref[columns].astype(F32)[None], columns)
        ctx_grad[at, :] = dot(grad[at, :], w_dense[...], 1, 1).astype(BF16)
        for name in ("act", "slope"):
            row_copy(name, block).start()

    for later in range(2, blocks):
        for name in ("tokens", "cot"):
            row_copy(name, later).start()
    last_weights().start()
    one_block(0, copies.wait)

    @pl.loop(1, blocks)
    def _(block):
        one_block(block, lambda *names: None)

    copies.start("stats", stats, stats_hbm)

    @pl.loop(0, ctx.shape[1] // (2 * HEAD_DIM))
    def _(pair):
        for head in range(2):
            attend(pair, head)

    copies.start("ctx", ctx, ctx_hbm)
    copies.start("qkv_grad", qkv_grad, qkv_grad_hbm)
    last_weights().wait()

    @pl.loop(0, parts)
    def _(part):
        columns = span(part, size)
        tokens[:, columns] = (
            dot(ctx[...], w_dense[:, columns], 1, 0) + dot(act[...], w_fc2[:, columns], 1, 0)
        ).astype(BF16)
        branch_copy(part).start()

    for name in ("hidden", "grad", "act", "slope"):
        for block in range(blocks):
            row_copy(name, block).wait()
    copies.wait("stats", "ctx", "qkv_grad")
    for part in range(parts):
        branch_copy(part).wait()


def forward(lengths, freq, tokens, cot, gain, bias, b_qkv, b_fc1, w_qkv, w_fc1, w_dense, w_fc2):
    slot_len, width = tokens.shape
    units, heads, ctx_width = w_fc2.shape[0], w_qkv.shape[1], w_dense.shape[0]
    row_kinds = (width, width, units, units, ctx_width, heads)

    def room(rows, columns, kind=BF16):
        return pltpu.VMEM((rows, columns), kind)

    return kernel_call(
        forward_kernel,
        "forward",
        [made(slot_len, columns) for columns in row_kinds]
        + [made(slot_len, 128, F32), made(slot_len, width)],
        grid=(1,),
        in_specs=[SCALARS] + [kept(a) for a in (freq, gain, bias, b_qkv, b_fc1)] + [AWAY] * 6,
        out_specs=[AWAY] * 8,
        scratch_shapes=[room(slot_len, width)] * 3
        + [pltpu.VMEM(w.shape, BF16) for w in (w_qkv, w_fc1, w_dense, w_fc2)]
        + [
            room(slot_len, heads),
            room(slot_len, units),
            room(slot_len, units),
            room(slot_len, ctx_width),
            room(slot_len, ctx_width),
            room(slot_len, heads),
        ]
        + [room(slot_len, 128, F32)] * 4
        + [
            room(slot_len, HEAD_DIM, F32),
            room(slot_len, 2 * HEAD_DIM),
            room(slot_len, 6 * HEAD_DIM),
            pltpu.SemaphoreType.DMA((80,)),
        ],
    )(lengths, freq, gain, bias, b_qkv, b_fc1, tokens, cot, w_qkv, w_fc1, w_dense, w_fc2)


def backward_kernel(
    places_ref,
    grad_hbm,
    slope_hbm,
    qkv_grad_hbm,
    tokens_hbm,
    stats_hbm,
    w_fc2_hbm,
    w_fc1_hbm,
    w_qkv_hbm,
    norm_sum_ref,
    grad_sum_ref,
    head_sum_ref,
    unit_sum_ref,
    up_grad_hbm,
    *rest,
):
    blocks, scratch = rest[: len(BLOCK_NAMES)], rest[len(BLOCK_NAMES) :]
    grad, slope, qkv_grad, tokens, stats, w_fc2, w_fc1, w_qkv, *scratch = scratch
    up_grad, hidden, gain_sum, shift_sum, grad_sum, head_sum, unit_sum, sems = scratch
    copies = Copies(sems)
    slot_len, width = grad.shape
    units, size = w_fc2.shape[0], 512

    def part_of(part):
        return span(part, size)

    def bring_rows(name, part, source, target):
        at = part_of(part)
        copies.start((name, part), source.at[at, :], target.at[at, :])

    def add_to(ref, columns, array):
        ref[:, columns] += jnp.sum(array, axis=0, keepdims=True)

    def to_units(rows, part):
        at, columns = part_of(rows), part_of(part)
        up = dot(grad[at, :], w_fc2[columns, :], 1, 1) * slope[at, columns].astype(F32)
        up = up.astype(BF16)
        up_grad[at, columns] = up
        add_to(unit_sum, columns, up.astype(F32))

    def to_hidden(rows, part):
        at, columns = part_of(rows), part_of(part)
        result = dot(up_grad[at, :], w_fc1[columns, :], 1, 1) + dot(
            qkv_grad[at, :], w_qkv[columns, :], 1, 1
        )
        hidden[at, columns] = result.astype(BF16)
        normed = (tokens[at, columns].astype(F32) - stats[at, 0:1]) * stats[at, 1:2]
        add_to(gain_sum, columns, result * normed)
        add_to(shift_sum, columns, result)

    parts = width // size
    first_block = copies.numbered(("blocks",), parts * len(blocks))["blocks"]

    def blocks_of(which, do):
        each_block_copy(copies, places_ref, hidden, blocks, which, size, first_block, do)

    for part in range(2):
        bring_rows("grad", part, grad_hbm, grad)
        bring_rows("slope", part, slope_hbm, slope)
        bring_rows("w_fc2", part, w_fc2_hbm, w_fc2)
    for total in (gain_sum, shift_sum, grad_sum, head_sum, unit_sum):
        total[...] = jnp.zeros_like(total)
    copies.wait(("w_fc2", 0), ("grad", 0), ("slope", 0))
    copies.start("w_fc1", w_fc1_hbm, w_fc1)
    copies.start("w_qkv", w_qkv_hbm, w_qkv)
    copies.start("qkv_grad", qkv_grad_hbm, qkv_grad)
    copies.start("tokens", tokens_hbm, tokens)
    copies.start("stats", stats_hbm, stats)

    @pl.loop(0, 4)
    def _(turn):
        rows, part = turn // 2, turn % 2

        @pl.when(turn == 1)
        def _():
            copies.wait(("w_fc2", 1))

        @pl.when(turn == 2)
        def _():
            copies.wait(("grad", 1), ("slope", 1))

        to_units(rows, part)

        @pl.when(part == 0)
        def _():
            add_to(grad_sum, slice(0, width), grad[part_of(rows), :].astype(F32))

    copies.start("up_grad", up_grad, up_grad_hbm)
    copies.wait("w_fc1", "w_qkv", "qkv_grad", "tokens", "stats")
    add_to(head_sum, slice(0, qkv_grad.shape[1]), qkv_grad[...].astype(F32))

    @pl.loop(0, parts)
    def _(part):
        for rows in range(slot_len // size):
            to_hidden(rows, part)
        blocks_of((part,), start)

    for ref, first, total in (
        (norm_sum_ref, 0, gain_sum),
        (norm_sum_ref, 16, shift_sum),
        (grad_sum_ref, 0, grad_sum),
        (head_sum_ref, 0, head_sum),
        (unit_sum_ref, 0, unit_sum),
    ):
        share = total.shape[1] // 16
        if share < BLOCK:
            ref[...] = jnp.zeros_like(ref)
        for row in range(16):
            ref[first + row : first + row + 1, 0:share] = total[:, row * share : row * share + share]
    copies.wait("up_grad")
    blocks_of(range(parts), wait)


def backward(places, grad, slope, qkv_grad, tokens, stats, w_fc2, w_fc1, w_qkv):
    slot_len, width = tokens.shape
    units, heads = w_fc2.shape[0], w_qkv.shape[1]
    sizes = (width, width, width, heads, units)
    sums = [made(rows, BLOCK, F32) for rows in (32, 16, 16, 16)]
    arrays = (grad, slope, qkv_grad, tokens, stats, w_fc2, w_fc1, w_qkv)
    norm_sum, grad_sum, head_sum, unit_sum, up_grad, *blocks = kernel_call(
        backward_kernel,
        "backward",
        sums + [made(slot_len, units)] + block_shapes(width),
        grid=(1,),
        in_specs=[SCALARS] + [AWAY] * len(arrays),
        out_specs=[kept(array) for array in sums] + [AWAY] * (1 + len(BLOCK_NAMES)),
        scratch_shapes=[pltpu.VMEM(array.shape, array.dtype) for array in arrays]
        + [pltpu.VMEM((slot_len, units), BF16), pltpu.VMEM((slot_len, width), BF16)]
        + [pltpu.VMEM((1, size), F32) for size in sizes]
        + [pltpu.SemaphoreType.DMA((64,))],
    )(places, *arrays)
    sums = (norm_sum, grad_sum, head_sum, unit_sum)
    return up_grad, sums, dict(zip(BLOCK_NAMES, blocks))


def weight_kernel(order_ref, *refs):
    lefts, (first_ref, second_ref, *sums, out_ref) = refs[:AT_ONCE], refs[AT_ONCE:]
    cut, end = first_ref.shape[1], first_ref.shape[1] + second_ref.shape[1]
    left = jnp.concatenate([ref[...] for ref in lefts], axis=1)
    out_ref[:, 0:cut] = dot(left, first_ref[...], 0, 0).astype(BF16)
    out_ref[:, cut:end] = dot(left, second_ref[...], 0, 0).astype(BF16)
    if sums:
        for half in range(AT_ONCE):
            block = order_ref[AT_ONCE * pl.program_id(0) + half]
            lines = [
                ref[pl.ds(first + block, 1), :]
                for ref in sums
                for first in range(0, ref.shape[0], 16)
            ]
            lines.append(jnp.zeros((BLOCK - len(lines), BLOCK), F32))
            columns = jnp.concatenate(lines, axis=0).T
            out_ref[half * BLOCK : half * BLOCK + BLOCK, end:] = columns.astype(BF16)


def weight_blocks(order, left, first, second, *sums):
    slot_len = left.shape[0]
    width = first.shape[1] + second.shape[1] + (BLOCK if sums else 0)
    return kernel_call(
        weight_kernel,
        "weights",
        made(left.shape[1], width),
        prefetch=1,
        grid=(left.shape[1] // (AT_ONCE * BLOCK),),
        in_specs=[
            *[
                pl.BlockSpec(
                    (slot_len, BLOCK),
                    functools.partial(lambda at, i, order: (0, order[AT_ONCE * i + at]), at),
                )
                for at in range(AT_ONCE)
            ],
            kept(first),
            kept(second),
            *[kept(array) for array in sums],
        ],
        out_specs=pl.BlockSpec((AT_ONCE * BLOCK, width), lambda i, order: (i, 0)),
    )(order, *[left] * AT_ONCE, first, second, *sums)


def combine(name, *sums):
    arrays = [term[0] for terms in sums for term in terms]
    specs = [
        pl.BlockSpec((term[1], term[0].shape[1]), functools.partial(lambda at, _: (at, 0), term[2]))
        for terms in sums
        for term in terms
    ]
    heights = [max(term[4] for term in terms) for terms in sums]

    def kernel(*refs):
        ins, outs = list(refs[: len(arrays)]), refs[len(arrays) :]
        for terms, height, out in zip(sums, heights, outs):
            mine = [(ins.pop(0), term[3], term[4]) for term in terms]
            cuts = sorted({cut for _, low, high in mine for cut in (low, high)})
            for low, high in zip(cuts, cuts[1:]):
                parts = [
                    ref[low - first : high - first, :].astype(F32)
                    for ref, first, last in mine
                    if first <= low and high <= last
                ]
                out[low:high, :] = functools.reduce(lambda a, b: a + b, parts).astype(BF16)

    shapes = [made(height, terms[0][0].shape[1]) for height, terms in zip(heights, sums)]
    return kernel_call(
        kernel,
        name,
        shapes,
        grid=(1,),
        in_specs=specs,
        out_specs=[pl.BlockSpec(shape.shape, lambda _: (0, 0)) for shape in shapes],
    )(*arrays)


def whole_term(array, low=0):
    return (array, array.shape[0], 0, low, low + array.shape[0])


def output_kernel(lengths_ref, tokens_ref, branch_ref, b_dense_ref, b_fc2_ref, out_ref):
    bias = b_dense_ref[...].astype(F32) + b_fc2_ref[...].astype(F32)
    rows = tokens_ref.shape[0]
    place = pl.program_id(0) * rows + lax.broadcasted_iota(jnp.int32, (rows, 1), 0)
    total = jnp.where(
        place < ends_of(lengths_ref)[-1], branch_ref[...].astype(F32) + bias[None], 0.0
    )
    out_ref[...] = (tokens_ref[...].astype(F32) + total).astype(BF16)


def finish_output(lengths, tokens, branch_sum, b_dense, b_fc2):
    slot_len, width = tokens.shape
    row = pl.BlockSpec((ROWS, width), lambda i: (i, 0))
    return kernel_call(
        output_kernel,
        "output",
        made(slot_len, width),
        grid=(slot_len // ROWS,),
        in_specs=[SCALARS, row, row, kept(b_dense), kept(b_fc2)],
        out_specs=row,
    )(lengths, tokens, branch_sum, b_dense, b_fc2)


def input_kernel(places_ref, *refs):
    *terms, tokens_ref, cot_ref, stats_ref, gain_ref, out_ref = refs
    total = functools.reduce(lambda a, b: a + b, [t[...].astype(F32) for t in terms])
    inv_sigma = stats_ref[:, 1:2]
    normed = (tokens_ref[...].astype(F32) - stats_ref[:, 0:1]) * inv_sigma
    scaled = total * gain_ref[...].astype(F32)[None]
    out_ref[...] = (
        cot_ref[...].astype(F32)
        + inv_sigma
        * (
            scaled
            - jnp.mean(scaled, axis=1, keepdims=True)
            - normed * jnp.mean(scaled * normed, axis=1, keepdims=True)
        )
    ).astype(BF16)


def input_rows(places, terms, tokens, cot, stats, gain):
    width = tokens.shape[1]

    def mine(columns):
        return pl.BlockSpec((BLOCK, columns), lambda i, places: (places[0], 0))

    return kernel_call(
        input_kernel,
        "input",
        made(BLOCK, width),
        prefetch=1,
        grid=(1,),
        in_specs=[kept(t) for t in terms] + [mine(width), mine(width), mine(128), kept(gain)],
        out_specs=pl.BlockSpec((BLOCK, width), lambda *_: (0, 0)),
    )(places, *terms, tokens, cot, stats, gain)


def place_kernel(blocks, places_ref, *refs):
    pieces, out_ref, sems = refs[: len(blocks)], refs[-2], refs[-1]
    copies = []
    for i, ((offset, low, high), piece) in enumerate(zip(blocks, pieces)):
        first = pl.multiple_of(places_ref[OFFSETS.index(offset)] * BLOCK, BLOCK)
        copies.append(
            pltpu.make_async_copy(
                piece, out_ref.at[pl.ds(first + low, high - low), :], sems.at[i]
            )
        )
    for copy in copies:
        copy.start()
    for copy in copies:
        copy.wait()


def place_rows(places, blocks, pieces, whole=None):
    rest = {} if whole is None else {"input_output_aliases": {len(pieces) + 1: 0}}
    given = [] if whole is None else [whole]
    return kernel_call(
        functools.partial(place_kernel, blocks),
        "place",
        made(8 * BLOCK, pieces[0].shape[1]),
        in_specs=[SCALARS] + [NEAR] * len(pieces) + [AWAY] * len(given),
        out_specs=AWAY,
        scratch_shapes=[pltpu.SemaphoreType.DMA((len(pieces),))],
        **rest,
    )(places, *pieces, *given)


def up_kernel(near_ref, far_ref, first_ref, second_ref):
    total = near_ref[...].astype(F32) + far_ref[...].astype(F32)
    cut = first_ref.shape[1]
    first_ref[...] = total[:, :cut]
    second_ref[...] = total[:, cut:]


def down_kernel(near_ref, far_ref, first_ref, second_ref, sums_ref):
    total = near_ref[...].astype(F32) + far_ref[...].astype(F32)
    cut, end = first_ref.shape[0], first_ref.shape[0] + second_ref.shape[0]
    first_ref[...] = total[:, :cut].T
    second_ref[...] = total[:, cut:end].T
    sums_ref[...] = total[:, end:].T[: sums_ref.shape[0]]


def last_sum(kernel, name, shapes, near, far):
    return kernel_call(
        kernel,
        name,
        [made(*shape, F32) for shape in shapes],
        grid=(1,),
        in_specs=[pl.BlockSpec(far.shape, lambda _: (0, 0))] * 2,
        out_specs=[pl.BlockSpec(shape, lambda _: (0, 0)) for shape in shapes],
    )(near, far)


def shift(array, axis, size, by):
    return lax.ppermute(array, axis, [(i, (i + by) % size) for i in range(size)])


def y_up(array):
    return shift(array, "y", 4, 1)


def y_down(array):
    return shift(array, "y", 4, 3)


def across(array):
    return shift(array, "zl", 2, 1)


def after(arrays, *earlier):
    return lax.optimization_barrier((arrays, earlier))[0]


class TensorSum:
    def __init__(self, blocks):
        self.blocks = blocks

    def send_far(self):
        b = self.blocks
        self.far = across(b[0]), y_up(b[1]), y_down(b[2])

    def send_middle(self, earlier):
        b = self.blocks
        far = *self.far[:2], after(self.far[2], earlier)
        sent = combine(
            "middle",
            *[
                [whole_term(b[offset]), whole_term(part, low)]
                for offset, part, (low, _) in zip(((0, 2), (1, 1), (1, 3)), far, PARTS)
            ],
        )
        self.middle = y_up(sent[0]), across(sent[1]), y_down(sent[2])
        return sent

    def send_near(self, earlier):
        b = self.blocks
        two_on, diagonal, other = self.middle
        other = after(other, earlier)
        sent = combine(
            "near",
            [whole_term(b[(0, 1)]), whole_term(two_on), whole_term(diagonal)],
            [whole_term(b[(1, 0)]), whole_term(other)],
        )
        self.near = [y_up(sent[0]), across(sent[1]), y_down(after(b[(0, 3)], sent))]
        return sent

    def terms(self):
        return [self.blocks[(0, 0)], *self.near]


class TensorGather:
    def __init__(self, places, rows):
        self.places, self.rows = places, rows
        self.one = y_up(rows), y_down(rows), across(rows)

    def second(self, earlier):
        before, ahead, partner = self.one = after(self.one, earlier)
        self.two = y_down(ahead), across(ahead), y_up(partner)
        return self.one

    def third(self, earlier):
        two_on, diagonal, other = self.two = after(self.two, earlier)
        (a, b), (c, d), (e, f) = PARTS
        self.three = across(two_on[a:b]), y_down(diagonal[c:d]), y_up(other[e:f])
        blocks = [(0, 0), (0, 3), (0, 1), (1, 0), (0, 2), (1, 1), (1, 3)]
        self.whole = place_rows(
            self.places,
            [(offset, 0, BLOCK) for offset in blocks],
            [self.rows, *self.one, *self.two],
        )
        return self.whole

    def finish(self, earlier):
        parts = after(self.three, earlier)
        return place_rows(
            self.places, [(FAR, low, high) for low, high in PARTS], list(parts), self.whole
        )


class DataSum:
    def __init__(self, partial_sums, earlier):
        self.near = lax.psum_scatter(
            after(partial_sums, earlier), ("x", "core"), scatter_dimension=0, tiled=True
        )

    def send(self, earlier):
        self.near = after(self.near, earlier)
        self.far = shift(self.near[BLOCK:], "zh", 2, 1)

    def finish(self, kernel, name, shapes, earlier):
        return last_sum(kernel, name, shapes, self.near, after(self.far, earlier))


def dp_order():
    half = lax.axis_index("zh")
    return jnp.stack(
        [(half + part) % 2 * 8 + block for block in range(8) for part in range(2)]
    ).astype(jnp.int32)


def per_device(
    tokens,
    cotangent,
    seq_lengths,
    ln_gain,
    ln_bias,
    w_qkv,
    b_qkv,
    w_dense,
    b_dense,
    w_fc1,
    b_fc1,
    w_fc2,
    b_fc2,
):
    units = w_fc2.shape[0]
    plane, place = lax.axis_index("zl"), lax.axis_index("y")
    places = jnp.stack(
        [(plane + planes) % 2 * 4 + (place + steps) % 4 for planes, steps in OFFSETS]
    ).astype(jnp.int32)
    order = dp_order()
    frequency = 10000.0 ** (-jnp.arange(ROTARY // 2, dtype=F32) * 2.0 / ROTARY)
    frequency = jnp.tile(frequency, 8)[None]
    hidden, grad, activated, slope, context, qkv_grad, stats, branch_part = forward(
        seq_lengths,
        frequency,
        tokens,
        cotangent,
        ln_gain,
        ln_bias,
        b_qkv,
        b_fc1,
        w_qkv,
        w_fc1,
        w_dense,
        w_fc2,
    )
    branch_sum = lax.psum(branch_part, TENSOR)
    up_grad, sums, blocks = backward(
        after(places, branch_part), grad, slope, qkv_grad, tokens, stats, w_fc2, w_fc1, w_qkv
    )
    hidden_sum = TensorSum(blocks)
    hidden_sum.send_far()
    down_part = weight_blocks(after(order, up_grad), grad, activated, context, *sums)
    done = hidden_sum.send_middle(down_part)
    down = DataSum(down_part, done)
    up_part = weight_blocks(after(order, done), hidden, up_grad, qkv_grad)
    done = hidden_sum.send_near(up_part)
    up = DataSum(up_part, done)
    rows = input_rows(
        after(places, done), hidden_sum.terms(), tokens, cotangent, stats, ln_gain
    )
    input_grad = TensorGather(places, rows)
    down.send((rows, branch_sum))
    done = input_grad.second(down.near)
    up.send(done)
    output = finish_output(after(seq_lengths, up.near), tokens, branch_sum, b_dense, b_fc2)
    grad_fc2, grad_dense, small = down.finish(
        down_kernel,
        "down",
        ((units, BLOCK), (w_dense.shape[0], BLOCK), (8, BLOCK)),
        output,
    )
    norm_sum = small[:2]
    norm_across = across(norm_sum)
    input_grad.third(small)
    *three, up.far = after([*input_grad.three, up.far], input_grad.whole)
    input_grad.three = three
    norm_sum = norm_sum + after(norm_across, three[0])
    grad_fc1, grad_qkv = up.finish(
        up_kernel, "up", ((BLOCK, units), (BLOCK, w_qkv.shape[1])), input_grad.three[0]
    )
    norm_sum = norm_sum + y_up(norm_sum) + y_down(norm_sum) + shift(norm_sum, "y", 4, 2)
    input_grad = input_grad.finish(grad_qkv)
    out_bias = small[2]
    return (
        output,
        input_grad,
        norm_sum[0],
        norm_sum[1],
        grad_qkv,
        small[3, :48],
        grad_dense,
        out_bias,
        grad_fc1,
        small[4, :64],
        grad_fc2,
        out_bias,
    )


def solution(mesh):
    parts = Mesh(mesh.devices.reshape(2, 4, 2, 2, 4), DP + TENSOR)
    rows = P(DP, None)
    placed = (
        rows,
        rows,
        rows,
        P(),
        P(),
        P(None, TENSOR),
        P(TENSOR),
        P(TENSOR, None),
        P(),
        P(None, TENSOR),
        P(TENSOR),
        P(TENSOR, None),
        P(),
    )
    return jax.shard_map(
        per_device,
        mesh=parts,
        in_specs=placed,
        out_specs=(
            rows,
            rows,
            P(DP),
            P(DP),
            P(DP, TENSOR),
            P(TENSOR + DP),
            P(TENSOR, DP),
            P(DP),
            P(DP, TENSOR),
            P(TENSOR + DP),
            P(TENSOR, DP),
            P(DP),
        ),
        check_vma=False,
    )
```

```python
import functools

import jax
import jax.numpy as jnp
from jax import lax
from jax.experimental import pallas as pl
from jax.experimental.pallas import tpu as pltpu
from jax.sharding import Mesh
from jax.sharding import PartitionSpec as P

HEAD_DIM = 64
ROTARY = 32
DP = ("zh", "x", "core")
TENSOR = ("zl", "y")
BF16 = jnp.bfloat16
F32 = jnp.float32
ROWS = 256
QUERIES = 512
BLOCK = 128
AT_ONCE = 4
VMEM_BYTES = 56 * 2**20
GELU = 0.7978845608


def dot(left, right, left_dim, right_dim):
    return lax.dot_general(
        left, right, (((left_dim,), (right_dim,)), ((), ())), preferred_element_type=F32
    )


def kernel_call(kernel, name, out_shape, prefetch=0, vmem=VMEM_BYTES, flops=1, **spec):
    if prefetch:
        spec = {
            "grid_spec": pltpu.PrefetchScalarGridSpec(
                num_scalar_prefetch=prefetch,
                grid=spec.pop("grid"),
                in_specs=spec.pop("in_specs"),
                out_specs=spec.pop("out_specs"),
                scratch_shapes=spec.pop("scratch_shapes", ()),
            ),
            **spec,
        }
    return pl.pallas_call(
        kernel,
        out_shape=out_shape,
        compiler_params=pltpu.CompilerParams(vmem_limit_bytes=vmem),
        cost_estimate=pl.CostEstimate(flops=flops, bytes_accessed=1, transcendentals=0),
        name=name,
        **spec,
    )


def made(rows, columns, kind=BF16):
    return jax.ShapeDtypeStruct((rows, columns), kind)


def kept(array):
    return pl.BlockSpec(array.shape, lambda *_: (0,) * array.ndim)


AWAY = pl.BlockSpec(memory_space=pltpu.HBM)
NEAR = pl.BlockSpec(memory_space=pltpu.VMEM)
SCALARS = pl.BlockSpec(memory_space=pltpu.SMEM)


def ends_of(lengths_ref):
    ends = [lengths_ref[0, 0]]
    for place in range(1, lengths_ref.shape[1]):
        ends.append(ends[-1] + lengths_ref[0, place])
    return ends


def starts_at(ends, places):
    start = jnp.zeros_like(places)
    for end in ends:
        start = jnp.maximum(start, jnp.where(places >= end, end, 0))
    return start


def turned_halves(columns):
    lane = lax.broadcasted_iota(jnp.int32, columns.shape, 1)
    return jnp.where(
        lane % ROTARY < ROTARY // 2, pltpu.roll(columns, 112, 1), pltpu.roll(columns, 16, 1)
    )


def span(part, size, first=0):
    at = part * size + first
    return pl.ds(at if isinstance(at, int) else pl.multiple_of(at, BLOCK if size % BLOCK == 0 else size), size)


class Copies:
    def __init__(self, sems):
        self.sems, self.made = sems, {}

    def start(self, name, source, target):
        copy = pltpu.make_async_copy(source, target, self.sems.at[len(self.made)])
        self.made[name] = copy
        copy.start()

    def numbered(self, names, count):
        first = len(self.made)
        for at in range(len(names) * count):
            self.made[("kept", first + at)] = None
        return {name: first + at * count for at, name in enumerate(names)}

    def at(self, source, target, number):
        return pltpu.make_async_copy(source, target, self.sems.at[number])

    def wait(self, *names):
        for name in names:
            self.made[name].wait()


OFFSETS = tuple((planes, places) for planes in range(2) for places in range(4))
FAR = (1, 2)
CUTS = (0, 48, 96, 128)
PARTS = tuple(zip(CUTS, CUTS[1:]))
BLOCK_NAMES = tuple(o for o in OFFSETS if o != FAR) + (0, 1, 2)


def block_shapes(width):
    return [made(BLOCK, width)] * 7 + [made(high - low, width) for low, high in PARTS]


def block_copy(copies, place_ref_of, which, total, ref, columns, number):
    name = BLOCK_NAMES[which]
    low, high = PARTS[name] if isinstance(name, int) else (0, BLOCK)
    place = place_ref_of[OFFSETS.index(FAR if isinstance(name, int) else name)]
    first = pl.multiple_of(place * BLOCK, BLOCK) + low
    return copies.at(
        total.at[pl.ds(first, high - low), columns], ref.at[:, columns], number
    )


def each_block_copy(copies, places_ref, total, refs, parts, size, first, do):
    for part in parts:
        columns = span(part, size)
        for which, ref in enumerate(refs):
            number = first + part * len(refs) + which
            do(block_copy(copies, places_ref, which, total, ref, columns, number))


def start(copy):
    copy.start()


def wait(copy):
    copy.wait()


def forward_kernel(
    lengths_ref,
    freq_ref,
    gain_ref,
    bias_ref,
    b_qkv_ref,
    b_fc1_ref,
    tokens_hbm,
    cot_hbm,
    w_qkv_hbm,
    w_fc1_hbm,
    w_dense_hbm,
    w_fc2_hbm,
    hidden_hbm,
    grad_hbm,
    act_hbm,
    slope_hbm,
    ctx_hbm,
    qkv_grad_hbm,
    stats_hbm,
    branch_hbm,
    tokens,
    grad,
    hidden,
    w_qkv,
    w_fc1,
    w_dense,
    w_fc2,
    qkv,
    act,
    slope,
    ctx_grad,
    ctx,
    qkv_grad,
    cosines,
    sines,
    stats,
    turn_sum,
    value_sum,
    both_ctx,
    both_grad,
    sems,
):
    slot_len, width = tokens.shape
    blocks = slot_len // ROWS
    copies = Copies(sems)
    ends = ends_of(lengths_ref)
    row_copies = {
        "tokens": (tokens_hbm, tokens),
        "cot": (cot_hbm, grad),
        "hidden": (hidden, hidden_hbm),
        "grad": (grad, grad_hbm),
        "act": (act, act_hbm),
        "slope": (slope, slope_hbm),
    }
    numbers = copies.numbered(tuple(row_copies), blocks)
    parts, size = 4, width // 4
    first_branch = copies.numbered(("branch",), parts)["branch"]
    w_fc2_number = copies.numbered(("w_fc2",), 1)["w_fc2"]

    def rows_at(block, part=0, height=ROWS):
        return span(part, height, block * ROWS)

    def row_copy(name, block):
        source, target = row_copies[name]
        at = rows_at(block)
        return copies.at(source.at[at, :], target.at[at, :], numbers[name] + block)

    def normalise(block, part, height):
        at = rows_at(block, part, height)
        places = block * ROWS + part * height
        places = places + lax.broadcasted_iota(jnp.int32, (height, 128), 0)
        lane = lax.broadcasted_iota(jnp.int32, (height, 128), 1)
        position = (places - starts_at(ends, places)).astype(F32)
        angle = position * freq_ref[...]
        cosines[at, :] = jnp.where(lane % HEAD_DIM < ROTARY, jnp.cos(angle), 1.0)
        sine = jnp.sin(angle)
        sines[at, :] = jnp.where(
            lane % HEAD_DIM < ROTARY // 2, -sine, jnp.where(lane % HEAD_DIM < ROTARY, sine, 0.0)
        )
        valid = (places < ends[-1])[:, :1]
        inputs = tokens[at, :].astype(F32)
        mean = jnp.mean(inputs, axis=1, keepdims=True)
        center = inputs - mean
        inv_sigma = lax.rsqrt(jnp.mean(center * center, axis=1, keepdims=True) + 1e-05)
        stats[at, :] = jnp.where(lane == 0, mean, inv_sigma)
        hidden[at, :] = (
            center * inv_sigma * gain_ref[...].astype(F32)[None]
            + bias_ref[...].astype(F32)[None]
        ).astype(BF16)
        grad[at, :] = jnp.where(valid, grad[at, :], jnp.zeros((height, width), BF16))

    def turn(at, projected):
        lane = lax.broadcasted_iota(jnp.int32, (ROWS, 128), 1)
        cosine, sine = cosines[at, :], sines[at, :]
        for block in range(qkv.shape[1] // 128):
            columns = slice(block * 128, block * 128 + 128)
            plain = projected[:, columns]
            turned = plain * cosine + turned_halves(plain) * sine
            if block % 3 == 1:
                turned = jnp.where(lane < HEAD_DIM, plain, turned)
            if block % 3 == 2:
                turned = jnp.where(lane < HEAD_DIM, turned, plain)
            qkv[at, columns] = turned.astype(BF16)

    def activate(at, up, columns):
        square = up * up
        share = 0.5 * jnp.tanh(up * (GELU + (GELU * 0.044715) * square)) + 0.5
        active = up * share
        act[at, columns] = active.astype(BF16)
        slope[at, columns] = (
            share + active * (1.0 - share) * (2 * GELU + (6 * GELU * 0.044715) * square)
        ).astype(BF16)

    def attend(pair, head):
        heads = pl.ds(pl.multiple_of(pair * 6 * HEAD_DIM, 6 * HEAD_DIM), 6 * HEAD_DIM)
        wide = pl.ds(pl.multiple_of(pair * 2 * HEAD_DIM, 2 * HEAD_DIM), 2 * HEAD_DIM)
        at = 3 * HEAD_DIM * head
        mine = slice(HEAD_DIM * head, HEAD_DIM * head + HEAD_DIM)
        all_heads = qkv[:, heads]
        for block in reversed(range(slot_len // QUERIES)):
            rows = slice(block * QUERIES, block * QUERIES + QUERIES)
            reach = (block + 1) * QUERIES
            query = all_heads[rows, at : at + 64] * BF16(HEAD_DIM**-0.5)
            key = all_heads[0:reach, at + 64 : at + 128]
            value = all_heads[0:reach, at + 128 : at + 192]
            upstream = ctx_grad[rows, wide][:, mine]
            scores = dot(key, query, 1, 1)
            place = block * QUERIES + lax.broadcasted_iota(jnp.int32, (1, QUERIES), 1)
            begin = starts_at(ends, place)
            key_place = lax.broadcasted_iota(jnp.int32, (reach, QUERIES), 0)
            scores = jnp.where((key_place >= begin) & (key_place <= place), scores, -1e30)
            raised = jnp.exp(scores - jnp.max(scores, axis=0, keepdims=True))
            prob = raised * (1.0 / jnp.sum(raised, axis=0, keepdims=True))
            prob_low = prob.astype(BF16)
            context = dot(value, prob_low, 0, 0)
            prob_grad = dot(value, upstream, 1, 1)
            row_dot = jnp.sum(prob_grad * prob, axis=0, keepdims=True)
            score_grad = (prob * (prob_grad - row_dot)).astype(BF16)
            query_grad = dot(key, score_grad, 0, 0)
            value_part = dot(prob_low, upstream, 1, 0)
            key_part = dot(score_grad, query, 1, 0)
            if reach == slot_len:
                value_sum[...] = value_part
                turn_sum[:, 64:128] = key_part
            else:
                value_sum[0:reach] += value_part
                turn_sum[0:reach, 64:128] += key_part
            turn_sum[rows, 0:64] = query_grad.T * HEAD_DIM**-0.5
            both_ctx[rows, mine] = context.T.astype(BF16)
        both = turn_sum[...]
        both = both * cosines[...] - turned_halves(both) * sines[...]
        both_grad[:, at : at + 128] = both.astype(BF16)
        both_grad[:, at + 128 : at + 192] = value_sum[...].astype(BF16)
        if head:
            ctx[:, wide] = both_ctx[...]
            qkv_grad[:, heads] = both_grad[...]

    def last_weights():
        return copies.at(w_fc2_hbm, w_fc2, w_fc2_number)

    def branch_copy(part):
        columns = span(part, size)
        return copies.at(
            tokens.at[:, columns], branch_hbm.at[:, columns], first_branch + part
        )

    for name in ("tokens", "cot"):
        row_copy(name, 0).start()
    copies.start("w_qkv", w_qkv_hbm, w_qkv)
    for name in ("tokens", "cot"):
        row_copy(name, 1).start()
    copies.start("w_fc1", w_fc1_hbm, w_fc1)
    copies.start("w_dense", w_dense_hbm, w_dense)

    def one_block(block, ready):
        for name in ("tokens", "cot"):
            row_copy(name, block).wait()
        for part in range(4):
            normalise(block, part, ROWS // 4)
        for name in ("hidden", "grad"):
            row_copy(name, block).start()
        ready("w_qkv")
        at = rows_at(block)
        turn(at, dot(hidden[at, :], w_qkv[...], 1, 0) + b_qkv_ref[...].astype(F32)[None])
        ready("w_fc1", "w_dense")
        half = w_fc1.shape[1] // 2
        for part in range(2):
            columns = slice(part * half, part * half + half)
            up = dot(hidden[at, :], w_fc1[:, columns], 1, 0)
            activate(at, up + b_fc1_ref[columns].astype(F32)[None], columns)
        ctx_grad[at, :] = dot(grad[at, :], w_dense[...], 1, 1).astype(BF16)
        for name in ("act", "slope"):
            row_copy(name, block).start()

    for later in range(2, blocks):
        for name in ("tokens", "cot"):
            row_copy(name, later).start()
    last_weights().start()
    one_block(0, copies.wait)

    @pl.loop(1, blocks)
    def _(block):
        one_block(block, lambda *names: None)

    copies.start("stats", stats, stats_hbm)

    @pl.loop(0, ctx.shape[1] // (2 * HEAD_DIM))
    def _(pair):
        for head in range(2):
            attend(pair, head)

    copies.start("ctx", ctx, ctx_hbm)
    copies.start("qkv_grad", qkv_grad, qkv_grad_hbm)
    last_weights().wait()

    @pl.loop(0, parts)
    def _(part):
        columns = span(part, size)
        tokens[:, columns] = (
            dot(ctx[...], w_dense[:, columns], 1, 0) + dot(act[...], w_fc2[:, columns], 1, 0)
        ).astype(BF16)
        branch_copy(part).start()

    for name in ("hidden", "grad", "act", "slope"):
        for block in range(blocks):
            row_copy(name, block).wait()
    copies.wait("stats", "ctx", "qkv_grad")
    for part in range(parts):
        branch_copy(part).wait()


def forward(lengths, freq, tokens, cot, gain, bias, b_qkv, b_fc1, w_qkv, w_fc1, w_dense, w_fc2):
    slot_len, width = tokens.shape
    units, heads, ctx_width = w_fc2.shape[0], w_qkv.shape[1], w_dense.shape[0]
    row_kinds = (width, width, units, units, ctx_width, heads)

    def room(rows, columns, kind=BF16):
        return pltpu.VMEM((rows, columns), kind)

    return kernel_call(
        forward_kernel,
        "forward",
        [made(slot_len, columns) for columns in row_kinds]
        + [made(slot_len, 128, F32), made(slot_len, width)],
        grid=(1,),
        in_specs=[SCALARS] + [kept(a) for a in (freq, gain, bias, b_qkv, b_fc1)] + [AWAY] * 6,
        out_specs=[AWAY] * 8,
        scratch_shapes=[room(slot_len, width)] * 3
        + [pltpu.VMEM(w.shape, BF16) for w in (w_qkv, w_fc1, w_dense, w_fc2)]
        + [
            room(slot_len, heads),
            room(slot_len, units),
            room(slot_len, units),
            room(slot_len, ctx_width),
            room(slot_len, ctx_width),
            room(slot_len, heads),
        ]
        + [room(slot_len, 128, F32)] * 4
        + [
            room(slot_len, HEAD_DIM, F32),
            room(slot_len, 2 * HEAD_DIM),
            room(slot_len, 6 * HEAD_DIM),
            pltpu.SemaphoreType.DMA((80,)),
        ],
    )(lengths, freq, gain, bias, b_qkv, b_fc1, tokens, cot, w_qkv, w_fc1, w_dense, w_fc2)


def backward_kernel(
    places_ref,
    grad_hbm,
    slope_hbm,
    qkv_grad_hbm,
    tokens_hbm,
    stats_hbm,
    w_fc2_hbm,
    w_fc1_hbm,
    w_qkv_hbm,
    norm_sum_ref,
    grad_sum_ref,
    head_sum_ref,
    unit_sum_ref,
    up_grad_hbm,
    *rest,
):
    blocks, scratch = rest[: len(BLOCK_NAMES)], rest[len(BLOCK_NAMES) :]
    grad, slope, qkv_grad, tokens, stats, w_fc2, w_fc1, w_qkv, *scratch = scratch
    up_grad, hidden, gain_sum, shift_sum, grad_sum, head_sum, unit_sum, sems = scratch
    copies = Copies(sems)
    slot_len, width = grad.shape
    units, size = w_fc2.shape[0], 512

    def part_of(part):
        return span(part, size)

    def bring_rows(name, part, source, target):
        at = part_of(part)
        copies.start((name, part), source.at[at, :], target.at[at, :])

    def add_to(ref, columns, array):
        ref[:, columns] += jnp.sum(array, axis=0, keepdims=True)

    def to_units(rows, part):
        at, columns = part_of(rows), part_of(part)
        up = dot(grad[at, :], w_fc2[columns, :], 1, 1) * slope[at, columns].astype(F32)
        up = up.astype(BF16)
        up_grad[at, columns] = up
        add_to(unit_sum, columns, up.astype(F32))

    def to_hidden(rows, part):
        at, columns = part_of(rows), part_of(part)
        result = dot(up_grad[at, :], w_fc1[columns, :], 1, 1) + dot(
            qkv_grad[at, :], w_qkv[columns, :], 1, 1
        )
        hidden[at, columns] = result.astype(BF16)
        normed = (tokens[at, columns].astype(F32) - stats[at, 0:1]) * stats[at, 1:2]
        add_to(gain_sum, columns, result * normed)
        add_to(shift_sum, columns, result)

    parts = width // size
    first_block = copies.numbered(("blocks",), parts * len(blocks))["blocks"]

    def blocks_of(which, do):
        each_block_copy(copies, places_ref, hidden, blocks, which, size, first_block, do)

    for part in range(2):
        bring_rows("grad", part, grad_hbm, grad)
        bring_rows("slope", part, slope_hbm, slope)
        bring_rows("w_fc2", part, w_fc2_hbm, w_fc2)
    for total in (gain_sum, shift_sum, grad_sum, head_sum, unit_sum):
        total[...] = jnp.zeros_like(total)
    copies.wait(("w_fc2", 0), ("grad", 0), ("slope", 0))
    copies.start("w_fc1", w_fc1_hbm, w_fc1)
    copies.start("w_qkv", w_qkv_hbm, w_qkv)
    copies.start("qkv_grad", qkv_grad_hbm, qkv_grad)
    copies.start("tokens", tokens_hbm, tokens)
    copies.start("stats", stats_hbm, stats)

    @pl.loop(0, 4)
    def _(turn):
        rows, part = turn // 2, turn % 2

        @pl.when(turn == 1)
        def _():
            copies.wait(("w_fc2", 1))

        @pl.when(turn == 2)
        def _():
            copies.wait(("grad", 1), ("slope", 1))

        to_units(rows, part)

        @pl.when(part == 0)
        def _():
            add_to(grad_sum, slice(0, width), grad[part_of(rows), :].astype(F32))

    copies.start("up_grad", up_grad, up_grad_hbm)
    copies.wait("w_fc1", "w_qkv", "qkv_grad", "tokens", "stats")
    add_to(head_sum, slice(0, qkv_grad.shape[1]), qkv_grad[...].astype(F32))

    @pl.loop(0, parts)
    def _(part):
        for rows in range(slot_len // size):
            to_hidden(rows, part)
        blocks_of((part,), start)

    for ref, first, total in (
        (norm_sum_ref, 0, gain_sum),
        (norm_sum_ref, 16, shift_sum),
        (grad_sum_ref, 0, grad_sum),
        (head_sum_ref, 0, head_sum),
        (unit_sum_ref, 0, unit_sum),
    ):
        share = total.shape[1] // 16
        if share < BLOCK:
            ref[...] = jnp.zeros_like(ref)
        for row in range(16):
            ref[first + row : first + row + 1, 0:share] = total[:, row * share : row * share + share]
    copies.wait("up_grad")
    blocks_of(range(parts), wait)


def backward(places, grad, slope, qkv_grad, tokens, stats, w_fc2, w_fc1, w_qkv):
    slot_len, width = tokens.shape
    units, heads = w_fc2.shape[0], w_qkv.shape[1]
    sizes = (width, width, width, heads, units)
    sums = [made(rows, BLOCK, F32) for rows in (32, 16, 16, 16)]
    arrays = (grad, slope, qkv_grad, tokens, stats, w_fc2, w_fc1, w_qkv)
    norm_sum, grad_sum, head_sum, unit_sum, up_grad, *blocks = kernel_call(
        backward_kernel,
        "backward",
        sums + [made(slot_len, units)] + block_shapes(width),
        grid=(1,),
        in_specs=[SCALARS] + [AWAY] * len(arrays),
        out_specs=[kept(array) for array in sums] + [AWAY] * (1 + len(BLOCK_NAMES)),
        scratch_shapes=[pltpu.VMEM(array.shape, array.dtype) for array in arrays]
        + [pltpu.VMEM((slot_len, units), BF16), pltpu.VMEM((slot_len, width), BF16)]
        + [pltpu.VMEM((1, size), F32) for size in sizes]
        + [pltpu.SemaphoreType.DMA((64,))],
    )(places, *arrays)
    sums = (norm_sum, grad_sum, head_sum, unit_sum)
    return up_grad, sums, dict(zip(BLOCK_NAMES, blocks))


def weight_kernel(order_ref, *refs):
    lefts, (first_ref, second_ref, *sums, out_ref) = refs[:AT_ONCE], refs[AT_ONCE:]
    cut, end = first_ref.shape[1], first_ref.shape[1] + second_ref.shape[1]
    left = jnp.concatenate([ref[...] for ref in lefts], axis=1)
    out_ref[:, 0:cut] = dot(left, first_ref[...], 0, 0).astype(BF16)
    out_ref[:, cut:end] = dot(left, second_ref[...], 0, 0).astype(BF16)
    if sums:
        for half in range(AT_ONCE):
            block = order_ref[AT_ONCE * pl.program_id(0) + half]
            lines = [
                ref[pl.ds(first + block, 1), :]
                for ref in sums
                for first in range(0, ref.shape[0], 16)
            ]
            lines.append(jnp.zeros((BLOCK - len(lines), BLOCK), F32))
            columns = jnp.concatenate(lines, axis=0).T
            out_ref[half * BLOCK : half * BLOCK + BLOCK, end:] = columns.astype(BF16)


def weight_blocks(order, left, first, second, *sums):
    slot_len = left.shape[0]
    width = first.shape[1] + second.shape[1] + (BLOCK if sums else 0)
    return kernel_call(
        weight_kernel,
        "weights",
        made(left.shape[1], width),
        prefetch=1,
        grid=(left.shape[1] // (AT_ONCE * BLOCK),),
        in_specs=[
            *[
                pl.BlockSpec(
                    (slot_len, BLOCK),
                    functools.partial(lambda at, i, order: (0, order[AT_ONCE * i + at]), at),
                )
                for at in range(AT_ONCE)
            ],
            kept(first),
            kept(second),
            *[kept(array) for array in sums],
        ],
        out_specs=pl.BlockSpec((AT_ONCE * BLOCK, width), lambda i, order: (i, 0)),
    )(order, *[left] * AT_ONCE, first, second, *sums)


def combine(name, *sums):
    arrays = [term[0] for terms in sums for term in terms]
    specs = [
        pl.BlockSpec((term[1], term[0].shape[1]), functools.partial(lambda at, _: (at, 0), term[2]))
        for terms in sums
        for term in terms
    ]
    heights = [max(term[4] for term in terms) for terms in sums]

    def kernel(*refs):
        ins, outs = list(refs[: len(arrays)]), refs[len(arrays) :]
        for terms, height, out in zip(sums, heights, outs):
            mine = [(ins.pop(0), term[3], term[4]) for term in terms]
            cuts = sorted({cut for _, low, high in mine for cut in (low, high)})
            for low, high in zip(cuts, cuts[1:]):
                parts = [
                    ref[low - first : high - first, :].astype(F32)
                    for ref, first, last in mine
                    if first <= low and high <= last
                ]
                out[low:high, :] = functools.reduce(lambda a, b: a + b, parts).astype(BF16)

    shapes = [made(height, terms[0][0].shape[1]) for height, terms in zip(heights, sums)]
    return kernel_call(
        kernel,
        name,
        shapes,
        grid=(1,),
        in_specs=specs,
        out_specs=[pl.BlockSpec(shape.shape, lambda _: (0, 0)) for shape in shapes],
    )(*arrays)


def whole_term(array, low=0):
    return (array, array.shape[0], 0, low, low + array.shape[0])


def output_kernel(lengths_ref, tokens_ref, branch_ref, b_dense_ref, b_fc2_ref, out_ref):
    bias = b_dense_ref[...].astype(F32) + b_fc2_ref[...].astype(F32)
    rows = tokens_ref.shape[0]
    place = pl.program_id(0) * rows + lax.broadcasted_iota(jnp.int32, (rows, 1), 0)
    total = jnp.where(
        place < ends_of(lengths_ref)[-1], branch_ref[...].astype(F32) + bias[None], 0.0
    )
    out_ref[...] = (tokens_ref[...].astype(F32) + total).astype(BF16)


def finish_output(lengths, tokens, branch_sum, b_dense, b_fc2):
    slot_len, width = tokens.shape
    row = pl.BlockSpec((ROWS, width), lambda i: (i, 0))
    return kernel_call(
        output_kernel,
        "output",
        made(slot_len, width),
        grid=(slot_len // ROWS,),
        in_specs=[SCALARS, row, row, kept(b_dense), kept(b_fc2)],
        out_specs=row,
    )(lengths, tokens, branch_sum, b_dense, b_fc2)


def input_kernel(places_ref, *refs):
    *terms, tokens_ref, cot_ref, stats_ref, gain_ref, out_ref = refs
    total = functools.reduce(lambda a, b: a + b, [t[...].astype(F32) for t in terms])
    inv_sigma = stats_ref[:, 1:2]
    normed = (tokens_ref[...].astype(F32) - stats_ref[:, 0:1]) * inv_sigma
    scaled = total * gain_ref[...].astype(F32)[None]
    out_ref[...] = (
        cot_ref[...].astype(F32)
        + inv_sigma
        * (
            scaled
            - jnp.mean(scaled, axis=1, keepdims=True)
            - normed * jnp.mean(scaled * normed, axis=1, keepdims=True)
        )
    ).astype(BF16)


def input_rows(places, terms, tokens, cot, stats, gain):
    width = tokens.shape[1]

    def mine(columns):
        return pl.BlockSpec((BLOCK, columns), lambda i, places: (places[0], 0))

    return kernel_call(
        input_kernel,
        "input",
        made(BLOCK, width),
        prefetch=1,
        grid=(1,),
        in_specs=[kept(t) for t in terms] + [mine(width), mine(width), mine(128), kept(gain)],
        out_specs=pl.BlockSpec((BLOCK, width), lambda *_: (0, 0)),
    )(places, *terms, tokens, cot, stats, gain)


def place_kernel(blocks, places_ref, *refs):
    pieces, out_ref, sems = refs[: len(blocks)], refs[-2], refs[-1]
    copies = []
    for i, ((offset, low, high), piece) in enumerate(zip(blocks, pieces)):
        first = pl.multiple_of(places_ref[OFFSETS.index(offset)] * BLOCK, BLOCK)
        copies.append(
            pltpu.make_async_copy(
                piece, out_ref.at[pl.ds(first + low, high - low), :], sems.at[i]
            )
        )
    for copy in copies:
        copy.start()
    for copy in copies:
        copy.wait()


def place_rows(places, blocks, pieces, whole=None):
    rest = {} if whole is None else {"input_output_aliases": {len(pieces) + 1: 0}}
    given = [] if whole is None else [whole]
    return kernel_call(
        functools.partial(place_kernel, blocks),
        "place",
        made(8 * BLOCK, pieces[0].shape[1]),
        in_specs=[SCALARS] + [NEAR] * len(pieces) + [AWAY] * len(given),
        out_specs=AWAY,
        scratch_shapes=[pltpu.SemaphoreType.DMA((len(pieces),))],
        **rest,
    )(places, *pieces, *given)


def up_kernel(near_ref, far_ref, first_ref, second_ref):
    total = near_ref[...].astype(F32) + far_ref[...].astype(F32)
    cut = first_ref.shape[1]
    first_ref[...] = total[:, :cut]
    second_ref[...] = total[:, cut:]


def down_kernel(near_ref, far_ref, first_ref, second_ref, sums_ref):
    total = near_ref[...].astype(F32) + far_ref[...].astype(F32)
    cut, end = first_ref.shape[0], first_ref.shape[0] + second_ref.shape[0]
    first_ref[...] = total[:, :cut].T
    second_ref[...] = total[:, cut:end].T
    sums_ref[...] = total[:, end:].T[: sums_ref.shape[0]]


def last_sum(kernel, name, shapes, near, far):
    return kernel_call(
        kernel,
        name,
        [made(*shape, F32) for shape in shapes],
        grid=(1,),
        in_specs=[pl.BlockSpec(far.shape, lambda _: (0, 0))] * 2,
        out_specs=[pl.BlockSpec(shape, lambda _: (0, 0)) for shape in shapes],
    )(near, far)


def shift(array, axis, size, by):
    return lax.ppermute(array, axis, [(i, (i + by) % size) for i in range(size)])


def y_up(array):
    return shift(array, "y", 4, 1)


def y_down(array):
    return shift(array, "y", 4, 3)


def across(array):
    return shift(array, "zl", 2, 1)


def after(arrays, *earlier):
    return lax.optimization_barrier((arrays, earlier))[0]


class TensorSum:
    def __init__(self, blocks):
        self.blocks = blocks

    def send_far(self):
        b = self.blocks
        self.far = across(b[0]), y_up(b[1]), y_down(b[2])

    def send_middle(self, earlier):
        b = self.blocks
        far = *self.far[:2], after(self.far[2], earlier)
        sent = combine(
            "middle",
            *[
                [whole_term(b[offset]), whole_term(part, low)]
                for offset, part, (low, _) in zip(((0, 2), (1, 1), (1, 3)), far, PARTS)
            ],
        )
        self.middle = y_up(sent[0]), across(sent[1]), y_down(sent[2])
        return sent

    def send_near(self, earlier):
        b = self.blocks
        two_on, diagonal, other = self.middle
        other = after(other, earlier)
        sent = combine(
            "near",
            [whole_term(b[(0, 1)]), whole_term(two_on), whole_term(diagonal)],
            [whole_term(b[(1, 0)]), whole_term(other)],
        )
        self.near = [y_up(sent[0]), across(sent[1]), y_down(after(b[(0, 3)], sent))]
        return sent

    def terms(self):
        return [self.blocks[(0, 0)], *self.near]


class TensorGather:
    def __init__(self, places, rows):
        self.places, self.rows = places, rows
        self.one = y_up(rows), y_down(rows), across(rows)

    def second(self, earlier):
        before, ahead, partner = self.one = after(self.one, earlier)
        self.two = y_down(ahead), across(ahead), y_up(partner)
        return self.one

    def third(self, earlier):
        two_on, diagonal, other = self.two = after(self.two, earlier)
        (a, b), (c, d), (e, f) = PARTS
        self.three = across(two_on[a:b]), y_down(diagonal[c:d]), y_up(other[e:f])
        blocks = [(0, 0), (0, 3), (0, 1), (1, 0), (0, 2), (1, 1), (1, 3)]
        self.whole = place_rows(
            self.places,
            [(offset, 0, BLOCK) for offset in blocks],
            [self.rows, *self.one, *self.two],
        )
        return self.whole

    def finish(self, earlier):
        parts = after(self.three, earlier)
        return place_rows(
            self.places, [(FAR, low, high) for low, high in PARTS], list(parts), self.whole
        )


class DataSum:
    def __init__(self, partial_sums, earlier):
        self.near = lax.psum_scatter(
            after(partial_sums, earlier), ("x", "core"), scatter_dimension=0, tiled=True
        )

    def send(self, earlier):
        self.near = after(self.near, earlier)
        self.far = shift(self.near[BLOCK:], "zh", 2, 1)

    def finish(self, kernel, name, shapes, earlier):
        return last_sum(kernel, name, shapes, self.near, after(self.far, earlier))


def dp_order():
    half = lax.axis_index("zh")
    return jnp.stack(
        [(half + part) % 2 * 8 + block for block in range(8) for part in range(2)]
    ).astype(jnp.int32)


def per_device(
    tokens,
    cotangent,
    seq_lengths,
    ln_gain,
    ln_bias,
    w_qkv,
    b_qkv,
    w_dense,
    b_dense,
    w_fc1,
    b_fc1,
    w_fc2,
    b_fc2,
):
    units = w_fc2.shape[0]
    plane, place = lax.axis_index("zl"), lax.axis_index("y")
    places = jnp.stack(
        [(plane + planes) % 2 * 4 + (place + steps) % 4 for planes, steps in OFFSETS]
    ).astype(jnp.int32)
    order = dp_order()
    frequency = 10000.0 ** (-jnp.arange(ROTARY // 2, dtype=F32) * 2.0 / ROTARY)
    frequency = jnp.tile(frequency, 8)[None]
    hidden, grad, activated, slope, context, qkv_grad, stats, branch_part = forward(
        seq_lengths,
        frequency,
        tokens,
        cotangent,
        ln_gain,
        ln_bias,
        b_qkv,
        b_fc1,
        w_qkv,
        w_fc1,
        w_dense,
        w_fc2,
    )
    branch_sum = lax.psum(branch_part, TENSOR)
    up_grad, sums, blocks = backward(
        after(places, branch_part), grad, slope, qkv_grad, tokens, stats, w_fc2, w_fc1, w_qkv
    )
    hidden_sum = TensorSum(blocks)
    hidden_sum.send_far()
    down_part = weight_blocks(after(order, up_grad), grad, activated, context, *sums)
    done = hidden_sum.send_middle(down_part)
    down = DataSum(down_part, done)
    up_part = weight_blocks(after(order, done), hidden, up_grad, qkv_grad)
    done = hidden_sum.send_near(up_part)
    up = DataSum(up_part, done)
    rows = input_rows(
        after(places, done), hidden_sum.terms(), tokens, cotangent, stats, ln_gain
    )
    input_grad = TensorGather(places, rows)
    down.send((rows, branch_sum))
    done = input_grad.second(down.near)
    output = finish_output(after(seq_lengths, done), tokens, branch_sum, b_dense, b_fc2)
    grad_fc2, grad_dense, small = down.finish(
        down_kernel,
        "down",
        ((units, BLOCK), (w_dense.shape[0], BLOCK), (8, BLOCK)),
        output,
    )
    norm_sum = small[:2]
    norm_across = across(norm_sum)
    up.send(output)
    input_grad.third((output, up.near))
    *three, up.far = after([*input_grad.three, up.far], input_grad.whole)
    input_grad.three = three
    norm_sum = norm_sum + after(norm_across, three[0])
    grad_fc1, grad_qkv = up.finish(
        up_kernel, "up", ((BLOCK, units), (BLOCK, w_qkv.shape[1])), input_grad.three[0]
    )
    norm_sum = norm_sum + y_up(norm_sum) + y_down(norm_sum) + shift(norm_sum, "y", 4, 2)
    input_grad = input_grad.finish(grad_qkv)
    out_bias = small[2]
    return (
        output,
        input_grad,
        norm_sum[0],
        norm_sum[1],
        grad_qkv,
        small[3, :48],
        grad_dense,
        out_bias,
        grad_fc1,
        small[4, :64],
        grad_fc2,
        out_bias,
    )


def solution(mesh):
    parts = Mesh(mesh.devices.reshape(2, 4, 2, 2, 4), DP + TENSOR)
    rows = P(DP, None)
    placed = (
        rows,
        rows,
        rows,
        P(),
        P(),
        P(None, TENSOR),
        P(TENSOR),
        P(TENSOR, None),
        P(),
        P(None, TENSOR),
        P(TENSOR),
        P(TENSOR, None),
        P(),
    )
    return jax.shard_map(
        per_device,
        mesh=parts,
        in_specs=placed,
        out_specs=(
            rows,
            rows,
            P(DP),
            P(DP),
            P(DP, TENSOR),
            P(TENSOR + DP),
            P(TENSOR, DP),
            P(DP),
            P(DP, TENSOR),
            P(TENSOR + DP),
            P(TENSOR, DP),
            P(DP),
        ),
        check_vma=False,
    )
```
